128 devices in a mesh: gx: 8 (over y_lo, z), gy: 16 (over y_hi, x, core).
Axes of the slice: x: 4, y: 4 (y_hi: 2, y_lo: 2; y = y_hi * 2 + y_lo), z: 4, core: 2. Of those that a mesh axis runs over, the one named last changes fastest.
Arguments:
- positions: float32 [3, 8, 16, 32768], P(None, 'gx', 'gy'), may hold values from 0 to 1024, as said below
- polarity: float32 [8, 16, 32768], P('gx', 'gy'), may hold values from 0.4 to 2.5
- dipoles: float32 [6, 8, 16, 32768], P(None, 'gx', 'gy'), may hold values from -6 to 6
- perm_fields: float32 [6, 8, 16, 32768], P(None, 'gx', 'gy'), may hold values from -6 to 6
- pair_list: int32 [8, 16, 2, 2048], P('gx', 'gy'), may hold values from 0 to 2303, as said below
- tile_counts: int32 [8, 16], P('gx', 'gy'), may hold values from 256 to 2048, as said below
Outputs:
- field: float32 [6, 8, 16, 32768], P(None, 'gx', 'gy')
- induced: float32 [6, 8, 16, 32768], P(None, 'gx', 'gy')
The draws below stay inside these ranges and needn't reach their ends.
Inputs may be any that keep to these rules, and one draw needn't show every extreme that they name: `pair_list`: entry [0, p] is a tile of the domain itself; entry [1, p] = s * 256 + t names tile t of image s, the domain at offset (s // 3 - 1, s % 3 - 1) along (gx, gy), s = 4 being the domain itself. Slots at or past the domain's count are unused. `tile_counts`: some domains use all 2048 slots. `positions`: site k of tile t lies within 0.6 along each coordinate of the point (2 (k % 8) + 1, 2 ((k // 8) % 8) + 1, 4 t + 2 (k // 64) + 1); every domain is 16 wide along both periodic directions.
All inputs are finite; a program needn't handle non-finite values.
Results may differ from the reference program's by a relative error of at most 0.0003.
Values sent between devices are 32-bit elements; how exact they have to be, the bound alone decides.
A program may use at most 128 MiB of HBM per device.

```python
import math
import jax
import jax.numpy as jnp
from jax import lax

TILE = 128
TILES_DEV = 256
ATOM_DEV = 32768
PMAX = 2048
N_GX = 8
N_GY = 16


def draw_positions(key, part):
    key = jax.random.fold_in(key, 5)
    site_index = jnp.arange(ATOM_DEV, dtype=jnp.int32)
    within = site_index % TILE
    tile_index = site_index // TILE
    lattice = jnp.stack([within % 8, within // 8 % 8, 2 * tile_index + within // 64]).astype(jnp.float32) * 2.0 + 1.0
    draw_shape = (3, N_GX, N_GY, ATOM_DEV)
    jitter = jnp.clip(0.2 * jax.random.normal(key, draw_shape, jnp.float32), -0.5, 0.5)
    return lattice[:, None, None, :] + jitter


def draw_pair_list(key, part):
    key = jax.random.fold_in(key, 7)
    first_key, second_key, third_key = jax.random.split(key, 3)
    draw_shape = (N_GX, N_GY, PMAX)
    near_tile = jax.random.randint(first_key, draw_shape, 0, TILES_DEV)
    image_slot = jax.random.randint(second_key, draw_shape, 0, 9)
    tile_step = jax.random.randint(third_key, draw_shape, -2, 3)
    far_tile = jnp.clip(near_tile + tile_step, 0, TILES_DEV - 1)
    far_entry = image_slot * TILES_DEV + far_tile
    near_tile = near_tile.at[..., 0].set(0)
    far_entry = far_entry.at[..., 0].set(4 * TILES_DEV)
    near_tile = near_tile.at[..., -1].set(TILES_DEV - 1)
    far_entry = far_entry.at[..., -1].set(9 * TILES_DEV - 1)
    return jnp.stack([near_tile, far_entry], 2).astype(jnp.int32)


def draw_tile_counts(key, part):
    key = jax.random.fold_in(key, 9)
    first_key, second_key = jax.random.split(key, 2)
    device_total = N_GX * N_GY
    device_rank = jax.random.permutation(first_key, device_total)
    base_count = jax.random.randint(second_key, (device_total,), PMAX // 8, 3 * PMAX // 8 + 1)
    base_count = jnp.where(device_rank == 4, PMAX // 8, base_count)
    return jnp.where(device_rank < 4, PMAX, base_count).reshape(N_GX, N_GY).astype(jnp.int32)


def steps_of(key, extent, shards, least, largest):
    loudness, own = 1.0, jax.random.fold_in(key, 6)
    for position, blocks in shards:
        steps = jnp.exp(jax.random.uniform(jax.random.fold_in(own, position), (blocks,), jnp.float32, least / len(shards), largest / len(shards)))
        loudness = loudness * jnp.repeat(steps, extent[position] // blocks).reshape([-1 if axis == position else 1 for axis in range(len(extent))])
    return loudness


def normal_values(key, shape, deviation, most, cuts=(), held_as=jnp.bfloat16):
    entries = deviation * jax.random.normal(key, shape, jnp.float32)
    if cuts:
        entries = entries * steps_of(key, shape, cuts, -0.22, 0.18)
    return jnp.clip(entries, -most, most).astype(held_as)


def setup_inputs(seed: int = 0) -> dict:
    streams_of = jax.random.split(jax.random.key(seed), 7)
    return {
        "positions": draw_positions(jax.random.fold_in(streams_of[6], 71), 0),
        "polarity": jnp.clip(jnp.exp(math.log(2.5) - 1.8325814 * jax.random.uniform(streams_of[1], (N_GX, N_GY, ATOM_DEV), jnp.float32) ** steps_of(streams_of[1], (N_GX, N_GY, ATOM_DEV), ((0, 8), (1, 16)), -0.2, 0.2)), 0.4, 2.5),
        "dipoles": normal_values(streams_of[2], (6, N_GX, N_GY, ATOM_DEV), 1.0, 6.0, ((1, 8), (2, 16)), jnp.float32),
        "perm_fields": normal_values(streams_of[3], (6, N_GX, N_GY, ATOM_DEV), 1.0, 6.0, ((1, 8), (2, 16)), jnp.float32),
        "pair_list": draw_pair_list(jax.random.fold_in(streams_of[6], 71), 0),
        "tile_counts": draw_tile_counts(jax.random.fold_in(streams_of[6], 71), 0),
    }


thole = 0.39
domain_edge = 16.0

def pair_terms(near_sites, far_sites, self_flag):
    diagonal_ones = jnp.eye(TILE, dtype=jnp.float32)
    self_mask = self_flag[:, None, None] * diagonal_ones[None]
    keep_mask = 1.0 - self_mask
    delta_x = near_sites[:, 0, :, None] - far_sites[:, 0, None, :]
    delta_y = near_sites[:, 1, :, None] - far_sites[:, 1, None, :]
    delta_z = near_sites[:, 2, :, None] - far_sites[:, 2, None, :]
    dist_sq = delta_x * delta_x + delta_y * delta_y + delta_z * delta_z + self_mask
    distance = jnp.sqrt(dist_sq)
    inv_sq = 1.0 / dist_sq
    inv_cube = inv_sq / distance
    pol_scale = jnp.sqrt(near_sites[:, 3, :, None] * far_sites[:, 3, None, :])
    damp_arg = thole * dist_sq * distance / pol_scale
    lam_three = -jnp.expm1(-damp_arg)
    lam_five = lam_three - damp_arg * jnp.exp(-damp_arg)
    coef_three = keep_mask * lam_three * inv_cube
    coef_five = 3.0 * keep_mask * lam_five * inv_cube * inv_sq
    deltas = (delta_x, delta_y, delta_z)
    near_out = []
    far_out = []
    for set_row in (4, 7):
        dip_far = far_sites[:, set_row:set_row + 3]
        dip_near = near_sites[:, set_row:set_row + 3]
        dot_far = delta_x * dip_far[:, 0, None, :] + delta_y * dip_far[:, 1, None, :] + delta_z * dip_far[:, 2, None, :]
        dot_near = delta_x * dip_near[:, 0, :, None] + delta_y * dip_near[:, 1, :, None] + delta_z * dip_near[:, 2, :, None]
        for column in range(3):
            near_out.append(lax.optimization_barrier(jnp.sum(coef_five * dot_far * deltas[column] - coef_three * dip_far[:, column, None, :], axis=2)))
            far_out.append(lax.optimization_barrier(jnp.sum(coef_five * dot_near * deltas[column] - coef_three * dip_near[:, column, :, None], axis=1)))
    far_keep = (1.0 - self_flag)[:, None, None]
    return (jnp.stack(near_out, 1), jnp.stack(far_out, 1) * far_keep)

def device_terms(own_rows, halo_rows, slot_table, used_count):
    own_tiles = own_rows.reshape(10, TILES_DEV, TILE).transpose(1, 0, 2)
    halo_tiles = halo_rows.reshape(9, 10, TILES_DEV, TILE).transpose(0, 2, 1, 3).reshape(9 * TILES_DEV, 10, TILE)
    batch_rows = PMAX // 16
    rounds = (used_count + batch_rows - 1) // batch_rows
    row_range = jnp.arange(batch_rows, dtype=jnp.int32)

    def one_round(round_index, partial_value):
        near_acc, far_acc = partial_value
        first_row = (round_index * batch_rows).astype(jnp.int32)
        slot_ids = lax.dynamic_slice_in_dim(slot_table, first_row, batch_rows, 1)
        near_sites = own_tiles[slot_ids[0]]
        far_sites = halo_tiles[slot_ids[1]]
        self_flag = (slot_ids[1] == slot_ids[0] + 4 * TILES_DEV).astype(jnp.float32)
        live_rows = (first_row + row_range < used_count).astype(jnp.float32)
        near_part, far_part = pair_terms(near_sites, far_sites, self_flag)
        near_acc = near_acc.at[slot_ids[0]].add(near_part.reshape(batch_rows, 6 * TILE) * live_rows[:, None])
        far_acc = far_acc.at[slot_ids[1]].add(far_part.reshape(batch_rows, 6 * TILE) * live_rows[:, None])
        return (near_acc, far_acc)
    start_acc = (jnp.zeros((TILES_DEV, 6 * TILE), jnp.float32), jnp.zeros((9 * TILES_DEV, 6 * TILE), jnp.float32))
    return lax.fori_loop(0, rounds, one_round, start_acc)

def reference(positions, polarity, dipoles, perm_fields, pair_list, tile_counts):
    device_total = N_GX * N_GY
    sites = jnp.concatenate([positions, polarity[None], dipoles], 0)
    images = []
    for row_off in (-1, 0, 1):
        for col_off in (-1, 0, 1):
            rolled = jnp.roll(sites, (-row_off, -col_off), axis=(1, 2))
            rolled = rolled.at[0].add(row_off * domain_edge).at[1].add(col_off * domain_edge)
            images.append(rolled)
    halo_sites = jnp.stack(images, 0)
    own_rows = sites.reshape(10, device_total, ATOM_DEV).transpose(1, 0, 2)
    halo_rows = halo_sites.reshape(9, 10, device_total, ATOM_DEV).transpose(2, 0, 1, 3)
    slot_table = pair_list.reshape(device_total, 2, PMAX)
    used = tile_counts.reshape(device_total)
    near_acc, far_acc = lax.map(lambda packed: device_terms(*packed), (own_rows, halo_rows, slot_table, used))
    far_grid = far_acc.reshape(N_GX, N_GY, 9, TILES_DEV, 6 * TILE)
    total_field = near_acc.reshape(N_GX, N_GY, TILES_DEV, 6 * TILE)
    slot_number = 0
    for row_off in (-1, 0, 1):
        for col_off in (-1, 0, 1):
            total_field = total_field + jnp.roll(far_grid[:, :, slot_number], (row_off, col_off), axis=(0, 1))
            slot_number = slot_number + 1
    field = total_field.reshape(N_GX, N_GY, TILES_DEV, 6, TILE).transpose(3, 0, 1, 2, 4).reshape(6, N_GX, N_GY, ATOM_DEV)
    induced = polarity[None] * (perm_fields + field)
    return (field, induced)
```

```python
import jax
import jax.numpy as jnp
from jax import lax
from jax.experimental import pallas as pl
from jax.experimental.pallas import tpu as pltpu
from jax.sharding import PartitionSpec as P

TILE = 128
TILES = 256
ROWS = 10 * TILES
UNROLL = 4

thole = 0.39
domain_edge = 16.0

F32 = jnp.float32
BF16 = jnp.bfloat16


def three_parts(value):
    high = value.astype(BF16)
    rest = value - high.astype(F32)
    middle = rest.astype(BF16)
    low = (rest - middle.astype(F32)).astype(BF16)
    return high, middle, low


def rows_of():
    sub = lax.broadcasted_iota(jnp.int32, (8, TILE), 0)
    second = (sub == 3) | (sub == 4) | (sub == 5) | (sub == 7)
    is_x = (sub == 0) | (sub == 3)
    is_y = (sub == 1) | (sub == 4)
    is_z = (sub == 2) | (sub == 5)
    return sub, second, is_x, is_y, is_z


def load_row(ref, row):
    return jnp.broadcast_to(ref[pl.ds(row, 1), :], (8, TILE))


def site_vectors(ref, base, centre):
    sub, second, is_x, is_y, is_z = rows_of()
    dips = [load_row(ref, base + k * TILES) for k in range(6)]
    pos = [load_row(ref, base + (6 + k) * TILES) - centre[k] for k in range(3)]
    pol = load_row(ref, base + 9 * TILES)
    mu = [jnp.where(second, dips[3 + j], dips[j]) for j in range(3)]
    mixed = jnp.where(is_x, pos[0], jnp.where(is_y, pos[1], jnp.where(is_z, pos[2], 1.0)))
    own = jnp.where(is_x, mu[0], jnp.where(is_y, mu[1], jnp.where(is_z, mu[2], 0.0)))
    return mu, pos, pol, mixed, own


def dipole_rows(mu, pos, mixed, own):
    dots = pos[0] * mu[0] + pos[1] * mu[1] + pos[2] * mu[2]
    tripled = 3.0 * mixed
    left = jnp.concatenate([tripled * mu[0], tripled * mu[1], tripled * mu[2], tripled * dots], 0)
    blank = jnp.zeros((16, TILE), BF16)
    right = jnp.concatenate([jnp.zeros((8, TILE), F32), -own], 0)
    out = []
    for l, r in zip(three_parts(left), three_parts(right)):
        out.append(jnp.concatenate([l, jnp.concatenate([blank, r], 0)], 1))
    return jnp.concatenate(out, 0)


def geometry_rows(first_three, fourth, fifth):
    sub = lax.broadcasted_iota(jnp.int32, (8, TILE), 0)
    rows = jnp.where(sub == 0, first_three[0], jnp.where(sub == 1, first_three[1], jnp.where(sub == 2, first_three[2], jnp.where(sub == 3, fourth, jnp.where(sub == 4, fifth, 0.0)))))
    return tuple(p.astype(F32) for p in three_parts(rows))


def scale_rows(scale, pattern):
    sub = lax.broadcasted_iota(jnp.int32, (8, TILE), 0)
    parts = [p.astype(F32) for p in three_parts(scale)]
    out = jnp.zeros((8, TILE), F32)
    for row, part in enumerate(pattern):
        out = jnp.where(sub == row, parts[part], out)
    return out


def squared(pos):
    return pos[0] * pos[0] + pos[1] * pos[1] + pos[2] * pos[2]


def assemble(parts, pos, mixed):
    sub, second, _, _, _ = rows_of()
    g = pos[0] * parts[0] + pos[1] * parts[1] + pos[2] * parts[2] - parts[3]
    s0 = jnp.broadcast_to(g[6:7], (8, TILE))
    s1 = jnp.broadcast_to(g[7:8], (8, TILE))
    s = jnp.where(second, s1, s0)
    return mixed * s - g


def kernel(starts_ref, homes_ref, remotes_ref, x_ref, out_ref, geo_ref, dip_ref, acc_ref):
    eye = (
        lax.broadcasted_iota(jnp.int32, (TILE, TILE), 0) == lax.broadcasted_iota(jnp.int32, (TILE, TILE), 1)
    )
    eye16 = jnp.where(eye, 1.0, 0.0).astype(BF16)
    zero8 = jnp.zeros((8, TILE), F32)
    own_base = 4 * ROWS

    def clear(i, _):
        out_ref[pl.ds(pl.multiple_of(i * 64, 64), 64), :] = jnp.zeros((64, TILE), F32)
        return 0

    lax.fori_loop(0, out_ref.shape[0] // 64, clear, 0)

    def prepare(t, _):
        centre = (8.0, 8.0, (4 * t + 2).astype(F32))
        mu, pos, pol, mixed, own = site_vectors(x_ref, own_base + t, centre)
        dip_ref[t] = dipole_rows(mu, pos, mixed, own)
        hi, mid, lo = geometry_rows([-2.0 * p for p in pos], 1.0, squared(pos))
        scale = (-thole) * lax.rsqrt(pol)
        q = scale_rows(scale, (0, 1, 0, 1, 0, 2))
        stack = jnp.concatenate([hi, mid, hi, mid, hi, lo, q, zero8], 0).astype(BF16)
        geo_ref[t] = lax.dot_general(
            eye16, stack, (((1,), (1,)), ((), ())), preferred_element_type=F32
        ).astype(BF16)
        acc_ref[t] = jnp.zeros((32, TILE), F32)
        return 0

    lax.fori_loop(0, TILES, prepare, 0)

    def pair(home, remote_base, shift, self_flag):
        centre = (8.0 - shift[0], 8.0 - shift[1], (4 * home + 2).astype(F32))
        mu, pos, pol, mixed, own = site_vectors(x_ref, remote_base, centre)
        hi, mid, lo = geometry_rows(pos, squared(pos), 1.0)
        q = scale_rows(lax.rsqrt(pol), (0, 0, 1, 1, 2, 0))
        left = jnp.concatenate([hi, hi, mid, mid, lo, hi, zero8, zero8], 0).astype(BF16)
        right = jnp.concatenate([jnp.zeros((48, TILE), F32), q, zero8], 0).astype(BF16)
        both = jnp.dot(
            geo_ref[home], jnp.concatenate([left, right], 1), preferred_element_type=F32
        )
        dist_sq = both[:, :TILE]
        if self_flag is not None:
            mask = jnp.where(eye, self_flag, 0.0)
            dist_sq = jnp.where(mask > 0.5, 1.0, dist_sq)
        inv = lax.rsqrt(dist_sq)
        inv_sq = inv * inv
        inv_cube = inv_sq * inv
        cube = dist_sq * inv * dist_sq
        damp = cube * both[:, TILE:]
        decay = jnp.exp(damp)
        lam_three = 1.0 - decay
        lam_five = lam_three + damp * decay
        three = lam_three * inv_cube
        five = lam_five * inv_cube * inv_sq
        if self_flag is not None:
            three = three * (1.0 - mask)
            five = five * (1.0 - mask)
        three_hi = three.astype(BF16)
        three_lo = (three - three_hi.astype(F32)).astype(BF16)
        five_hi = five.astype(BF16)
        five_lo = (five - five_hi.astype(F32)).astype(BF16)
        rem = dipole_rows(mu, pos, mixed, own)
        nt = (((1,), (1,)), ((), ()))
        square = jnp.concatenate(
            [jnp.concatenate([five_hi, three_hi], 1), jnp.concatenate([five_lo, three_lo], 1)], 0
        )
        h1 = lax.dot_general(rem, square, nt, preferred_element_type=F32)
        home_dip = dip_ref[home]
        square = jnp.concatenate(
            [jnp.concatenate([five_hi, five_lo], 1), jnp.concatenate([three_hi, three_lo], 1)], 0
        )
        r1 = jnp.dot(home_dip, square, preferred_element_type=F32)
        h = h1[0:32, :TILE] + (h1[32:64, :TILE] + h1[0:32, TILE:]) + (h1[64:96, :TILE] + h1[32:64, TILE:])
        r = r1[0:32, :TILE] + (r1[32:64, :TILE] + r1[0:32, TILE:]) + (r1[64:96, :TILE] + r1[32:64, TILE:])
        field = assemble([r[8 * j:8 * j + 8] for j in range(4)], pos, mixed)
        if self_flag is not None:
            field = field * (1.0 - self_flag)
        return h, field

    for g in range(9):
        shift = (domain_edge * (g // 3 - 1), domain_edge * (g % 3 - 1))
        first = starts_ref[2 * g]
        last = starts_ref[2 * g + 1]

        def step(i, _, g=g, shift=shift, first=first, last=last):
            todo = []
            for k in range(UNROLL):
                p = first + i * UNROLL + k
                live = p < last
                slot = jnp.minimum(p, last - 1)
                home = homes_ref[g, slot]
                remote = remotes_ref[g, slot]
                flag = None
                if g == 4:
                    flag = (home == remote).astype(F32)
                h, field = pair(home, g * ROWS + remote, shift, flag)
                todo.append((jnp.where(live, home, TILES), jnp.where(live, remote, TILES), h, field))
            for home, remote, h, field in todo:
                acc_ref[home] += h
                at = pl.ds(g * OUT_ROWS + remote, 8, stride=OUT_STRIDE)
                out_ref[at, :] += field
            return 0

        lax.fori_loop(0, (last - first + UNROLL - 1) // UNROLL, step, 0)

    def finish(t, _):
        centre = (8.0, 8.0, (4 * t + 2).astype(F32))
        mu, pos, pol, mixed, own = site_vectors(x_ref, own_base + t, centre)
        field = assemble([acc_ref[t, 8 * j:8 * j + 8] for j in range(4)], pos, mixed)
        at = pl.ds(4 * OUT_ROWS + t, 8, stride=OUT_STRIDE)
        out_ref[at, :] += field
        return 0

    lax.fori_loop(0, TILES, finish, 0)


OUT_STRIDE = TILES + 8
OUT_ROWS = 8 * OUT_STRIDE


def field_kernel(starts, homes, remotes, x):
    smem = pl.BlockSpec(memory_space=pltpu.SMEM)
    vmem = pl.BlockSpec(memory_space=pltpu.VMEM)
    return pl.pallas_call(
        kernel,
        out_shape=jax.ShapeDtypeStruct((9 * OUT_ROWS, TILE), F32),
        in_specs=[smem, smem, smem, vmem],
        out_specs=vmem,
        scratch_shapes=[
            pltpu.VMEM((TILES, TILE, 64), BF16),
            pltpu.VMEM((TILES, 96, 2 * TILE), BF16),
            pltpu.VMEM((TILES + 1, 32, TILE), F32),
        ],
        compiler_params=pltpu.CompilerParams(vmem_limit_bytes=60 * 1024 * 1024),
        name="pair_fields",
    )(starts, homes, remotes, x)


def around(value, axis):
    count = lax.axis_size(axis)
    forward = [(i, (i + 1) % count) for i in range(count)]
    backward = [((i + 1) % count, i) for i in range(count)]
    return [lax.ppermute(value, axis, forward), value, lax.ppermute(value, axis, backward)]


def shifted(value, axis, steps):
    count = lax.axis_size(axis)
    pairs = [(source, (source + steps) % count) for source in range(count)]
    return lax.ppermute(value, axis, pairs)


def local(positions, polarity, dipoles, perm_fields, pair_list, tile_counts):
    slot_total = pair_list.shape[3]
    sites = jnp.concatenate([dipoles, positions, polarity[None]], 0).reshape(1, 10 * TILES, TILE)
    rows = jnp.concatenate(around(sites, "gx"), 0)[:, None]
    halo = jnp.concatenate(around(rows, "gy"), 1).reshape(9 * ROWS, TILE)

    table = pair_list.reshape(2, slot_total)
    live = jnp.arange(slot_total, dtype=jnp.int32) < tile_counts.reshape(())
    far = jnp.where(live, table[1], 16 * TILES)
    far, near = lax.sort((far, table[0]), num_keys=1)
    bounds = jnp.arange(slot_total, dtype=jnp.int32)[:16] * TILES
    bounds = jnp.sum((far[None, :] < bounds[:, None]).astype(jnp.int32), 1)
    bounds = jnp.concatenate([bounds, jnp.zeros((slot_total - 16,), jnp.int32)])
    lists = jnp.stack([far, near, bounds])[None]
    lists = jnp.concatenate(around(lists, "gx"), 0)[:, None]
    lists = jnp.concatenate(around(lists, "gy"), 1).reshape(9, 3, slot_total)
    starts = []
    for g in range(9):
        starts += [lists[g, 2, 8 - g], lists[g, 2, 9 - g]]
    homes = lists[:, 0] & (TILES - 1)
    remotes = lists[:, 1]

    terms = field_kernel(jnp.stack(starts), homes, remotes, halo)
    terms = terms.reshape(3, 3, 8, OUT_STRIDE, TILE)[:, :, :6, :TILES]
    column = terms[:, 1] + shifted(terms[:, 0], "gy", -1) + shifted(terms[:, 2], "gy", 1)
    field = column[1] + shifted(column[0], "gx", -1) + shifted(column[2], "gx", 1)
    field = field.reshape(6, 1, 1, TILES * TILE)
    induced = polarity[None] * (perm_fields + field)
    return (field, induced)


def solution(mesh):
    placed = (
        P(None, "gx", "gy", None),
        P("gx", "gy", None),
        P(None, "gx", "gy", None),
        P(None, "gx", "gy", None),
        P("gx", "gy", None, None),
        P("gx", "gy"),
    )
    return jax.shard_map(
        local,
        mesh=mesh,
        in_specs=placed,
        out_specs=(P(None, "gx", "gy", None), P(None, "gx", "gy", None)),
        check_vma=False,
    )
```

```python
import jax
import jax.numpy as jnp
from jax import lax
from jax.experimental import pallas as pl
from jax.experimental.pallas import tpu as pltpu
from jax.sharding import PartitionSpec as P

TILE = 128
TILES = 256
ROWS = 10 * TILES
UNROLL = 4
PARTS = 3
DUMMY = TILES

thole = 0.39
domain_edge = 16.0

F32 = jnp.float32
BF16 = jnp.bfloat16


def three_parts(value):
    high = value.astype(BF16)
    rest = value - high.astype(F32)
    middle = rest.astype(BF16)
    low = (rest - middle.astype(F32)).astype(BF16)
    return high, middle, low


def rows_of():
    sub = lax.broadcasted_iota(jnp.int32, (8, TILE), 0)
    second = (sub == 3) | (sub == 4) | (sub == 5) | (sub == 7)
    is_x = (sub == 0) | (sub == 3)
    is_y = (sub == 1) | (sub == 4)
    is_z = (sub == 2) | (sub == 5)
    return sub, second, is_x, is_y, is_z


def load_row(ref, row):
    return jnp.broadcast_to(ref[pl.ds(row, 1), :], (8, TILE))


def site_vectors(ref, base, centre):
    sub, second, is_x, is_y, is_z = rows_of()
    dips = [load_row(ref, base + k * TILES) for k in range(6)]
    pos = [load_row(ref, base + (6 + k) * TILES) - centre[k] for k in range(3)]
    pol = load_row(ref, base + 9 * TILES)
    mu = [jnp.where(second, dips[3 + j], dips[j]) for j in range(3)]
    mixed = jnp.where(is_x, pos[0], jnp.where(is_y, pos[1], jnp.where(is_z, pos[2], 1.0)))
    own = jnp.where(is_x, mu[0], jnp.where(is_y, mu[1], jnp.where(is_z, mu[2], 0.0)))
    return mu, pos, pol, mixed, own


def dipole_rows(mu, pos, mixed, own):
    dots = pos[0] * mu[0] + pos[1] * mu[1] + pos[2] * mu[2]
    tripled = 3.0 * mixed
    left = jnp.concatenate([tripled * mu[0], tripled * mu[1], tripled * mu[2], tripled * dots], 0)
    blank = jnp.zeros((16, TILE), BF16)
    right = jnp.concatenate([jnp.zeros((8, TILE), F32), -own], 0)
    out = []
    for l, r in zip(three_parts(left), three_parts(right)):
        out.append(jnp.concatenate([l, jnp.concatenate([blank, r], 0)], 1))
    return jnp.concatenate(out[:PARTS], 0)


def geometry_rows(first_three, fourth, fifth):
    sub = lax.broadcasted_iota(jnp.int32, (8, TILE), 0)
    rows = jnp.where(sub == 0, first_three[0], jnp.where(sub == 1, first_three[1], jnp.where(sub == 2, first_three[2], jnp.where(sub == 3, fourth, jnp.where(sub == 4, fifth, 0.0)))))
    return tuple(p.astype(F32) for p in three_parts(rows))


def scale_rows(scale, pattern):
    sub = lax.broadcasted_iota(jnp.int32, (8, TILE), 0)
    parts = [p.astype(F32) for p in three_parts(scale)]
    out = jnp.zeros((8, TILE), F32)
    for row, part in enumerate(pattern):
        out = jnp.where(sub == row, parts[part], out)
    return out


def squared(pos):
    return pos[0] * pos[0] + pos[1] * pos[1] + pos[2] * pos[2]


def assemble(parts, pos, mixed):
    sub, second, _, _, _ = rows_of()
    g = pos[0] * parts[0] + pos[1] * parts[1] + pos[2] * parts[2] - parts[3]
    s0 = jnp.broadcast_to(g[6:7], (8, TILE))
    s1 = jnp.broadcast_to(g[7:8], (8, TILE))
    s = jnp.where(second, s1, s0)
    return mixed * s - g


def kernel(
    lists_ref, low_ref, mid_ref, high_ref, out_ref,
    copy_sem, x_ref, geo_ref, dip_ref, acc_ref, eye_ref, near_ref, far_ref, dist_ref, coef_ref,
):
    eye = (
        lax.broadcasted_iota(jnp.int32, (TILE, TILE), 0) == lax.broadcasted_iota(jnp.int32, (TILE, TILE), 1)
    )
    eye16 = jnp.where(eye, 1.0, 0.0).astype(BF16)
    zero8 = jnp.zeros((8, TILE), F32)
    own_base = 4 * ROWS
    copies = []
    for column, source in enumerate((low_ref, mid_ref, high_ref)):
        for row in range(3):
            place = x_ref.at[pl.ds((3 * row + column) * ROWS, ROWS), :]
            copies.append(pltpu.make_async_copy(source.at[row], place, copy_sem.at[3 * row + column]))
            copies[-1].start()
    nt = (((1,), (1,)), ((), ()))
    eye_ref[0] = jnp.zeros((TILE, 2 * TILE), BF16)
    eye_ref[1] = jnp.concatenate(
        [jnp.where(eye, FAR_AWAY, 0.0).astype(BF16), jnp.zeros((TILE, TILE), BF16)], 1
    )

    def clear(i, _):
        out_ref[pl.ds(pl.multiple_of(i * 64, 64), 64), :] = jnp.zeros((64, TILE), F32)
        return 0

    lax.fori_loop(0, out_ref.shape[0] // 64, clear, 0)
    for copy in copies:
        copy.wait()

    def prepare(t, _):
        centre = (8.0, 8.0, (4 * t + 2).astype(F32))
        mu, pos, pol, mixed, own = site_vectors(x_ref, own_base + t, centre)
        dip_ref[t] = dipole_rows(mu, pos, mixed, own)
        hi, mid, lo = geometry_rows([-2.0 * p for p in pos], 1.0, squared(pos))
        scale = (-thole) * lax.rsqrt(pol)
        q = scale_rows(scale, (0, 1, 0, 1, 0, 2))
        stack = jnp.concatenate([hi, mid, hi, mid, hi, lo, q, zero8], 0).astype(BF16)
        moved = lax.dot_general(eye16, stack, nt, preferred_element_type=F32).astype(BF16)
        geo_ref[t] = jnp.concatenate([moved, eye16], 1)
        acc_ref[t] = jnp.zeros((32, TILE), F32)
        return 0

    lax.fori_loop(0, TILES, prepare, 0, unroll=4)
    geo_ref[DUMMY] = geo_ref[0]
    dip_ref[DUMMY] = dip_ref[0]

    def blank(first):
        for k in range(first[1]):
            near_ref[first[0] + k] = DUMMY
            far_ref[first[0] + k] = 4 * TILES

    blank((0, 2 * UNROLL))
    total = jnp.int32(2 * UNROLL)
    for g in range(9):
        first = lists_ref[3 * g + 2, 8 - g]
        last = lists_ref[3 * g + 2, 9 - g]

        def place(p, at, g=g):
            near_ref[at] = lists_ref[3 * g, p] & (TILES - 1)
            far_ref[at] = lists_ref[3 * g + 1, p] + g * TILES
            return at + 1

        total = lax.fori_loop(first, last, place, total)
    blank((total, 3 * UNROLL))
    groups = (total - 2 * UNROLL + UNROLL - 1) // UNROLL

    def origin(home, far):
        grid = far // TILES
        row = (grid * 11) // 32
        column = grid - 3 * row
        return (
            8.0 - domain_edge * (row - 1).astype(F32),
            8.0 - domain_edge * (column - 1).astype(F32),
            (4 * home + 2).astype(F32),
        )

    def distances(u, at):
        home = near_ref[at]
        far = far_ref[at]
        grid = far // TILES
        base = grid * ROWS + (far - grid * TILES)
        pos = [load_row(x_ref, base + (6 + k) * TILES) - c for k, c in enumerate(origin(home, far))]
        pol = load_row(x_ref, base + 9 * TILES)
        hi, mid, lo = geometry_rows(pos, squared(pos), 1.0)
        q = scale_rows(lax.rsqrt(pol), (0, 0, 1, 1, 2, 0))
        left = jnp.concatenate([hi, hi, mid, mid, lo, hi, zero8, zero8], 0).astype(BF16)
        right = jnp.concatenate([jnp.zeros((48, TILE), F32), q, zero8], 0).astype(BF16)
        same = (far == 4 * TILES + home).astype(jnp.int32)
        operand = jnp.concatenate([jnp.concatenate([left, right], 1), eye_ref[same]], 0)
        dist_ref[u] = jnp.dot(geo_ref[home], operand, preferred_element_type=F32)

    def coefficients(u):
        dist_sq = dist_ref[u, :, :TILE]
        inv = lax.rsqrt(dist_sq)
        inv_sq = inv * inv
        inv_cube = inv_sq * inv
        cube = dist_sq * inv * dist_sq
        damp = cube * dist_ref[u, :, TILE:]
        decay = jnp.exp(damp)
        lam_three = 1.0 - decay
        lam_five = lam_three + damp * decay
        three = lam_three * inv_cube
        five = lam_five * inv_cube * inv_sq
        three_hi = three.astype(BF16)
        five_hi = five.astype(BF16)
        coef_ref[u, 0] = five_hi
        coef_ref[u, 1] = (five - five_hi.astype(F32)).astype(BF16)
        coef_ref[u, 2] = three_hi
        coef_ref[u, 3] = (three - three_hi.astype(F32)).astype(BF16)

    def folded(sums):
        total = sums[0:32, :TILE]
        for k in range(1, PARTS):
            total = total + (sums[32 * k:32 * k + 32, :TILE] + sums[32 * k - 32:32 * k, TILE:])
        return total

    def sums(u, at):
        home = near_ref[at]
        far = far_ref[at]
        grid = far // TILES
        remote = far - grid * TILES
        mu, pos, pol, mixed, own = site_vectors(x_ref, grid * ROWS + remote, origin(home, far))
        rem = dipole_rows(mu, pos, mixed, own)
        five_hi, five_lo, three_hi, three_lo = [coef_ref[u, k] for k in range(4)]
        square = jnp.concatenate(
            [jnp.concatenate([five_hi, three_hi], 1), jnp.concatenate([five_lo, three_lo], 1)], 0
        )
        h = folded(lax.dot_general(rem, square, nt, preferred_element_type=F32))
        square = jnp.concatenate(
            [jnp.concatenate([five_hi, five_lo], 1), jnp.concatenate([three_hi, three_lo], 1)], 0
        )
        r = folded(jnp.dot(dip_ref[home], square, preferred_element_type=F32))
        field = assemble([r[8 * j:8 * j + 8] for j in range(4)], pos, mixed)
        unused = (home == DUMMY) | (far == 4 * TILES + home)
        target = jnp.where(unused, 4 * OUT_ROWS + DUMMY, grid * OUT_ROWS + remote)
        return home, target, h, field

    def step(i, _):
        first = i * UNROLL
        done = [sums(u, first + u) for u in range(UNROLL)]
        for u in range(UNROLL):
            coefficients(u)
        for u in range(UNROLL):
            distances(u, first + 2 * UNROLL + u)
        for home, target, h, field in done:
            acc_ref[home] += h
            out_ref[pl.ds(target, 8, stride=OUT_STRIDE), :] += field
        return 0

    lax.fori_loop(0, groups + 2, step, 0)

    def finish(t, _):
        centre = (8.0, 8.0, (4 * t + 2).astype(F32))
        mu, pos, pol, mixed, own = site_vectors(x_ref, own_base + t, centre)
        field = assemble([acc_ref[t, 8 * j:8 * j + 8] for j in range(4)], pos, mixed)
        out_ref[pl.ds(4 * OUT_ROWS + t, 8, stride=OUT_STRIDE), :] += field
        return 0

    lax.fori_loop(0, TILES, finish, 0, unroll=4)


FAR_AWAY = 2.0 ** 60
LIST = 9 * 2048 + 5 * UNROLL
OUT_STRIDE = TILES + 8
OUT_ROWS = 8 * OUT_STRIDE


def field_kernel(lists, low, middle, high):
    smem = pl.BlockSpec(memory_space=pltpu.SMEM)
    away = pl.BlockSpec(memory_space=pl.ANY)
    vmem = pl.BlockSpec(memory_space=pltpu.VMEM)
    return pl.pallas_call(
        kernel,
        out_shape=jax.ShapeDtypeStruct((9 * OUT_ROWS, TILE), F32),
        in_specs=[smem, away, away, away],
        out_specs=vmem,
        scratch_shapes=[
            pltpu.SemaphoreType.DMA((9,)),
            pltpu.VMEM((9 * ROWS, TILE), F32),
            pltpu.VMEM((TILES + 1, TILE, 64 + TILE), BF16),
            pltpu.VMEM((TILES + 1, 32 * PARTS, 2 * TILE), BF16),
            pltpu.VMEM((TILES + 1, 32, TILE), F32),
            pltpu.VMEM((2, TILE, 2 * TILE), BF16),
            pltpu.SMEM((LIST,), jnp.int32),
            pltpu.SMEM((LIST,), jnp.int32),
            pltpu.VMEM((UNROLL, TILE, 2 * TILE), F32),
            pltpu.VMEM((UNROLL, 4, TILE, TILE), BF16),
        ],
        compiler_params=pltpu.CompilerParams(vmem_limit_bytes=63 * 1024 * 1024),
        name="pair_fields",
    )(lists, low, middle, high)


def around(value, axis):
    count = lax.axis_size(axis)
    forward = [(i, (i + 1) % count) for i in range(count)]
    backward = [((i + 1) % count, i) for i in range(count)]
    return [lax.ppermute(value, axis, forward), value, lax.ppermute(value, axis, backward)]


def shifted(value, axis, steps):
    count = lax.axis_size(axis)
    pairs = [(source, (source + steps) % count) for source in range(count)]
    return lax.ppermute(value, axis, pairs)


def local(positions, polarity, dipoles, perm_fields, pair_list, tile_counts):
    slot_total = pair_list.shape[3]
    sites = jnp.concatenate([dipoles, positions, polarity[None]], 0).reshape(1, 10 * TILES, TILE)
    rows = jnp.concatenate(around(sites, "gx"), 0)
    columns = around(rows, "gy")

    table = pair_list.reshape(2, slot_total)
    live = jnp.arange(slot_total, dtype=jnp.int32) < tile_counts.reshape(())
    far = jnp.where(live, table[1], 16 * TILES)
    far, near = lax.sort((far, table[0]), num_keys=1)
    bounds = jnp.arange(slot_total, dtype=jnp.int32)[:16] * TILES
    bounds = jnp.sum((far[None, :] < bounds[:, None]).astype(jnp.int32), 1)
    bounds = jnp.concatenate([bounds, jnp.zeros((slot_total - 16,), jnp.int32)])
    lists = jnp.stack([far, near, bounds])[None]
    lists = jnp.concatenate(around(lists, "gx"), 0)[:, None]
    lists = jnp.concatenate(around(lists, "gy"), 1).reshape(27, slot_total)
    terms = field_kernel(lists, *columns)
    terms = terms.reshape(3, 3, 8, OUT_STRIDE, TILE)[:, :, :6, :TILES]
    column = terms[:, 1] + shifted(terms[:, 0], "gy", -1) + shifted(terms[:, 2], "gy", 1)
    field = column[1] + shifted(column[0], "gx", -1) + shifted(column[2], "gx", 1)
    field = field.reshape(6, 1, 1, TILES * TILE)
    induced = polarity[None] * (perm_fields + field)
    return (field, induced)


def solution(mesh):
    placed = (
        P(None, "gx", "gy", None),
        P("gx", "gy", None),
        P(None, "gx", "gy", None),
        P(None, "gx", "gy", None),
        P("gx", "gy", None, None),
        P("gx", "gy"),
    )
    return jax.shard_map(
        local,
        mesh=mesh,
        in_specs=placed,
        out_specs=(P(None, "gx", "gy", None), P(None, "gx", "gy", None)),
        check_vma=False,
    )
```

```python
import jax
import jax.numpy as jnp
from jax import lax
from jax.experimental import pallas as pl
from jax.experimental.pallas import tpu as pltpu
from jax.sharding import PartitionSpec as P

TILE = 128
TILES = 256
ROWS = 10 * TILES
UNROLL = 2
HALVES = 6
PARTS = 3
DUMMY = TILES

thole = 0.39
domain_edge = 16.0

F32 = jnp.float32
BF16 = jnp.bfloat16


def three_parts(value):
    high = value.astype(BF16)
    rest = value - high.astype(F32)
    middle = rest.astype(BF16)
    low = (rest - middle.astype(F32)).astype(BF16)
    return high, middle, low


def rows_of():
    sub = lax.broadcasted_iota(jnp.int32, (8, TILE), 0)
    second = (sub == 3) | (sub == 4) | (sub == 5) | (sub == 7)
    is_x = (sub == 0) | (sub == 3)
    is_y = (sub == 1) | (sub == 4)
    is_z = (sub == 2) | (sub == 5)
    return sub, second, is_x, is_y, is_z


def load_row(ref, row):
    return jnp.broadcast_to(ref[pl.ds(row, 1), :], (8, TILE))


def site_vectors(ref, base, centre):
    sub, second, is_x, is_y, is_z = rows_of()
    dips = [load_row(ref, base + k * TILES) for k in range(6)]
    pos = [load_row(ref, base + (6 + k) * TILES) - centre[k] for k in range(3)]
    pol = load_row(ref, base + 9 * TILES)
    mu = [jnp.where(second, dips[3 + j], dips[j]) for j in range(3)]
    mixed = jnp.where(is_x, pos[0], jnp.where(is_y, pos[1], jnp.where(is_z, pos[2], 1.0)))
    own = jnp.where(is_x, mu[0], jnp.where(is_y, mu[1], jnp.where(is_z, mu[2], 0.0)))
    return mu, pos, pol, mixed, own


def dipole_rows(mu, pos, mixed, own):
    dots = pos[0] * mu[0] + pos[1] * mu[1] + pos[2] * mu[2]
    tripled = 3.0 * mixed
    left = jnp.concatenate([tripled * mu[0], tripled * mu[1], tripled * mu[2], tripled * dots], 0)
    blank = jnp.zeros((16, TILE), BF16)
    right = jnp.concatenate([jnp.zeros((8, TILE), F32), -own], 0)
    out = []
    for l, r in zip(three_parts(left), three_parts(right)):
        out.append(jnp.concatenate([l, jnp.concatenate([blank, r], 0)], 1))
    return jnp.concatenate(out[:PARTS], 0)


def geometry_rows(first_three, fourth, fifth):
    sub = lax.broadcasted_iota(jnp.int32, (8, TILE), 0)
    rows = jnp.where(sub == 0, first_three[0], jnp.where(sub == 1, first_three[1], jnp.where(sub == 2, first_three[2], jnp.where(sub == 3, fourth, jnp.where(sub == 4, fifth, 0.0)))))
    return tuple(p.astype(F32) for p in three_parts(rows))


def scale_rows(scale, pattern):
    sub = lax.broadcasted_iota(jnp.int32, (8, TILE), 0)
    parts = [p.astype(F32) for p in three_parts(scale)]
    out = jnp.zeros((8, TILE), F32)
    for row, part in enumerate(pattern):
        out = jnp.where(sub == row, parts[part], out)
    return out


def squared(pos):
    return pos[0] * pos[0] + pos[1] * pos[1] + pos[2] * pos[2]


def assemble(parts, pos, mixed):
    sub, second, _, _, _ = rows_of()
    g = pos[0] * parts[0] + pos[1] * parts[1] + pos[2] * parts[2] - parts[3]
    s0 = jnp.broadcast_to(g[6:7], (8, TILE))
    s1 = jnp.broadcast_to(g[7:8], (8, TILE))
    s = jnp.where(second, s1, s0)
    return mixed * s - g


def kernel(
    lists_ref, split_ref, *refs
):
    sources, refs = refs[:9], refs[9:]
    outs, refs = refs[:3], refs[3:]
    (
    out_ref, copy_sem, out_sem, x_ref, geo_ref, dip_ref, acc_ref, eye_ref, near_ref, base_ref, target_ref, grid_ref, dist_even, dist_odd, coef_even, coef_odd,
    ) = refs
    eye = (
        lax.broadcasted_iota(jnp.int32, (TILE, TILE), 0) == lax.broadcasted_iota(jnp.int32, (TILE, TILE), 1)
    )
    eye16 = jnp.where(eye, 1.0, 0.0).astype(BF16)
    zero8 = jnp.zeros((8, TILE), F32)
    own_base = 4 * ROWS
    copies = []
    for g, source in enumerate(sources):
        place = x_ref.at[pl.ds(g * ROWS, ROWS), :]
        copies.append(pltpu.make_async_copy(source, place, copy_sem.at[g]))
        copies[-1].start()
    nt = (((1,), (1,)), ((), ()))
    eye_ref[0] = jnp.zeros((TILE, 2 * TILE), BF16)
    eye_ref[1] = jnp.concatenate(
        [jnp.where(eye, FAR_AWAY, 0.0).astype(BF16), jnp.zeros((TILE, TILE), BF16)], 1
    )

    eye_ref[2] = jnp.concatenate([eye16, eye16], 1)

    def clear(i, _):
        out_ref[pl.ds(pl.multiple_of(i * 64, 64), 64), :] = jnp.zeros((64, TILE), F32)
        return 0

    lax.fori_loop(0, out_ref.shape[0] // 64, clear, 0)
    copies[4].wait()

    def prepare(t, _):
        centre = (8.0, 8.0, (4 * t + 2).astype(F32))
        mu, pos, pol, mixed, own = site_vectors(x_ref, own_base + t, centre)
        dip_ref[t] = dipole_rows(mu, pos, mixed, own)
        hi, mid, lo = geometry_rows([-2.0 * p for p in pos], 1.0, squared(pos))
        scale = (-thole) * lax.rsqrt(pol)
        q = scale_rows(scale, (0, 1, 0, 1, 0, 2))
        stack = jnp.concatenate([hi, mid, hi, mid, hi, lo, q, zero8], 0).astype(BF16)
        moved = lax.dot_general(eye16, stack, nt, preferred_element_type=F32).astype(BF16)
        geo_ref[t] = moved
        acc_ref[t] = jnp.zeros((32, TILE), F32)
        return 0

    lax.fori_loop(0, TILES, prepare, 0, unroll=4)
    for g in range(9):
        if g != 4:
            copies[g].wait()
    geo_ref[DUMMY] = geo_ref[0]
    dip_ref[DUMMY] = dip_ref[0]

    def blank(at):
        near_ref[at] = DUMMY
        base_ref[at] = own_base
        target_ref[at] = UNUSED
        grid_ref[at] = 4

    for k in range(2 * UNROLL):
        blank(k)
    total = jnp.int32(2 * UNROLL)
    def put(at, home, remote, g):
        target = remote + g * OUT_ROWS
        if g == 4:
            target = jnp.where(remote == home, UNUSED, target)
        near_ref[at] = home
        base_ref[at] = remote + g * ROWS
        target_ref[at] = target
        grid_ref[at] = g
        return at + 1

    for g in range(9):
        first = lists_ref[3 * g + 2, 8 - g]
        last = lists_ref[3 * g + 2, 9 - g]
        if g != 4:
            last = first + split_ref[g]

        def incoming(p, at, g=g):
            return put(at, lists_ref[3 * g, p] & (TILES - 1), lists_ref[3 * g + 1, p], g)

        total = lax.fori_loop(first, last, incoming, total)
        if g != 4:
            first = lists_ref[14, g] + split_ref[9 + g]
            last = lists_ref[14, g + 1]

            def kept(p, at, g=g):
                return put(at, lists_ref[13, p], lists_ref[12, p] & (TILES - 1), g)

            total = lax.fori_loop(first, last, kept, total)
    for k in range((HALVES + 2) * UNROLL):
        blank(total + k)
    groups = (total - 2 * UNROLL + UNROLL - 1) // UNROLL

    def origin(at):
        grid = grid_ref[at]
        row = (grid * 11) // 32
        column = grid - 3 * row
        return (
            24.0 - domain_edge * row.astype(F32),
            24.0 - domain_edge * column.astype(F32),
            (4 * near_ref[at] + 2).astype(F32),
        )

    def distances(dist_ref, u, at):
        base = base_ref[at]
        pos = [load_row(x_ref, base + (6 + k) * TILES) - c for k, c in enumerate(origin(at))]
        pol = load_row(x_ref, base + 9 * TILES)
        hi, mid, lo = geometry_rows(pos, squared(pos), 1.0)
        q = scale_rows(lax.rsqrt(pol), (0, 0, 1, 1, 2, 0))
        left = jnp.concatenate([hi, hi, mid, mid, lo, hi, zero8, zero8], 0).astype(BF16)
        right = jnp.concatenate([jnp.zeros((48, TILE), F32), q, zero8], 0).astype(BF16)
        same = (target_ref[at] == UNUSED).astype(jnp.int32)
        operand = jnp.concatenate([eye_ref[same], jnp.concatenate([left, right], 1)], 0)
        rows = jnp.concatenate([eye_ref[2, :, :TILE], geo_ref[near_ref[at]]], 1)
        dist_ref[u] = jnp.dot(rows, operand, preferred_element_type=F32)

    def coefficients(dist_ref, coef_ref, u):
        dist_sq = dist_ref[u, :, :TILE]
        inv = lax.rsqrt(dist_sq)
        inv_sq = inv * inv
        inv_cube = inv_sq * inv
        cube = dist_sq * inv * dist_sq
        damp = cube * dist_ref[u, :, TILE:]
        decay = jnp.exp(damp)
        lam_three = 1.0 - decay
        lam_five = lam_three + damp * decay
        three = lam_three * inv_cube
        five = lam_five * inv_cube * inv_sq
        three_hi = three.astype(BF16)
        five_hi = five.astype(BF16)
        coef_ref[u, 0] = five_hi
        coef_ref[u, 1] = (five - five_hi.astype(F32)).astype(BF16)
        coef_ref[u, 2] = three_hi
        coef_ref[u, 3] = (three - three_hi.astype(F32)).astype(BF16)

    def folded(sums):
        total = sums[0:32, :TILE]
        for k in range(1, PARTS):
            total = total + (sums[32 * k:32 * k + 32, :TILE] + sums[32 * k - 32:32 * k, TILE:])
        return total

    def sums(coef_ref, u, at):
        mu, pos, pol, mixed, own = site_vectors(x_ref, base_ref[at], origin(at))
        rem = dipole_rows(mu, pos, mixed, own)
        five_hi, five_lo, three_hi, three_lo = [coef_ref[u, k] for k in range(4)]
        square = jnp.concatenate(
            [jnp.concatenate([five_hi, three_hi], 1), jnp.concatenate([five_lo, three_lo], 1)], 0
        )
        h = folded(lax.dot_general(rem, square, nt, preferred_element_type=F32))
        square = jnp.concatenate(
            [jnp.concatenate([five_hi, five_lo], 1), jnp.concatenate([three_hi, three_lo], 1)], 0
        )
        r = folded(jnp.dot(dip_ref[near_ref[at]], square, preferred_element_type=F32))
        field = assemble([r[8 * j:8 * j + 8] for j in range(4)], pos, mixed)
        return near_ref[at], target_ref[at], h, field

    def half(first, dist_now, dist_next, coef_now, coef_next):
        done = [sums(coef_now, u, first + u) for u in range(UNROLL)]
        for u in range(UNROLL):
            coefficients(dist_now, coef_next, u)
        for u in range(UNROLL):
            distances(dist_next, u, first + 2 * UNROLL + u)
        for home, target, h, field in done:
            acc_ref[home] += h
            out_ref[pl.ds(target, 8, stride=OUT_STRIDE), :] += field

    even = (dist_even, dist_odd, coef_even, coef_odd)
    odd = (dist_odd, dist_even, coef_odd, coef_even)

    def step(i, _):
        for k in range(HALVES):
            half((HALVES * i + k) * UNROLL, *(odd if k % 2 else even))
        return 0

    lax.fori_loop(0, (groups + 1 + HALVES) // HALVES, step, 0)

    sends = []
    for g in range(9):
        for k in range(6):
            source = out_ref.at[pl.ds(g * OUT_ROWS + k * OUT_STRIDE, TILES), :]
            place = outs[g % 3].at[g // 3, k]
            sends.append(pltpu.make_async_copy(source, place, out_sem.at[6 * g + k]))
    for k, send in enumerate(sends):
        if k // 6 != 4:
            send.start()

    def finish(t, _):
        centre = (8.0, 8.0, (4 * t + 2).astype(F32))
        mu, pos, pol, mixed, own = site_vectors(x_ref, own_base + t, centre)
        field = assemble([acc_ref[t, 8 * j:8 * j + 8] for j in range(4)], pos, mixed)
        out_ref[pl.ds(4 * OUT_ROWS + t, 8, stride=OUT_STRIDE), :] += field
        return 0

    lax.fori_loop(0, TILES, finish, 0, unroll=4)
    for send in sends[24:30]:
        send.start()
    for send in sends:
        send.wait()


FAR_AWAY = 2.0 ** 60
LIST = 18 * 2048 + (HALVES + 4) * UNROLL
OUT_STRIDE = TILES + 8
OUT_ROWS = 8 * OUT_STRIDE
UNUSED = 4 * OUT_ROWS + DUMMY


def field_kernel(lists, split, *sites):
    smem = pl.BlockSpec(memory_space=pltpu.SMEM)
    away = pl.BlockSpec(memory_space=pl.ANY)
    return pl.pallas_call(
        kernel,
        out_shape=[jax.ShapeDtypeStruct((3, 6, TILES, TILE), F32)] * 3,
        in_specs=[smem, smem] + [away] * 9,
        out_specs=[away] * 3,
        scratch_shapes=[
            pltpu.VMEM((9 * OUT_ROWS, TILE), F32),
            pltpu.SemaphoreType.DMA((9,)),
            pltpu.SemaphoreType.DMA((54,)),
            pltpu.VMEM((9 * ROWS, TILE), F32),
            pltpu.VMEM((TILES + 1, TILE, 64), BF16),
            pltpu.VMEM((TILES + 1, 32 * PARTS, 2 * TILE), BF16),
            pltpu.VMEM((TILES + 1, 32, TILE), F32),
            pltpu.VMEM((3, TILE, 2 * TILE), BF16),
            pltpu.SMEM((LIST,), jnp.int32),
            pltpu.SMEM((LIST,), jnp.int32),
            pltpu.SMEM((LIST,), jnp.int32),
            pltpu.SMEM((LIST,), jnp.int32),
            pltpu.VMEM((UNROLL, TILE, 2 * TILE), F32),
            pltpu.VMEM((UNROLL, TILE, 2 * TILE), F32),
            pltpu.VMEM((UNROLL, 4, TILE, TILE), BF16),
            pltpu.VMEM((UNROLL, 4, TILE, TILE), BF16),
        ],
        compiler_params=pltpu.CompilerParams(vmem_limit_bytes=63 * 1024 * 1024),
        name="pair_fields",
    )(lists, split, *sites)


def grid_roll(value, row, column):
    if row:
        value = pltpu.roll(value, (-row) % 8, 0)
    if column:
        value = pltpu.roll(value, (-column) % TILE, 1)
    return value


def balance_kernel(counts_ref, split_ref):
    steps = [(s // 3 - 1, s % 3 - 1) for s in range(9)]
    counts = [counts_ref[8 * s:8 * s + 8, :] for s in range(9)]
    others = [s for s in range(9) if s != 4]

    def arriving(given, s):
        return grid_roll(given, -steps[s][0], -steps[s][1])

    def relax(_, given):
        load = counts[4]
        for s, part in zip(others, given):
            load = load + (counts[s] - part) + arriving(part, s)
        out = []
        for s, part in zip(others, given):
            excess = load - grid_roll(load, *steps[s])
            out.append(jnp.clip(part + excess * 0.055, 0.0, counts[s]))
        return tuple(out)

    given = lax.fori_loop(0, 32, relax, tuple(counts[s] for s in others))
    zero = jnp.zeros((8, TILE), F32)
    split_ref[32:40, :] = zero
    split_ref[104:112, :] = zero
    for s, part in zip(others, given):
        part = jnp.floor(part)
        g = 8 - s
        split_ref[8 * g:8 * g + 8, :] = arriving(part, s)
        split_ref[72 + 8 * s:80 + 8 * s, :] = part


def balance(counts):
    return pl.pallas_call(
        balance_kernel,
        out_shape=jax.ShapeDtypeStruct((144, TILE), F32),
        name="balance",
    )(counts)


def around(value, axis):
    count = lax.axis_size(axis)
    forward = [(i, (i + 1) % count) for i in range(count)]
    backward = [((i + 1) % count, i) for i in range(count)]
    return [lax.ppermute(value, axis, forward), value, lax.ppermute(value, axis, backward)]


def shifted(value, axis, steps):
    count = lax.axis_size(axis)
    pairs = [(source, (source + steps) % count) for source in range(count)]
    return lax.ppermute(value, axis, pairs)


def local(positions, polarity, dipoles, perm_fields, pair_list, tile_counts):
    slot_total = pair_list.shape[3]
    sites = jnp.concatenate([dipoles, positions, polarity[None]], 0).reshape(10 * TILES, TILE)

    table = pair_list.reshape(2, slot_total)
    live = jnp.arange(slot_total, dtype=jnp.int32) < tile_counts.reshape(())
    far = jnp.where(live, table[1], 16 * TILES)
    far, near = lax.sort((far, table[0]), num_keys=1)
    bounds = jnp.arange(slot_total, dtype=jnp.int32)[:16] * TILES
    bounds = jnp.sum((far[None, :] < bounds[:, None]).astype(jnp.int32), 1)
    counts = (bounds[1:10] - bounds[:9]).astype(F32)
    bounds = jnp.concatenate([bounds, jnp.zeros((slot_total - 16,), jnp.int32)])
    lists = jnp.stack([far, near, bounds])[None]
    lists = jnp.concatenate(around(lists, "gx"), 0)[:, None]

    middle = around(sites, "gx")
    sides = around(sites, "gy")
    middle[0], middle[2], lists, sides[0], sides[2] = lax.optimization_barrier(
        (middle[0], middle[2], lists, sides[0], sides[2])
    )
    lists = jnp.concatenate(around(lists, "gy"), 1).reshape(27, slot_total)
    everyone = lax.all_gather(lax.all_gather(counts, "gy"), "gx")
    everyone = jnp.tile(everyone.transpose(2, 0, 1), (1, 1, 8)).reshape(72, TILE)
    split = balance(everyone).reshape(18, 8, TILE)
    here = (0, lax.axis_index("gx"), lax.axis_index("gy"))
    split = lax.dynamic_slice(split, here, (18, 1, 1)).reshape(18).astype(jnp.int32)
    upper = around(middle[0], "gy")
    lower = around(middle[2], "gy")
    low, mid, high = field_kernel(lists, split, *upper, *sides, *lower)
    column = mid + shifted(low, "gy", -1) + shifted(high, "gy", 1)
    field = column[1] + shifted(column[0], "gx", -1) + shifted(column[2], "gx", 1)
    field = field.reshape(6, 1, 1, TILES * TILE)
    induced = polarity[None] * (perm_fields + field)
    return (field, induced)


def solution(mesh):
    placed = (
        P(None, "gx", "gy", None),
        P("gx", "gy", None),
        P(None, "gx", "gy", None),
        P(None, "gx", "gy", None),
        P("gx", "gy", None, None),
        P("gx", "gy"),
    )
    return jax.shard_map(
        local,
        mesh=mesh,
        in_specs=placed,
        out_specs=(P(None, "gx", "gy", None), P(None, "gx", "gy", None)),
        check_vma=False,
    )
```

```python
import jax
import jax.numpy as jnp
from jax import lax
from jax.experimental import pallas as pl
from jax.experimental.pallas import tpu as pltpu
from jax.sharding import PartitionSpec as P

TILE = 128
TILES = 256
ROWS = 10 * TILES
UNROLL = 2
HALVES = 6
PARTS = 3
DUMMY = TILES
GRID = 2 * TILES

thole = 0.39
domain_edge = 16.0

F32 = jnp.float32
BF16 = jnp.bfloat16


def three_parts(value):
    high = value.astype(BF16)
    rest = value - high.astype(F32)
    middle = rest.astype(BF16)
    low = (rest - middle.astype(F32)).astype(BF16)
    return high, middle, low


def rows_of():
    sub = lax.broadcasted_iota(jnp.int32, (8, TILE), 0)
    second = (sub == 3) | (sub == 4) | (sub == 5) | (sub == 7)
    is_x = (sub == 0) | (sub == 3)
    is_y = (sub == 1) | (sub == 4)
    is_z = (sub == 2) | (sub == 5)
    return sub, second, is_x, is_y, is_z


def load_row(ref, row):
    return jnp.broadcast_to(ref[pl.ds(row, 1), :], (8, TILE))


def site_vectors(ref, base, centre):
    sub, second, is_x, is_y, is_z = rows_of()
    dips = [load_row(ref, base + k * TILES) for k in range(6)]
    pos = [load_row(ref, base + (6 + k) * TILES) - centre[k] for k in range(3)]
    pol = load_row(ref, base + 9 * TILES)
    mu = [jnp.where(second, dips[3 + j], dips[j]) for j in range(3)]
    mixed = jnp.where(is_x, pos[0], jnp.where(is_y, pos[1], jnp.where(is_z, pos[2], 1.0)))
    own = jnp.where(is_x, mu[0], jnp.where(is_y, mu[1], jnp.where(is_z, mu[2], 0.0)))
    return mu, pos, pol, mixed, own


def dipole_rows(mu, pos, mixed, own):
    dots = pos[0] * mu[0] + pos[1] * mu[1] + pos[2] * mu[2]
    tripled = 3.0 * mixed
    left = jnp.concatenate([tripled * mu[0], tripled * mu[1], tripled * mu[2], tripled * dots], 0)
    blank = jnp.zeros((16, TILE), BF16)
    right = jnp.concatenate([jnp.zeros((8, TILE), F32), -own], 0)
    out = []
    for l, r in zip(three_parts(left), three_parts(right)):
        out.append(jnp.concatenate([l, jnp.concatenate([blank, r], 0)], 1))
    return jnp.concatenate(out[:PARTS], 0)


def geometry_rows(first_three, fourth, fifth):
    sub = lax.broadcasted_iota(jnp.int32, (8, TILE), 0)
    rows = jnp.where(sub == 0, first_three[0], jnp.where(sub == 1, first_three[1], jnp.where(sub == 2, first_three[2], jnp.where(sub == 3, fourth, jnp.where(sub == 4, fifth, 0.0)))))
    return tuple(p.astype(F32) for p in three_parts(rows))


def scale_rows(scale, pattern):
    sub = lax.broadcasted_iota(jnp.int32, (8, TILE), 0)
    parts = [p.astype(F32) for p in three_parts(scale)]
    out = jnp.zeros((8, TILE), F32)
    for row, part in enumerate(pattern):
        out = jnp.where(sub == row, parts[part], out)
    return out


def squared(pos):
    return pos[0] * pos[0] + pos[1] * pos[1] + pos[2] * pos[2]


def assemble(parts, pos, mixed):
    sub, second, _, _, _ = rows_of()
    g = pos[0] * parts[0] + pos[1] * parts[1] + pos[2] * parts[2] - parts[3]
    s0 = jnp.broadcast_to(g[6:7], (8, TILE))
    s1 = jnp.broadcast_to(g[7:8], (8, TILE))
    s = jnp.where(second, s1, s0)
    return mixed * s - g


def kernel(
    lists_ref, *refs
):
    sources, refs = refs[:9], refs[9:]
    outs, refs = refs[:3], refs[3:]
    (
    out_ref, copy_sem, out_sem, x_ref, geo_ref, dip_ref, acc_ref, eye_ref, near_ref, base_ref, target_ref, dist_even, dist_odd, coef_even, coef_odd,
    ) = refs
    eye = (
        lax.broadcasted_iota(jnp.int32, (TILE, TILE), 0) == lax.broadcasted_iota(jnp.int32, (TILE, TILE), 1)
    )
    eye16 = jnp.where(eye, 1.0, 0.0).astype(BF16)
    zero8 = jnp.zeros((8, TILE), F32)
    own_base = 4 * ROWS
    copies = []
    for g, source in enumerate(sources):
        place = x_ref.at[pl.ds(g * ROWS, ROWS), :]
        copies.append(pltpu.make_async_copy(source, place, copy_sem.at[g]))
        copies[-1].start()
    nt = (((1,), (1,)), ((), ()))
    eye_ref[0] = jnp.zeros((TILE, 2 * TILE), BF16)
    eye_ref[1] = jnp.concatenate(
        [jnp.where(eye, FAR_AWAY, 0.0).astype(BF16), jnp.zeros((TILE, TILE), BF16)], 1
    )

    eye_ref[2] = jnp.concatenate([eye16, eye16], 1)

    def clear(i, _):
        out_ref[pl.ds(pl.multiple_of(i * 64, 64), 64), :] = jnp.zeros((64, TILE), F32)
        return 0

    lax.fori_loop(0, out_ref.shape[0] // 64, clear, 0)
    copies[4].wait()

    def prepare(t, _):
        centre = (8.0, 8.0, (4 * t + 2).astype(F32))
        mu, pos, pol, mixed, own = site_vectors(x_ref, own_base + t, centre)
        dip_ref[t] = dipole_rows(mu, pos, mixed, own)
        hi, mid, lo = geometry_rows([-2.0 * p for p in pos], 1.0, squared(pos))
        scale = (-thole) * lax.rsqrt(pol)
        q = scale_rows(scale, (0, 1, 0, 1, 0, 2))
        stack = jnp.concatenate([hi, mid, hi, mid, hi, lo, q, zero8], 0).astype(BF16)
        moved = lax.dot_general(eye16, stack, nt, preferred_element_type=F32).astype(BF16)
        geo_ref[t] = moved
        acc_ref[t] = jnp.zeros((32, TILE), F32)
        return 0

    lax.fori_loop(0, TILES, prepare, 0, unroll=4)
    for g in range(9):
        if g != 4:
            copies[g].wait()
    geo_ref[DUMMY] = geo_ref[0]
    dip_ref[DUMMY] = dip_ref[0]

    def blank(at):
        near_ref[at] = DUMMY + 4 * GRID
        base_ref[at] = own_base
        target_ref[at] = UNUSED

    for k in range(2 * UNROLL):
        blank(k)
    total = jnp.int32(2 * UNROLL)
    def put(at, home, remote, g):
        target = remote + g * OUT_ROWS
        if g == 4:
            target = jnp.where(remote == home, UNUSED, target)
        near_ref[at] = home + g * GRID
        base_ref[at] = remote + g * ROWS
        target_ref[at] = target
        return at + 1

    for g in range(9):
        first = lists_ref[3 * g + 2, 8 - g]
        last = lists_ref[3 * g + 2, 9 - g]

        def incoming(p, at, g=g):
            return put(at, lists_ref[3 * g, p] & (TILES - 1), lists_ref[3 * g + 1, p], g)

        total = lax.fori_loop(first, last, incoming, total)
    for k in range((HALVES + 2) * UNROLL):
        blank(total + k)
    groups = (total - 2 * UNROLL + UNROLL - 1) // UNROLL

    def home_of(at):
        return near_ref[at] & (GRID - 1)

    def origin(at):
        grid = near_ref[at] // GRID
        row = (grid * 11) // 32
        column = grid - 3 * row
        return (
            24.0 - domain_edge * row.astype(F32),
            24.0 - domain_edge * column.astype(F32),
            (4 * home_of(at) + 2).astype(F32),
        )

    def distances(dist_ref, u, at):
        base = base_ref[at]
        pos = [load_row(x_ref, base + (6 + k) * TILES) - c for k, c in enumerate(origin(at))]
        pol = load_row(x_ref, base + 9 * TILES)
        hi, mid, lo = geometry_rows(pos, squared(pos), 1.0)
        q = scale_rows(lax.rsqrt(pol), (0, 0, 1, 1, 2, 0))
        left = jnp.concatenate([hi, hi, mid, mid, lo, hi, zero8, zero8], 0).astype(BF16)
        right = jnp.concatenate([jnp.zeros((48, TILE), F32), q, zero8], 0).astype(BF16)
        same = (target_ref[at] == UNUSED).astype(jnp.int32)
        operand = jnp.concatenate([eye_ref[same], jnp.concatenate([left, right], 1)], 0)
        rows = jnp.concatenate([eye_ref[2, :, :TILE], geo_ref[home_of(at)]], 1)
        dist_ref[u] = jnp.dot(rows, operand, preferred_element_type=F32)

    def coefficients(dist_ref, coef_ref, u):
        dist_sq = dist_ref[u, :, :TILE]
        inv = lax.rsqrt(dist_sq)
        inv_sq = inv * inv
        inv_cube = inv_sq * inv
        cube = dist_sq * inv * dist_sq
        damp = cube * dist_ref[u, :, TILE:]
        decay = jnp.exp(damp)
        lam_three = 1.0 - decay
        lam_five = lam_three + damp * decay
        three = lam_three * inv_cube
        five = lam_five * inv_cube * inv_sq
        three_hi = three.astype(BF16)
        five_hi = five.astype(BF16)
        coef_ref[u, 0] = five_hi
        coef_ref[u, 1] = (five - five_hi.astype(F32)).astype(BF16)
        coef_ref[u, 2] = three_hi
        coef_ref[u, 3] = (three - three_hi.astype(F32)).astype(BF16)

    def folded(sums):
        total = sums[0:32, :TILE]
        for k in range(1, PARTS):
            total = total + (sums[32 * k:32 * k + 32, :TILE] + sums[32 * k - 32:32 * k, TILE:])
        return total

    def sums(coef_ref, u, at):
        mu, pos, pol, mixed, own = site_vectors(x_ref, base_ref[at], origin(at))
        rem = dipole_rows(mu, pos, mixed, own)
        five_hi, five_lo, three_hi, three_lo = [coef_ref[u, k] for k in range(4)]
        square = jnp.concatenate(
            [jnp.concatenate([five_hi, three_hi], 1), jnp.concatenate([five_lo, three_lo], 1)], 0
        )
        h = folded(lax.dot_general(rem, square, nt, preferred_element_type=F32))
        square = jnp.concatenate(
            [jnp.concatenate([five_hi, five_lo], 1), jnp.concatenate([three_hi, three_lo], 1)], 0
        )
        r = folded(jnp.dot(dip_ref[home_of(at)], square, preferred_element_type=F32))
        field = assemble([r[8 * j:8 * j + 8] for j in range(4)], pos, mixed)
        return home_of(at), target_ref[at], h, field

    def half(first, dist_now, dist_next, coef_now, coef_next):
        done = [sums(coef_now, u, first + u) for u in range(UNROLL)]
        for u in range(UNROLL):
            coefficients(dist_now, coef_next, u)
        for u in range(UNROLL):
            distances(dist_next, u, first + 2 * UNROLL + u)
        for home, target, h, field in done:
            acc_ref[home] += h
            out_ref[pl.ds(target, 8, stride=OUT_STRIDE), :] += field

    even = (dist_even, dist_odd, coef_even, coef_odd)
    odd = (dist_odd, dist_even, coef_odd, coef_even)

    def step(i, _):
        for k in range(HALVES):
            half((HALVES * i + k) * UNROLL, *(odd if k % 2 else even))
        return 0

    lax.fori_loop(0, (groups + 1 + HALVES) // HALVES, step, 0)

    sends = []
    for g in range(9):
        for k in range(6):
            source = out_ref.at[pl.ds(g * OUT_ROWS + k * OUT_STRIDE, TILES), :]
            place = outs[g % 3].at[g // 3, k]
            sends.append(pltpu.make_async_copy(source, place, out_sem.at[6 * g + k]))
    for k, send in enumerate(sends):
        if k // 6 != 4:
            send.start()

    def finish(t, _):
        centre = (8.0, 8.0, (4 * t + 2).astype(F32))
        mu, pos, pol, mixed, own = site_vectors(x_ref, own_base + t, centre)
        field = assemble([acc_ref[t, 8 * j:8 * j + 8] for j in range(4)], pos, mixed)
        out_ref[pl.ds(4 * OUT_ROWS + t, 8, stride=OUT_STRIDE), :] += field
        return 0

    lax.fori_loop(0, TILES, finish, 0, unroll=4)
    for send in sends[24:30]:
        send.start()
    for send in sends:
        send.wait()


FAR_AWAY = 2.0 ** 60
LIST = 9 * 2048 + (HALVES + 4) * UNROLL
OUT_STRIDE = TILES + 8
OUT_ROWS = 8 * OUT_STRIDE
UNUSED = 4 * OUT_ROWS + DUMMY


def field_kernel(lists, *sites):
    smem = pl.BlockSpec(memory_space=pltpu.SMEM)
    away = pl.BlockSpec(memory_space=pl.ANY)
    return pl.pallas_call(
        kernel,
        out_shape=[jax.ShapeDtypeStruct((3, 6, TILES, TILE), F32)] * 3,
        in_specs=[smem] + [away] * 9,
        out_specs=[away] * 3,
        scratch_shapes=[
            pltpu.VMEM((9 * OUT_ROWS, TILE), F32),
            pltpu.SemaphoreType.DMA((9,)),
            pltpu.SemaphoreType.DMA((54,)),
            pltpu.VMEM((9 * ROWS, TILE), F32),
            pltpu.VMEM((TILES + 1, TILE, 64), BF16),
            pltpu.VMEM((TILES + 1, 32 * PARTS, 2 * TILE), BF16),
            pltpu.VMEM((TILES + 1, 32, TILE), F32),
            pltpu.VMEM((3, TILE, 2 * TILE), BF16),
            pltpu.SMEM((LIST,), jnp.int32),
            pltpu.SMEM((LIST,), jnp.int32),
            pltpu.SMEM((LIST,), jnp.int32),
            pltpu.VMEM((UNROLL, TILE, 2 * TILE), F32),
            pltpu.VMEM((UNROLL, TILE, 2 * TILE), F32),
            pltpu.VMEM((UNROLL, 4, TILE, TILE), BF16),
            pltpu.VMEM((UNROLL, 4, TILE, TILE), BF16),
        ],
        compiler_params=pltpu.CompilerParams(vmem_limit_bytes=63 * 1024 * 1024),
        name="pair_fields",
    )(lists, *sites)


def around(value, axis):
    count = lax.axis_size(axis)
    forward = [(i, (i + 1) % count) for i in range(count)]
    backward = [((i + 1) % count, i) for i in range(count)]
    return [lax.ppermute(value, axis, forward), value, lax.ppermute(value, axis, backward)]


def shifted(value, axis, steps):
    count = lax.axis_size(axis)
    pairs = [(source, (source + steps) % count) for source in range(count)]
    return lax.ppermute(value, axis, pairs)


def local(positions, polarity, dipoles, perm_fields, pair_list, tile_counts):
    slot_total = pair_list.shape[3]
    sites = jnp.concatenate([dipoles, positions, polarity[None]], 0).reshape(10 * TILES, TILE)

    table = pair_list.reshape(2, slot_total)
    live = jnp.arange(slot_total, dtype=jnp.int32) < tile_counts.reshape(())
    far = jnp.where(live, table[1], 16 * TILES)
    far, near = lax.sort((far, table[0]), num_keys=1)
    bounds = jnp.arange(slot_total, dtype=jnp.int32)[:16] * TILES
    bounds = jnp.sum((far[None, :] < bounds[:, None]).astype(jnp.int32), 1)
    bounds = jnp.concatenate([bounds, jnp.zeros((slot_total - 16,), jnp.int32)])
    lists = jnp.stack([far, near, bounds])[None]
    lists = jnp.concatenate(around(lists, "gx"), 0)[:, None]

    middle = around(sites, "gx")
    sides = around(sites, "gy")
    middle[0], middle[2], lists, sides[0], sides[2] = lax.optimization_barrier(
        (middle[0], middle[2], lists, sides[0], sides[2])
    )
    lists = jnp.concatenate(around(lists, "gy"), 1).reshape(27, slot_total)
    upper = around(middle[0], "gy")
    lower = around(middle[2], "gy")
    low, mid, high = field_kernel(lists, *upper, *sides, *lower)
    column = mid + shifted(low, "gy", -1) + shifted(high, "gy", 1)
    field = column[1] + shifted(column[0], "gx", -1) + shifted(column[2], "gx", 1)
    field = field.reshape(6, 1, 1, TILES * TILE)
    induced = polarity[None] * (perm_fields + field)
    return (field, induced)


def solution(mesh):
    placed = (
        P(None, "gx", "gy", None),
        P("gx", "gy", None),
        P(None, "gx", "gy", None),
        P(None, "gx", "gy", None),
        P("gx", "gy", None, None),
        P("gx", "gy"),
    )
    return jax.shard_map(
        local,
        mesh=mesh,
        in_specs=placed,
        out_specs=(P(None, "gx", "gy", None), P(None, "gx", "gy", None)),
        check_vma=False,
    )
```

```python
import jax
import jax.numpy as jnp
from jax import lax
from jax.experimental import pallas as pl
from jax.experimental.pallas import tpu as pltpu
from jax.sharding import PartitionSpec as P

TILE = 128
TILES = 256
ROWS = 10 * TILES
UNROLL = 2
HALVES = 6
PARTS = 3
DUMMY = TILES
GRID = 2 * TILES

thole = 0.39
domain_edge = 16.0

F32 = jnp.float32
BF16 = jnp.bfloat16


def three_parts(value):
    high = value.astype(BF16)
    rest = value - high.astype(F32)
    middle = rest.astype(BF16)
    low = (rest - middle.astype(F32)).astype(BF16)
    return high, middle, low


def rows_of():
    sub = lax.broadcasted_iota(jnp.int32, (8, TILE), 0)
    second = (sub == 3) | (sub == 4) | (sub == 5) | (sub == 7)
    is_x = (sub == 0) | (sub == 3)
    is_y = (sub == 1) | (sub == 4)
    is_z = (sub == 2) | (sub == 5)
    return sub, second, is_x, is_y, is_z


def load_row(ref, row):
    return jnp.broadcast_to(ref[pl.ds(row, 1), :], (8, TILE))


def site_vectors(ref, base, centre):
    sub, second, is_x, is_y, is_z = rows_of()
    dips = [load_row(ref, base + k * TILES) for k in range(6)]
    pos = [load_row(ref, base + (6 + k) * TILES) - centre[k] for k in range(3)]
    pol = load_row(ref, base + 9 * TILES)
    mu = [jnp.where(second, dips[3 + j], dips[j]) for j in range(3)]
    mixed = jnp.where(is_x, pos[0], jnp.where(is_y, pos[1], jnp.where(is_z, pos[2], 1.0)))
    own = jnp.where(is_x, mu[0], jnp.where(is_y, mu[1], jnp.where(is_z, mu[2], 0.0)))
    return mu, pos, pol, mixed, own


def dipole_rows(mu, pos, mixed, own):
    dots = pos[0] * mu[0] + pos[1] * mu[1] + pos[2] * mu[2]
    tripled = 3.0 * mixed
    left = jnp.concatenate([tripled * mu[0], tripled * mu[1], tripled * mu[2], tripled * dots], 0)
    blank = jnp.zeros((16, TILE), BF16)
    right = jnp.concatenate([jnp.zeros((8, TILE), F32), -own], 0)
    out = []
    for l, r in zip(three_parts(left), three_parts(right)):
        out.append(jnp.concatenate([l, jnp.concatenate([blank, r], 0)], 1))
    return jnp.concatenate(out[:PARTS], 0)


def geometry_rows(first_three, fourth, fifth):
    sub = lax.broadcasted_iota(jnp.int32, (8, TILE), 0)
    rows = jnp.where(sub == 0, first_three[0], jnp.where(sub == 1, first_three[1], jnp.where(sub == 2, first_three[2], jnp.where(sub == 3, fourth, jnp.where(sub == 4, fifth, 0.0)))))
    return tuple(p.astype(F32) for p in three_parts(rows))


def scale_rows(scale, pattern):
    sub = lax.broadcasted_iota(jnp.int32, (8, TILE), 0)
    parts = [p.astype(F32) for p in three_parts(scale)]
    out = jnp.zeros((8, TILE), F32)
    for row, part in enumerate(pattern):
        out = jnp.where(sub == row, parts[part], out)
    return out


def squared(pos):
    return pos[0] * pos[0] + pos[1] * pos[1] + pos[2] * pos[2]


def assemble(parts, pos, mixed):
    sub, second, _, _, _ = rows_of()
    g = pos[0] * parts[0] + pos[1] * parts[1] + pos[2] * parts[2] - parts[3]
    s0 = jnp.broadcast_to(g[6:7], (8, TILE))
    s1 = jnp.broadcast_to(g[7:8], (8, TILE))
    s = jnp.where(second, s1, s0)
    return mixed * s - g


def kernel(
    lists_ref, *refs
):
    sources, refs = refs[:9], refs[9:]
    outs, refs = refs[:3], refs[3:]
    (
    out_ref, copy_sem, out_sem, x_ref, geo_ref, dip_ref, acc_ref, eye_ref, near_ref, base_ref, target_ref, dist_even, dist_odd, coef_even, coef_odd,
    ) = refs
    eye = (
        lax.broadcasted_iota(jnp.int32, (TILE, TILE), 0) == lax.broadcasted_iota(jnp.int32, (TILE, TILE), 1)
    )
    eye16 = jnp.where(eye, 1.0, 0.0).astype(BF16)
    zero8 = jnp.zeros((8, TILE), F32)
    own_base = 4 * ROWS
    copies = []
    for g, source in enumerate(sources):
        place = x_ref.at[pl.ds(g * ROWS, ROWS), :]
        copies.append(pltpu.make_async_copy(source, place, copy_sem.at[g]))
        copies[-1].start()
    nt = (((1,), (1,)), ((), ()))
    eye_ref[0] = jnp.zeros((TILE, 2 * TILE), BF16)
    eye_ref[1] = jnp.concatenate(
        [jnp.where(eye, FAR_AWAY, 0.0).astype(BF16), jnp.zeros((TILE, TILE), BF16)], 1
    )

    eye_ref[2] = jnp.concatenate([eye16, eye16], 1)

    def clear(i, _):
        out_ref[pl.ds(pl.multiple_of(i * 64, 64), 64), :] = jnp.zeros((64, TILE), F32)
        return 0

    lax.fori_loop(0, out_ref.shape[0] // 64, clear, 0)
    copies[4].wait()

    def prepare(t, _):
        centre = (8.0, 8.0, (4 * t + 2).astype(F32))
        mu, pos, pol, mixed, own = site_vectors(x_ref, own_base + t, centre)
        dip_ref[t] = dipole_rows(mu, pos, mixed, own)
        hi, mid, lo = geometry_rows([-2.0 * p for p in pos], 1.0, squared(pos))
        scale = (-thole) * lax.rsqrt(pol)
        q = scale_rows(scale, (0, 1, 0, 1, 0, 2))
        stack = jnp.concatenate([hi, mid, hi, mid, hi, lo, q, zero8], 0).astype(BF16)
        moved = lax.dot_general(eye16, stack, nt, preferred_element_type=F32).astype(BF16)
        geo_ref[t] = moved
        acc_ref[t] = jnp.zeros((32, TILE), F32)
        return 0

    lax.fori_loop(0, TILES, prepare, 0, unroll=4)
    for g in range(9):
        if g != 4:
            copies[g].wait()
    geo_ref[DUMMY] = geo_ref[0]
    dip_ref[DUMMY] = dip_ref[0]

    def blank(at):
        near_ref[at] = DUMMY + 4 * GRID
        base_ref[at] = own_base
        target_ref[at] = UNUSED

    for k in range(2 * UNROLL):
        blank(k)
    total = jnp.int32(2 * UNROLL)
    def put(at, home, remote, g):
        target = remote + g * OUT_ROWS
        if g == 4:
            target = jnp.where(remote == home, UNUSED, target)
        near_ref[at] = home + g * GRID
        base_ref[at] = remote + g * ROWS
        target_ref[at] = target
        return at + 1

    for g in range(9):
        first = lists_ref[3 * g + 2, 8 - g]
        last = lists_ref[3 * g + 2, 9 - g]

        def incoming(p, at, g=g):
            return put(at, lists_ref[3 * g, p] & (TILES - 1), lists_ref[3 * g + 1, p], g)

        total = lax.fori_loop(first, last, incoming, total)
    for k in range((HALVES + 2) * UNROLL):
        blank(total + k)
    groups = (total - 2 * UNROLL + UNROLL - 1) // UNROLL

    def home_of(at):
        return near_ref[at] & (GRID - 1)

    def origin(at):
        grid = near_ref[at] // GRID
        row = (grid * 11) // 32
        column = grid - 3 * row
        return (
            24.0 - domain_edge * row.astype(F32),
            24.0 - domain_edge * column.astype(F32),
            (4 * home_of(at) + 2).astype(F32),
        )

    def distances(dist_ref, u, at):
        base = base_ref[at]
        pos = [load_row(x_ref, base + (6 + k) * TILES) - c for k, c in enumerate(origin(at))]
        pol = load_row(x_ref, base + 9 * TILES)
        hi, mid, lo = geometry_rows(pos, squared(pos), 1.0)
        q = scale_rows(lax.rsqrt(pol), (0, 0, 1, 1, 2, 0))
        left = jnp.concatenate([hi, hi, mid, mid, lo, hi, zero8, zero8], 0).astype(BF16)
        right = jnp.concatenate([jnp.zeros((48, TILE), F32), q, zero8], 0).astype(BF16)
        same = (target_ref[at] == UNUSED).astype(jnp.int32)
        operand = jnp.concatenate([eye_ref[same], jnp.concatenate([left, right], 1)], 0)
        rows = jnp.concatenate([eye_ref[2, :, :TILE], geo_ref[home_of(at)]], 1)
        dist_ref[u] = jnp.dot(rows, operand, preferred_element_type=F32)

    def coefficients(dist_ref, coef_ref, u):
        dist_sq = dist_ref[u, :, :TILE]
        inv = lax.rsqrt(dist_sq)
        inv_sq = inv * inv
        inv_cube = inv_sq * inv
        cube = dist_sq * inv * dist_sq
        damp = cube * dist_ref[u, :, TILE:]
        decay = jnp.exp(damp)
        lam_three = 1.0 - decay
        lam_five = lam_three + damp * decay
        three = lam_three * inv_cube
        five = lam_five * inv_cube * inv_sq
        three_hi = three.astype(BF16)
        five_hi = five.astype(BF16)
        coef_ref[u, 0] = five_hi
        coef_ref[u, 1] = (five - five_hi.astype(F32)).astype(BF16)
        coef_ref[u, 2] = three_hi
        coef_ref[u, 3] = (three - three_hi.astype(F32)).astype(BF16)

    def folded(sums):
        total = sums[0:32, :TILE]
        for k in range(1, PARTS):
            total = total + (sums[32 * k:32 * k + 32, :TILE] + sums[32 * k - 32:32 * k, TILE:])
        return total

    def sums(coef_ref, u, at):
        mu, pos, pol, mixed, own = site_vectors(x_ref, base_ref[at], origin(at))
        rem = dipole_rows(mu, pos, mixed, own)
        five_hi, five_lo, three_hi, three_lo = [coef_ref[u, k] for k in range(4)]
        square = jnp.concatenate(
            [jnp.concatenate([five_hi, three_hi], 1), jnp.concatenate([five_lo, three_lo], 1)], 0
        )
        h = folded(lax.dot_general(rem, square, nt, preferred_element_type=F32))
        square = jnp.concatenate(
            [jnp.concatenate([five_hi, five_lo], 1), jnp.concatenate([three_hi, three_lo], 1)], 0
        )
        r = folded(jnp.dot(dip_ref[home_of(at)], square, preferred_element_type=F32))
        field = assemble([r[8 * j:8 * j + 8] for j in range(4)], pos, mixed)
        return home_of(at), target_ref[at], h, field

    def half(first, dist_now, dist_next, coef_now, coef_next):
        done = [sums(coef_now, u, first + u) for u in range(UNROLL)]
        for u in range(UNROLL):
            coefficients(dist_now, coef_next, u)
        for u in range(UNROLL):
            distances(dist_next, u, first + 2 * UNROLL + u)
        for home, target, h, field in done:
            acc_ref[home] += h
            out_ref[pl.ds(target, 8, stride=OUT_STRIDE), :] += field

    even = (dist_even, dist_odd, coef_even, coef_odd)
    odd = (dist_odd, dist_even, coef_odd, coef_even)

    def step(i, _):
        for k in range(HALVES):
            half((HALVES * i + k) * UNROLL, *(odd if k % 2 else even))
        return 0

    lax.fori_loop(0, (groups + 1 + HALVES) // HALVES, step, 0)

    sends = []
    for g in range(9):
        for k in range(6):
            source = out_ref.at[pl.ds(g * OUT_ROWS + k * OUT_STRIDE, TILES), :]
            place = outs[g % 3].at[g // 3, k]
            sends.append(pltpu.make_async_copy(source, place, out_sem.at[6 * g + k]))
    for k, send in enumerate(sends):
        if k // 6 != 4:
            send.start()

    def finish(t, _):
        centre = (8.0, 8.0, (4 * t + 2).astype(F32))
        mu, pos, pol, mixed, own = site_vectors(x_ref, own_base + t, centre)
        field = assemble([acc_ref[t, 8 * j:8 * j + 8] for j in range(4)], pos, mixed)
        out_ref[pl.ds(4 * OUT_ROWS + t, 8, stride=OUT_STRIDE), :] += field
        return 0

    lax.fori_loop(0, TILES, finish, 0, unroll=4)
    for send in sends[24:30]:
        send.start()
    for send in sends:
        send.wait()


FAR_AWAY = 2.0 ** 60
LIST = 9 * 2048 + (HALVES + 4) * UNROLL
OUT_STRIDE = TILES + 8
OUT_ROWS = 8 * OUT_STRIDE
UNUSED = 4 * OUT_ROWS + DUMMY


def field_kernel(lists, *sites):
    smem = pl.BlockSpec(memory_space=pltpu.SMEM)
    away = pl.BlockSpec(memory_space=pl.ANY)
    return pl.pallas_call(
        kernel,
        out_shape=[jax.ShapeDtypeStruct((3, 6, TILES, TILE), F32)] * 3,
        in_specs=[smem] + [away] * 9,
        out_specs=[away] * 3,
        scratch_shapes=[
            pltpu.VMEM((9 * OUT_ROWS, TILE), F32),
            pltpu.SemaphoreType.DMA((9,)),
            pltpu.SemaphoreType.DMA((54,)),
            pltpu.VMEM((9 * ROWS, TILE), F32),
            pltpu.VMEM((TILES + 1, TILE, 64), BF16),
            pltpu.VMEM((TILES + 1, 32 * PARTS, 2 * TILE), BF16),
            pltpu.VMEM((TILES + 1, 32, TILE), F32),
            pltpu.VMEM((3, TILE, 2 * TILE), BF16),
            pltpu.SMEM((LIST,), jnp.int32),
            pltpu.SMEM((LIST,), jnp.int32),
            pltpu.SMEM((LIST,), jnp.int32),
            pltpu.VMEM((UNROLL, TILE, 2 * TILE), F32),
            pltpu.VMEM((UNROLL, TILE, 2 * TILE), F32),
            pltpu.VMEM((UNROLL, 4, TILE, TILE), BF16),
            pltpu.VMEM((UNROLL, 4, TILE, TILE), BF16),
        ],
        compiler_params=pltpu.CompilerParams(vmem_limit_bytes=63 * 1024 * 1024),
        name="pair_fields",
    )(lists, *sites)


CHUNKS = 4


def halo_kernel(sites_ref, lists_ref, *refs):
    outs, lists_out = refs[:8], refs[8]
    send_sem, recv_sem, list_send, list_recv, own_sem = refs[9:]
    outs = outs[:4] + (None,) + outs[4:]
    gx, gy = lax.axis_index("gx"), lax.axis_index("gy")
    n_gx, n_gy = lax.axis_size("gx"), lax.axis_size("gy")
    mesh_id = pl.DeviceIdType.MESH
    size = ROWS // CHUNKS

    def device(g):
        return (lax.rem(gx + g // 3 - 1 + n_gx, n_gx), lax.rem(gy + g % 3 - 1 + n_gy, n_gy))

    barrier = pltpu.get_barrier_semaphore()
    others = [g for g in range(9) if g != 4]
    for g in others:
        pl.semaphore_signal(barrier, inc=1, device_id=device(g), device_id_type=mesh_id)
    pl.semaphore_wait(barrier, 8)

    def piece(g, source, target, chunk):
        rows = pl.ds(chunk * size, size)
        return pltpu.make_async_remote_copy(
            src_ref=source.at[rows, :],
            dst_ref=outs[g].at[rows, :],
            send_sem=send_sem.at[g, chunk],
            recv_sem=recv_sem.at[g, chunk],
            device_id=device(target),
            device_id_type=mesh_id,
        )

    straight = {}
    for chunk in range(CHUNKS):
        for g in (1, 7, 3, 5):
            straight[g, chunk] = piece(g, sites_ref, 8 - g, chunk)
    for chunk in range(CHUNKS):
        for g in (1, 7):
            straight[g, chunk].start()
    for chunk in range(CHUNKS):
        for g in (3, 5):
            straight[g, chunk].start()
    listed = []
    for g in others:
        listed.append(
            pltpu.make_async_remote_copy(
                src_ref=lists_ref,
                dst_ref=lists_out.at[g],
                send_sem=list_send.at[g],
                recv_sem=list_recv.at[g],
                device_id=device(8 - g),
                device_id_type=mesh_id,
            )
        )
        listed[-1].start()
    own = pltpu.make_async_copy(lists_ref, lists_out.at[4], own_sem)
    own.start()
    passed = []
    for chunk in range(CHUNKS):
        for g in (1, 7):
            straight[g, chunk].wait_recv()
            for side in (-1, 1):
                passed.append(piece(g + side, outs[g], 4 - side, chunk))
                passed[-1].start()
    for chunk in range(CHUNKS):
        for g in (3, 5):
            straight[g, chunk].wait()
        for g in (1, 7):
            straight[g, chunk].wait_send()
    for copy in passed + listed:
        copy.wait()
    own.wait()


def halo_exchange(sites, lists):
    away = pl.BlockSpec(memory_space=pl.ANY)
    shapes = [jax.ShapeDtypeStruct(sites.shape, sites.dtype)] * 8
    shapes.append(jax.ShapeDtypeStruct((9,) + lists.shape, lists.dtype))
    return pl.pallas_call(
        halo_kernel,
        out_shape=shapes,
        in_specs=[away] * 2,
        out_specs=[away] * 9,
        scratch_shapes=[
            pltpu.SemaphoreType.DMA((9, CHUNKS)),
            pltpu.SemaphoreType.DMA((9, CHUNKS)),
            pltpu.SemaphoreType.DMA((9,)),
            pltpu.SemaphoreType.DMA((9,)),
            pltpu.SemaphoreType.DMA,
        ],
        compiler_params=pltpu.CompilerParams(collective_id=0, has_side_effects=True),
        name="halo",
    )(sites, lists)


def shifted(value, axis, steps):
    count = lax.axis_size(axis)
    pairs = [(source, (source + steps) % count) for source in range(count)]
    return lax.ppermute(value, axis, pairs)


def local(positions, polarity, dipoles, perm_fields, pair_list, tile_counts):
    slot_total = pair_list.shape[3]
    sites = jnp.concatenate([dipoles, positions, polarity[None]], 0).reshape(10 * TILES, TILE)

    table = pair_list.reshape(2, slot_total)
    live = jnp.arange(slot_total, dtype=jnp.int32) < tile_counts.reshape(())
    far = jnp.where(live, table[1], 16 * TILES)
    far, near = lax.sort((far, table[0]), num_keys=1)
    bounds = jnp.arange(slot_total, dtype=jnp.int32)[:16] * TILES
    bounds = jnp.sum((far[None, :] < bounds[:, None]).astype(jnp.int32), 1)
    bounds = jnp.concatenate([bounds, jnp.zeros((slot_total - 16,), jnp.int32)])
    lists = jnp.stack([far, near, bounds])
    *around_sites, lists = halo_exchange(sites, lists)
    low, mid, high = field_kernel(
        lists.reshape(27, slot_total), *around_sites[:4], sites, *around_sites[4:]
    )
    column = mid + shifted(low, "gy", -1) + shifted(high, "gy", 1)
    field = column[1] + shifted(column[0], "gx", -1) + shifted(column[2], "gx", 1)
    field = field.reshape(6, 1, 1, TILES * TILE)
    induced = polarity[None] * (perm_fields + field)
    return (field, induced)


def solution(mesh):
    placed = (
        P(None, "gx", "gy", None),
        P("gx", "gy", None),
        P(None, "gx", "gy", None),
        P(None, "gx", "gy", None),
        P("gx", "gy", None, None),
        P("gx", "gy"),
    )
    return jax.shard_map(
        local,
        mesh=mesh,
        in_specs=placed,
        out_specs=(P(None, "gx", "gy", None), P(None, "gx", "gy", None)),
        check_vma=False,
    )
```

```python
import jax
import jax.numpy as jnp
from jax import lax
from jax.experimental import pallas as pl
from jax.experimental.pallas import tpu as pltpu
from jax.sharding import PartitionSpec as P

TILE = 128
TILES = 256
ROWS = 10 * TILES
UNROLL = 2
HALVES = 6
PARTS = 3
DUMMY = TILES
GRID = 2 * TILES

thole = 0.39
domain_edge = 16.0

F32 = jnp.float32
BF16 = jnp.bfloat16


def three_parts(value):
    high = value.astype(BF16)
    rest = value - high.astype(F32)
    middle = rest.astype(BF16)
    low = (rest - middle.astype(F32)).astype(BF16)
    return high, middle, low


def rows_of():
    sub = lax.broadcasted_iota(jnp.int32, (8, TILE), 0)
    second = (sub == 3) | (sub == 4) | (sub == 5) | (sub == 7)
    is_x = (sub == 0) | (sub == 3)
    is_y = (sub == 1) | (sub == 4)
    is_z = (sub == 2) | (sub == 5)
    return sub, second, is_x, is_y, is_z


def load_row(ref, row):
    return jnp.broadcast_to(ref[pl.ds(row, 1), :], (8, TILE))


def site_vectors(ref, base, centre):
    sub, second, is_x, is_y, is_z = rows_of()
    dips = [load_row(ref, base + k * TILES) for k in range(6)]
    pos = [load_row(ref, base + (6 + k) * TILES) - centre[k] for k in range(3)]
    pol = load_row(ref, base + 9 * TILES)
    mu = [jnp.where(second, dips[3 + j], dips[j]) for j in range(3)]
    mixed = jnp.where(is_x, pos[0], jnp.where(is_y, pos[1], jnp.where(is_z, pos[2], 1.0)))
    own = jnp.where(is_x, mu[0], jnp.where(is_y, mu[1], jnp.where(is_z, mu[2], 0.0)))
    return mu, pos, pol, mixed, own


def dipole_rows(mu, pos, mixed, own):
    dots = pos[0] * mu[0] + pos[1] * mu[1] + pos[2] * mu[2]
    tripled = 3.0 * mixed
    left = jnp.concatenate([tripled * mu[0], tripled * mu[1], tripled * mu[2], tripled * dots], 0)
    blank = jnp.zeros((16, TILE), BF16)
    right = jnp.concatenate([jnp.zeros((8, TILE), F32), -own], 0)
    out = []
    for l, r in zip(three_parts(left), three_parts(right)):
        out.append(jnp.concatenate([l, jnp.concatenate([blank, r], 0)], 1))
    return jnp.concatenate(out[:PARTS], 0)


def geometry_rows(first_three, fourth, fifth):
    sub = lax.broadcasted_iota(jnp.int32, (8, TILE), 0)
    rows = jnp.where(sub == 0, first_three[0], jnp.where(sub == 1, first_three[1], jnp.where(sub == 2, first_three[2], jnp.where(sub == 3, fourth, jnp.where(sub == 4, fifth, 0.0)))))
    return tuple(p.astype(F32) for p in three_parts(rows))


def scale_rows(scale, pattern):
    sub = lax.broadcasted_iota(jnp.int32, (8, TILE), 0)
    parts = [p.astype(F32) for p in three_parts(scale)]
    out = jnp.zeros((8, TILE), F32)
    for row, part in enumerate(pattern):
        out = jnp.where(sub == row, parts[part], out)
    return out


def squared(pos):
    return pos[0] * pos[0] + pos[1] * pos[1] + pos[2] * pos[2]


def assemble(parts, pos, mixed):
    sub, second, _, _, _ = rows_of()
    g = pos[0] * parts[0] + pos[1] * parts[1] + pos[2] * parts[2] - parts[3]
    s0 = jnp.broadcast_to(g[6:7], (8, TILE))
    s1 = jnp.broadcast_to(g[7:8], (8, TILE))
    s = jnp.where(second, s1, s0)
    return mixed * s - g


def kernel(
    lists_ref, *refs
):
    sources, refs = refs[:9], refs[9:]
    outs, refs = refs[:3], refs[3:]
    (
    out_ref, copy_sem, out_sem, x_ref, geo_ref, dip_ref, acc_ref, eye_ref, near_ref, base_ref, target_ref, dist_even, dist_odd, coef_even, coef_odd,
    ) = refs
    eye = (
        lax.broadcasted_iota(jnp.int32, (TILE, TILE), 0) == lax.broadcasted_iota(jnp.int32, (TILE, TILE), 1)
    )
    eye16 = jnp.where(eye, 1.0, 0.0).astype(BF16)
    zero8 = jnp.zeros((8, TILE), F32)
    own_base = 4 * ROWS
    copies = []
    for g, source in enumerate(sources):
        place = x_ref.at[pl.ds(g * ROWS, ROWS), :]
        copies.append(pltpu.make_async_copy(source, place, copy_sem.at[g]))
        copies[-1].start()
    nt = (((1,), (1,)), ((), ()))
    eye_ref[0] = jnp.zeros((TILE, 2 * TILE), BF16)
    eye_ref[1] = jnp.concatenate(
        [jnp.where(eye, FAR_AWAY, 0.0).astype(BF16), jnp.zeros((TILE, TILE), BF16)], 1
    )

    eye_ref[2] = jnp.concatenate([eye16, eye16], 1)

    def clear(i, _):
        out_ref[pl.ds(pl.multiple_of(i * 64, 64), 64), :] = jnp.zeros((64, TILE), F32)
        return 0

    lax.fori_loop(0, out_ref.shape[0] // 64, clear, 0)
    copies[4].wait()

    def prepare(t, _):
        centre = (8.0, 8.0, (4 * t + 2).astype(F32))
        mu, pos, pol, mixed, own = site_vectors(x_ref, own_base + t, centre)
        dip_ref[t] = dipole_rows(mu, pos, mixed, own)
        hi, mid, lo = geometry_rows([-2.0 * p for p in pos], 1.0, squared(pos))
        scale = (-thole) * lax.rsqrt(pol)
        q = scale_rows(scale, (0, 1, 0, 1, 0, 2))
        stack = jnp.concatenate([hi, mid, hi, mid, hi, lo, q, zero8], 0).astype(BF16)
        moved = lax.dot_general(eye16, stack, nt, preferred_element_type=F32).astype(BF16)
        geo_ref[t] = moved
        acc_ref[t] = jnp.zeros((32, TILE), F32)
        return 0

    lax.fori_loop(0, TILES, prepare, 0, unroll=4)
    for g in range(9):
        if g != 4:
            copies[g].wait()
    geo_ref[DUMMY] = geo_ref[0]
    dip_ref[DUMMY] = dip_ref[0]

    def blank(at):
        near_ref[at] = DUMMY + 4 * GRID
        base_ref[at] = own_base
        target_ref[at] = UNUSED

    for k in range(2 * UNROLL):
        blank(k)
    total = jnp.int32(2 * UNROLL)
    def put(at, home, remote, g):
        target = remote + g * OUT_ROWS
        if g == 4:
            target = jnp.where(remote == home, UNUSED, target)
        near_ref[at] = home + g * GRID
        base_ref[at] = remote + g * ROWS
        target_ref[at] = target
        return at + 1

    for g in range(9):
        first = lists_ref[3 * g + 2, 8 - g]
        last = lists_ref[3 * g + 2, 9 - g]

        def incoming(p, at, g=g):
            return put(at, lists_ref[3 * g, p] & (TILES - 1), lists_ref[3 * g + 1, p], g)

        total = lax.fori_loop(first, last, incoming, total)
    for k in range((HALVES + 2) * UNROLL):
        blank(total + k)
    groups = (total - 2 * UNROLL + UNROLL - 1) // UNROLL

    def home_of(at):
        return near_ref[at] & (GRID - 1)

    def origin(at):
        grid = near_ref[at] // GRID
        row = (grid * 11) // 32
        column = grid - 3 * row
        return (
            24.0 - domain_edge * row.astype(F32),
            24.0 - domain_edge * column.astype(F32),
            (4 * home_of(at) + 2).astype(F32),
        )

    def distances(dist_ref, u, at):
        base = base_ref[at]
        pos = [load_row(x_ref, base + (6 + k) * TILES) - c for k, c in enumerate(origin(at))]
        pol = load_row(x_ref, base + 9 * TILES)
        hi, mid, lo = geometry_rows(pos, squared(pos), 1.0)
        q = scale_rows(lax.rsqrt(pol), (0, 0, 1, 1, 2, 0))
        left = jnp.concatenate([hi, hi, mid, mid, lo, hi, zero8, zero8], 0).astype(BF16)
        right = jnp.concatenate([jnp.zeros((48, TILE), F32), q, zero8], 0).astype(BF16)
        same = (target_ref[at] == UNUSED).astype(jnp.int32)
        operand = jnp.concatenate([eye_ref[same], jnp.concatenate([left, right], 1)], 0)
        rows = jnp.concatenate([eye_ref[2, :, :TILE], geo_ref[home_of(at)]], 1)
        dist_ref[u] = jnp.dot(rows, operand, preferred_element_type=F32)

    def coefficients(dist_ref, coef_ref, u):
        dist_sq = dist_ref[u, :, :TILE]
        inv = lax.rsqrt(dist_sq)
        inv_sq = inv * inv
        inv_cube = inv_sq * inv
        cube = dist_sq * inv * dist_sq
        damp = cube * dist_ref[u, :, TILE:]
        decay = jnp.exp(damp)
        lam_three = 1.0 - decay
        lam_five = lam_three + damp * decay
        three = lam_three * inv_cube
        five = lam_five * inv_cube * inv_sq
        three_hi = three.astype(BF16)
        five_hi = five.astype(BF16)
        coef_ref[u, 0] = five_hi
        coef_ref[u, 1] = (five - five_hi.astype(F32)).astype(BF16)
        coef_ref[u, 2] = three_hi
        coef_ref[u, 3] = (three - three_hi.astype(F32)).astype(BF16)

    def folded(sums):
        total = sums[0:32, :TILE]
        for k in range(1, PARTS):
            total = total + (sums[32 * k:32 * k + 32, :TILE] + sums[32 * k - 32:32 * k, TILE:])
        return total

    def sums(coef_ref, u, at):
        mu, pos, pol, mixed, own = site_vectors(x_ref, base_ref[at], origin(at))
        rem = dipole_rows(mu, pos, mixed, own)
        five_hi, five_lo, three_hi, three_lo = [coef_ref[u, k] for k in range(4)]
        square = jnp.concatenate(
            [jnp.concatenate([five_hi, three_hi], 1), jnp.concatenate([five_lo, three_lo], 1)], 0
        )
        h = folded(lax.dot_general(rem, square, nt, preferred_element_type=F32))
        square = jnp.concatenate(
            [jnp.concatenate([five_hi, five_lo], 1), jnp.concatenate([three_hi, three_lo], 1)], 0
        )
        r = folded(jnp.dot(dip_ref[home_of(at)], square, preferred_element_type=F32))
        field = assemble([r[8 * j:8 * j + 8] for j in range(4)], pos, mixed)
        return home_of(at), target_ref[at], h, field

    def half(first, dist_now, dist_next, coef_now, coef_next):
        done = [sums(coef_now, u, first + u) for u in range(UNROLL)]
        for u in range(UNROLL):
            coefficients(dist_now, coef_next, u)
        for u in range(UNROLL):
            distances(dist_next, u, first + 2 * UNROLL + u)
        for home, target, h, field in done:
            acc_ref[home] += h
            out_ref[pl.ds(target, 8, stride=OUT_STRIDE), :] += field

    even = (dist_even, dist_odd, coef_even, coef_odd)
    odd = (dist_odd, dist_even, coef_odd, coef_even)

    def step(i, _):
        for k in range(HALVES):
            half((HALVES * i + k) * UNROLL, *(odd if k % 2 else even))
        return 0

    lax.fori_loop(0, (groups + 1 + HALVES) // HALVES, step, 0)

    sends = []
    for g in range(9):
        for k in range(6):
            source = out_ref.at[pl.ds(g * OUT_ROWS + k * OUT_STRIDE, TILES), :]
            place = outs[g % 3].at[g // 3, k]
            sends.append(pltpu.make_async_copy(source, place, out_sem.at[6 * g + k]))
    for k, send in enumerate(sends):
        if k // 6 != 4:
            send.start()

    def finish(t, _):
        centre = (8.0, 8.0, (4 * t + 2).astype(F32))
        mu, pos, pol, mixed, own = site_vectors(x_ref, own_base + t, centre)
        field = assemble([acc_ref[t, 8 * j:8 * j + 8] for j in range(4)], pos, mixed)
        out_ref[pl.ds(4 * OUT_ROWS + t, 8, stride=OUT_STRIDE), :] += field
        return 0

    lax.fori_loop(0, TILES, finish, 0, unroll=4)
    for send in sends[24:30]:
        send.start()
    for send in sends:
        send.wait()


FAR_AWAY = 2.0 ** 60
LIST = 9 * 2048 + (HALVES + 4) * UNROLL
OUT_STRIDE = TILES + 8
OUT_ROWS = 8 * OUT_STRIDE
UNUSED = 4 * OUT_ROWS + DUMMY


def field_kernel(lists, *sites):
    smem = pl.BlockSpec(memory_space=pltpu.SMEM)
    away = pl.BlockSpec(memory_space=pl.ANY)
    return pl.pallas_call(
        kernel,
        out_shape=[jax.ShapeDtypeStruct((3, 6, TILES, TILE), F32)] * 3,
        in_specs=[smem] + [away] * 9,
        out_specs=[away] * 3,
        scratch_shapes=[
            pltpu.VMEM((9 * OUT_ROWS, TILE), F32),
            pltpu.SemaphoreType.DMA((9,)),
            pltpu.SemaphoreType.DMA((54,)),
            pltpu.VMEM((9 * ROWS, TILE), F32),
            pltpu.VMEM((TILES + 1, TILE, 64), BF16),
            pltpu.VMEM((TILES + 1, 32 * PARTS, 2 * TILE), BF16),
            pltpu.VMEM((TILES + 1, 32, TILE), F32),
            pltpu.VMEM((3, TILE, 2 * TILE), BF16),
            pltpu.SMEM((LIST,), jnp.int32),
            pltpu.SMEM((LIST,), jnp.int32),
            pltpu.SMEM((LIST,), jnp.int32),
            pltpu.VMEM((UNROLL, TILE, 2 * TILE), F32),
            pltpu.VMEM((UNROLL, TILE, 2 * TILE), F32),
            pltpu.VMEM((UNROLL, 4, TILE, TILE), BF16),
            pltpu.VMEM((UNROLL, 4, TILE, TILE), BF16),
        ],
        compiler_params=pltpu.CompilerParams(vmem_limit_bytes=63 * 1024 * 1024),
        name="pair_fields",
    )(lists, *sites)


CHUNKS = 4
EDGE = 8


def halo_kernel(sites_ref, lists_ref, *refs):
    outs, lists_out = refs[:8], refs[8]
    send_sem, recv_sem, list_send, list_recv, own_sem = refs[9:]
    outs = outs[:4] + (None,) + outs[4:]
    gx, gy = lax.axis_index("gx"), lax.axis_index("gy")
    n_gx, n_gy = lax.axis_size("gx"), lax.axis_size("gy")
    mesh_id = pl.DeviceIdType.MESH
    size = ROWS // CHUNKS

    def device(g):
        return (lax.rem(gx + g // 3 - 1 + n_gx, n_gx), lax.rem(gy + g % 3 - 1 + n_gy, n_gy))

    barrier = pltpu.get_barrier_semaphore()
    others = [g for g in range(9) if g != 4]
    for g in others:
        pl.semaphore_signal(barrier, inc=1, device_id=device(g), device_id_type=mesh_id)
    pl.semaphore_wait(barrier, 8)

    def piece(g, source, target, chunk):
        rows = pl.ds(chunk * size, size)
        return pltpu.make_async_remote_copy(
            src_ref=source.at[rows, :],
            dst_ref=outs[g].at[rows, :],
            send_sem=send_sem.at[g, chunk],
            recv_sem=recv_sem.at[g, chunk],
            device_id=device(target),
            device_id_type=mesh_id,
        )

    straight = {}
    for chunk in range(CHUNKS):
        for g in (1, 7, 3, 5):
            straight[g, chunk] = piece(g, sites_ref, 8 - g, chunk)
    for chunk in range(CHUNKS):
        for g in (1, 7, 3, 5):
            straight[g, chunk].start()
    listed = []
    for g in others:
        listed.append(
            pltpu.make_async_remote_copy(
                src_ref=lists_ref,
                dst_ref=lists_out.at[g],
                send_sem=list_send.at[g],
                recv_sem=list_recv.at[g],
                device_id=device(8 - g),
                device_id_type=mesh_id,
            )
        )
        listed[-1].start()
    own = pltpu.make_async_copy(lists_ref, lists_out.at[4], own_sem)
    own.start()
    first_edge = lax.rem(gy, EDGE) == 0
    last_edge = lax.rem(gy, EDGE) == EDGE - 1
    onward = {
        1: ((~last_edge, 0, 1, 5), (~first_edge, 2, 1, 3)),
        7: ((~last_edge, 6, 7, 5), (~first_edge, 8, 7, 3)),
        3: ((first_edge, 0, 3, 7), (first_edge, 6, 3, 1)),
        5: ((last_edge, 2, 5, 7), (last_edge, 8, 5, 1)),
    }

    def pass_on(g, chunk, action):
        for condition, slot, here, target in onward[g]:

            @pl.when(condition)
            def _(slot=slot, here=here, target=target):
                action(piece(slot, outs[here], target, chunk))

    for chunk in range(CHUNKS):
        for g in (1, 7, 3, 5):
            straight[g, chunk].wait_recv()
            pass_on(g, chunk, lambda copy: copy.start())
    for chunk in range(CHUNKS):
        for g in (1, 7, 3, 5):
            straight[g, chunk].wait_send()
            pass_on(g, chunk, lambda copy: copy.wait_send())
        for g in (0, 2, 6, 8):
            piece(g, sites_ref, 8 - g, chunk).wait_recv()
    for copy in listed:
        copy.wait()
    own.wait()


def halo_exchange(sites, lists):
    away = pl.BlockSpec(memory_space=pl.ANY)
    shapes = [jax.ShapeDtypeStruct(sites.shape, sites.dtype)] * 8
    shapes.append(jax.ShapeDtypeStruct((9,) + lists.shape, lists.dtype))
    return pl.pallas_call(
        halo_kernel,
        out_shape=shapes,
        in_specs=[away] * 2,
        out_specs=[away] * 9,
        scratch_shapes=[
            pltpu.SemaphoreType.DMA((9, CHUNKS)),
            pltpu.SemaphoreType.DMA((9, CHUNKS)),
            pltpu.SemaphoreType.DMA((9,)),
            pltpu.SemaphoreType.DMA((9,)),
            pltpu.SemaphoreType.DMA,
        ],
        compiler_params=pltpu.CompilerParams(collective_id=0, has_side_effects=True),
        name="halo",
    )(sites, lists)


def shifted(value, axis, steps):
    count = lax.axis_size(axis)
    pairs = [(source, (source + steps) % count) for source in range(count)]
    return lax.ppermute(value, axis, pairs)


def local(positions, polarity, dipoles, perm_fields, pair_list, tile_counts):
    slot_total = pair_list.shape[3]
    sites = jnp.concatenate([dipoles, positions, polarity[None]], 0).reshape(10 * TILES, TILE)

    table = pair_list.reshape(2, slot_total)
    live = jnp.arange(slot_total, dtype=jnp.int32) < tile_counts.reshape(())
    far = jnp.where(live, table[1], 16 * TILES)
    far, near = lax.sort((far, table[0]), num_keys=1)
    bounds = jnp.arange(slot_total, dtype=jnp.int32)[:16] * TILES
    bounds = jnp.sum((far[None, :] < bounds[:, None]).astype(jnp.int32), 1)
    bounds = jnp.concatenate([bounds, jnp.zeros((slot_total - 16,), jnp.int32)])
    lists = jnp.stack([far, near, bounds])
    *around_sites, lists = halo_exchange(sites, lists)
    low, mid, high = field_kernel(
        lists.reshape(27, slot_total), *around_sites[:4], sites, *around_sites[4:]
    )
    column = mid + shifted(low, "gy", -1) + shifted(high, "gy", 1)
    field = column[1] + shifted(column[0], "gx", -1) + shifted(column[2], "gx", 1)
    field = field.reshape(6, 1, 1, TILES * TILE)
    induced = polarity[None] * (perm_fields + field)
    return (field, induced)


def solution(mesh):
    placed = (
        P(None, "gx", "gy", None),
        P("gx", "gy", None),
        P(None, "gx", "gy", None),
        P(None, "gx", "gy", None),
        P("gx", "gy", None, None),
        P("gx", "gy"),
    )
    return jax.shard_map(
        local,
        mesh=mesh,
        in_specs=placed,
        out_specs=(P(None, "gx", "gy", None), P(None, "gx", "gy", None)),
        check_vma=False,
    )
```

```python
import jax
import jax.numpy as jnp
from jax import lax
from jax.experimental import pallas as pl
from jax.experimental.pallas import tpu as pltpu
from jax.sharding import PartitionSpec as P

TILE = 128
TILES = 256
ROWS = 10 * TILES
UNROLL = 2
HALVES = 6
PARTS = 3
DUMMY = TILES
GRID = 2 * TILES

thole = 0.39
domain_edge = 16.0

F32 = jnp.float32
BF16 = jnp.bfloat16


def three_parts(value):
    high = value.astype(BF16)
    rest = value - high.astype(F32)
    middle = rest.astype(BF16)
    low = (rest - middle.astype(F32)).astype(BF16)
    return high, middle, low


def rows_of():
    sub = lax.broadcasted_iota(jnp.int32, (8, TILE), 0)
    second = (sub == 3) | (sub == 4) | (sub == 5) | (sub == 7)
    is_x = (sub == 0) | (sub == 3)
    is_y = (sub == 1) | (sub == 4)
    is_z = (sub == 2) | (sub == 5)
    return sub, second, is_x, is_y, is_z


def load_row(ref, row):
    return jnp.broadcast_to(ref[pl.ds(row, 1), :], (8, TILE))


def site_vectors(ref, base, centre):
    sub, second, is_x, is_y, is_z = rows_of()
    dips = [load_row(ref, base + k * TILES) for k in range(6)]
    pos = [load_row(ref, base + (6 + k) * TILES) - centre[k] for k in range(3)]
    pol = load_row(ref, base + 9 * TILES)
    mu = [jnp.where(second, dips[3 + j], dips[j]) for j in range(3)]
    mixed = jnp.where(is_x, pos[0], jnp.where(is_y, pos[1], jnp.where(is_z, pos[2], 1.0)))
    own = jnp.where(is_x, mu[0], jnp.where(is_y, mu[1], jnp.where(is_z, mu[2], 0.0)))
    return mu, pos, pol, mixed, own


def dipole_rows(mu, pos, mixed, own):
    dots = pos[0] * mu[0] + pos[1] * mu[1] + pos[2] * mu[2]
    tripled = 3.0 * mixed
    left = jnp.concatenate([tripled * mu[0], tripled * mu[1], tripled * mu[2], tripled * dots], 0)
    blank = jnp.zeros((16, TILE), BF16)
    right = jnp.concatenate([jnp.zeros((8, TILE), F32), -own], 0)
    out = []
    for l, r in zip(three_parts(left), three_parts(right)):
        out.append(jnp.concatenate([l, jnp.concatenate([blank, r], 0)], 1))
    return jnp.concatenate(out[:PARTS], 0)


def geometry_rows(first_three, fourth, fifth):
    sub = lax.broadcasted_iota(jnp.int32, (8, TILE), 0)
    rows = jnp.where(sub == 0, first_three[0], jnp.where(sub == 1, first_three[1], jnp.where(sub == 2, first_three[2], jnp.where(sub == 3, fourth, jnp.where(sub == 4, fifth, 0.0)))))
    return tuple(p.astype(F32) for p in three_parts(rows))


def scale_rows(scale, pattern):
    sub = lax.broadcasted_iota(jnp.int32, (8, TILE), 0)
    parts = [p.astype(F32) for p in three_parts(scale)]
    out = jnp.zeros((8, TILE), F32)
    for row, part in enumerate(pattern):
        out = jnp.where(sub == row, parts[part], out)
    return out


def squared(pos):
    return pos[0] * pos[0] + pos[1] * pos[1] + pos[2] * pos[2]


def assemble(parts, pos, mixed):
    sub, second, _, _, _ = rows_of()
    g = pos[0] * parts[0] + pos[1] * parts[1] + pos[2] * parts[2] - parts[3]
    s0 = jnp.broadcast_to(g[6:7], (8, TILE))
    s1 = jnp.broadcast_to(g[7:8], (8, TILE))
    s = jnp.where(second, s1, s0)
    return mixed * s - g


def kernel(
    lists_ref, split_ref, *refs
):
    sources, refs = refs[:9], refs[9:]
    outs, refs = refs[:3], refs[3:]
    (
    out_ref, copy_sem, out_sem, x_ref, geo_ref, dip_ref, acc_ref, eye_ref, near_ref, base_ref, target_ref, dist_even, dist_odd, coef_even, coef_odd,
    ) = refs
    eye = (
        lax.broadcasted_iota(jnp.int32, (TILE, TILE), 0) == lax.broadcasted_iota(jnp.int32, (TILE, TILE), 1)
    )
    eye16 = jnp.where(eye, 1.0, 0.0).astype(BF16)
    zero8 = jnp.zeros((8, TILE), F32)
    own_base = 4 * ROWS
    copies = []
    for g, source in enumerate(sources):
        place = x_ref.at[pl.ds(g * ROWS, ROWS), :]
        copies.append(pltpu.make_async_copy(source, place, copy_sem.at[g]))
        copies[-1].start()
    nt = (((1,), (1,)), ((), ()))
    eye_ref[0] = jnp.zeros((TILE, 2 * TILE), BF16)
    eye_ref[1] = jnp.concatenate(
        [jnp.where(eye, FAR_AWAY, 0.0).astype(BF16), jnp.zeros((TILE, TILE), BF16)], 1
    )

    eye_ref[2] = jnp.concatenate([eye16, eye16], 1)

    def clear(i, _):
        out_ref[pl.ds(pl.multiple_of(i * 64, 64), 64), :] = jnp.zeros((64, TILE), F32)
        return 0

    lax.fori_loop(0, out_ref.shape[0] // 64, clear, 0)
    copies[4].wait()

    def prepare(t, _):
        centre = (8.0, 8.0, (4 * t + 2).astype(F32))
        mu, pos, pol, mixed, own = site_vectors(x_ref, own_base + t, centre)
        dip_ref[t] = dipole_rows(mu, pos, mixed, own)
        hi, mid, lo = geometry_rows([-2.0 * p for p in pos], 1.0, squared(pos))
        scale = (-thole) * lax.rsqrt(pol)
        q = scale_rows(scale, (0, 1, 0, 1, 0, 2))
        stack = jnp.concatenate([hi, mid, hi, mid, hi, lo, q, zero8], 0).astype(BF16)
        moved = lax.dot_general(eye16, stack, nt, preferred_element_type=F32).astype(BF16)
        geo_ref[t] = moved
        acc_ref[t] = jnp.zeros((32, TILE), F32)
        return 0

    lax.fori_loop(0, TILES, prepare, 0, unroll=4)
    for g in range(9):
        if g != 4:
            copies[g].wait()
    geo_ref[DUMMY] = geo_ref[0]
    dip_ref[DUMMY] = dip_ref[0]

    def blank(at):
        near_ref[at] = DUMMY + 4 * GRID
        base_ref[at] = own_base
        target_ref[at] = UNUSED

    for k in range(2 * UNROLL):
        blank(k)
    total = jnp.int32(2 * UNROLL)
    def put(at, home, remote, g):
        target = remote + g * OUT_ROWS
        if g == 4:
            target = jnp.where(remote == home, UNUSED, target)
        near_ref[at] = home + g * GRID
        base_ref[at] = remote + g * ROWS
        target_ref[at] = target
        return at + 1

    for g in range(9):
        first = lists_ref[3 * g + 2, 8 - g]
        last = lists_ref[3 * g + 2, 9 - g]
        if g != 4:
            last = first + split_ref[g, 0]

        def incoming(p, at, g=g):
            return put(at, lists_ref[3 * g, p] & (TILES - 1), lists_ref[3 * g + 1, p], g)

        total = lax.fori_loop(first, last, incoming, total)
        if g != 4:
            first = lists_ref[14, g] + split_ref[9 + g, 0]
            last = lists_ref[14, g + 1]

            def kept(p, at, g=g):
                return put(at, lists_ref[13, p], lists_ref[12, p] & (TILES - 1), g)

            total = lax.fori_loop(first, last, kept, total)
    for k in range((HALVES + 2) * UNROLL):
        blank(total + k)
    groups = (total - 2 * UNROLL + UNROLL - 1) // UNROLL

    def home_of(at):
        return near_ref[at] & (GRID - 1)

    def origin(at):
        grid = near_ref[at] // GRID
        row = (grid * 11) // 32
        column = grid - 3 * row
        return (
            24.0 - domain_edge * row.astype(F32),
            24.0 - domain_edge * column.astype(F32),
            (4 * home_of(at) + 2).astype(F32),
        )

    def distances(dist_ref, u, at):
        base = base_ref[at]
        pos = [load_row(x_ref, base + (6 + k) * TILES) - c for k, c in enumerate(origin(at))]
        pol = load_row(x_ref, base + 9 * TILES)
        hi, mid, lo = geometry_rows(pos, squared(pos), 1.0)
        q = scale_rows(lax.rsqrt(pol), (0, 0, 1, 1, 2, 0))
        left = jnp.concatenate([hi, hi, mid, mid, lo, hi, zero8, zero8], 0).astype(BF16)
        right = jnp.concatenate([jnp.zeros((48, TILE), F32), q, zero8], 0).astype(BF16)
        same = (target_ref[at] == UNUSED).astype(jnp.int32)
        operand = jnp.concatenate([eye_ref[same], jnp.concatenate([left, right], 1)], 0)
        rows = jnp.concatenate([eye_ref[2, :, :TILE], geo_ref[home_of(at)]], 1)
        dist_ref[u] = jnp.dot(rows, operand, preferred_element_type=F32)

    def coefficients(dist_ref, coef_ref, u):
        dist_sq = dist_ref[u, :, :TILE]
        inv = lax.rsqrt(dist_sq)
        inv_sq = inv * inv
        inv_cube = inv_sq * inv
        cube = dist_sq * inv * dist_sq
        damp = cube * dist_ref[u, :, TILE:]
        decay = jnp.exp(damp)
        lam_three = 1.0 - decay
        lam_five = lam_three + damp * decay
        three = lam_three * inv_cube
        five = lam_five * inv_cube * inv_sq
        three_hi = three.astype(BF16)
        five_hi = five.astype(BF16)
        coef_ref[u, 0] = five_hi
        coef_ref[u, 1] = (five - five_hi.astype(F32)).astype(BF16)
        coef_ref[u, 2] = three_hi
        coef_ref[u, 3] = (three - three_hi.astype(F32)).astype(BF16)

    def folded(sums):
        total = sums[0:32, :TILE]
        for k in range(1, PARTS):
            total = total + (sums[32 * k:32 * k + 32, :TILE] + sums[32 * k - 32:32 * k, TILE:])
        return total

    def sums(coef_ref, u, at):
        mu, pos, pol, mixed, own = site_vectors(x_ref, base_ref[at], origin(at))
        rem = dipole_rows(mu, pos, mixed, own)
        five_hi, five_lo, three_hi, three_lo = [coef_ref[u, k] for k in range(4)]
        square = jnp.concatenate(
            [jnp.concatenate([five_hi, three_hi], 1), jnp.concatenate([five_lo, three_lo], 1)], 0
        )
        h = folded(lax.dot_general(rem, square, nt, preferred_element_type=F32))
        square = jnp.concatenate(
            [jnp.concatenate([five_hi, five_lo], 1), jnp.concatenate([three_hi, three_lo], 1)], 0
        )
        r = folded(jnp.dot(dip_ref[home_of(at)], square, preferred_element_type=F32))
        field = assemble([r[8 * j:8 * j + 8] for j in range(4)], pos, mixed)
        return home_of(at), target_ref[at], h, field

    def half(first, dist_now, dist_next, coef_now, coef_next):
        done = [sums(coef_now, u, first + u) for u in range(UNROLL)]
        for u in range(UNROLL):
            coefficients(dist_now, coef_next, u)
        for u in range(UNROLL):
            distances(dist_next, u, first + 2 * UNROLL + u)
        for home, target, h, field in done:
            acc_ref[home] += h
            out_ref[pl.ds(target, 8, stride=OUT_STRIDE), :] += field

    even = (dist_even, dist_odd, coef_even, coef_odd)
    odd = (dist_odd, dist_even, coef_odd, coef_even)

    def step(i, _):
        for k in range(HALVES):
            half((HALVES * i + k) * UNROLL, *(odd if k % 2 else even))
        return 0

    lax.fori_loop(0, (groups + 1 + HALVES) // HALVES, step, 0)

    sends = []
    for g in range(9):
        for k in range(6):
            source = out_ref.at[pl.ds(g * OUT_ROWS + k * OUT_STRIDE, TILES), :]
            place = outs[g % 3].at[g // 3, k]
            sends.append(pltpu.make_async_copy(source, place, out_sem.at[6 * g + k]))
    for k, send in enumerate(sends):
        if k // 6 != 4:
            send.start()

    def finish(t, _):
        centre = (8.0, 8.0, (4 * t + 2).astype(F32))
        mu, pos, pol, mixed, own = site_vectors(x_ref, own_base + t, centre)
        field = assemble([acc_ref[t, 8 * j:8 * j + 8] for j in range(4)], pos, mixed)
        out_ref[pl.ds(4 * OUT_ROWS + t, 8, stride=OUT_STRIDE), :] += field
        return 0

    lax.fori_loop(0, TILES, finish, 0, unroll=4)
    for send in sends[24:30]:
        send.start()
    for send in sends:
        send.wait()


FAR_AWAY = 2.0 ** 60
LIST = 9 * 2048 + (HALVES + 4) * UNROLL
OUT_STRIDE = TILES + 8
OUT_ROWS = 8 * OUT_STRIDE
UNUSED = 4 * OUT_ROWS + DUMMY


def field_kernel(lists, split, *sites):
    smem = pl.BlockSpec(memory_space=pltpu.SMEM)
    away = pl.BlockSpec(memory_space=pl.ANY)
    return pl.pallas_call(
        kernel,
        out_shape=[jax.ShapeDtypeStruct((3, 6, TILES, TILE), F32)] * 3,
        in_specs=[smem, smem] + [away] * 9,
        out_specs=[away] * 3,
        scratch_shapes=[
            pltpu.VMEM((9 * OUT_ROWS, TILE), F32),
            pltpu.SemaphoreType.DMA((9,)),
            pltpu.SemaphoreType.DMA((54,)),
            pltpu.VMEM((9 * ROWS, TILE), F32),
            pltpu.VMEM((TILES + 1, TILE, 64), BF16),
            pltpu.VMEM((TILES + 1, 32 * PARTS, 2 * TILE), BF16),
            pltpu.VMEM((TILES + 1, 32, TILE), F32),
            pltpu.VMEM((3, TILE, 2 * TILE), BF16),
            pltpu.SMEM((LIST,), jnp.int32),
            pltpu.SMEM((LIST,), jnp.int32),
            pltpu.SMEM((LIST,), jnp.int32),
            pltpu.VMEM((UNROLL, TILE, 2 * TILE), F32),
            pltpu.VMEM((UNROLL, TILE, 2 * TILE), F32),
            pltpu.VMEM((UNROLL, 4, TILE, TILE), BF16),
            pltpu.VMEM((UNROLL, 4, TILE, TILE), BF16),
        ],
        compiler_params=pltpu.CompilerParams(vmem_limit_bytes=63 * 1024 * 1024),
        name="pair_fields",
    )(lists, split, *sites)


CHUNKS = 4
TURNS = 5
EDGE = 8


def halo_kernel(sites_ref, lists_ref, counts_ref, *refs):
    outs, lists_out, split_ref = refs[:8], refs[8], refs[9]
    send_sem, recv_sem, list_send, list_recv, own_sem, *refs = refs[10:]
    nbr_counts, loads, mine, share_send, share_recv = refs
    outs = outs[:4] + (None,) + outs[4:]
    gx, gy = lax.axis_index("gx"), lax.axis_index("gy")
    n_gx, n_gy = lax.axis_size("gx"), lax.axis_size("gy")
    mesh_id = pl.DeviceIdType.MESH
    size = ROWS // CHUNKS

    def device(g):
        return (lax.rem(gx + g // 3 - 1 + n_gx, n_gx), lax.rem(gy + g % 3 - 1 + n_gy, n_gy))

    barrier = pltpu.get_barrier_semaphore()
    others = [g for g in range(9) if g != 4]
    for g in others:
        pl.semaphore_signal(barrier, inc=1, device_id=device(g), device_id_type=mesh_id)
    pl.semaphore_wait(barrier, 8)

    def piece(g, source, target, chunk):
        rows = pl.ds(chunk * size, size)
        return pltpu.make_async_remote_copy(
            src_ref=source.at[rows, :],
            dst_ref=outs[g].at[rows, :],
            send_sem=send_sem.at[g, chunk],
            recv_sem=recv_sem.at[g, chunk],
            device_id=device(target),
            device_id_type=mesh_id,
        )

    shared = []

    def share(turn, source, dest):
        for g in others:
            copy = pltpu.make_async_remote_copy(
                src_ref=source,
                dst_ref=dest.at[g],
                send_sem=share_send.at[turn, g],
                recv_sem=share_recv.at[turn, g],
                device_id=device(8 - g),
                device_id_type=mesh_id,
            )
            copy.start()
            shared.append(copy)

    share(0, counts_ref, nbr_counts)
    straight = {}
    for chunk in range(CHUNKS):
        for g in (1, 7, 3, 5):
            straight[g, chunk] = piece(g, sites_ref, 8 - g, chunk)
    for chunk in range(CHUNKS):
        for g in (1, 7, 3, 5):
            straight[g, chunk].start()
    listed = []
    for g in others:
        listed.append(
            pltpu.make_async_remote_copy(
                src_ref=lists_ref,
                dst_ref=lists_out.at[g],
                send_sem=list_send.at[g],
                recv_sem=list_recv.at[g],
                device_id=device(8 - g),
                device_id_type=mesh_id,
            )
        )
        listed[-1].start()
    own = pltpu.make_async_copy(lists_ref, lists_out.at[4], own_sem)
    own.start()
    first_edge = lax.rem(gy, EDGE) == 0
    last_edge = lax.rem(gy, EDGE) == EDGE - 1
    onward = {
        1: ((~last_edge, 0, 1, 5), (~first_edge, 2, 1, 3)),
        7: ((~last_edge, 6, 7, 5), (~first_edge, 8, 7, 3)),
        3: ((first_edge, 0, 3, 7), (first_edge, 6, 3, 1)),
        5: ((last_edge, 2, 5, 7), (last_edge, 8, 5, 1)),
    }

    def pass_on(g, chunk, action):
        for condition, slot, here, target in onward[g]:

            @pl.when(condition)
            def _(slot=slot, here=here, target=target):
                action(piece(slot, outs[here], target, chunk))

    incoming, outgoing, given, kept = {}, {}, {}, {}

    def balance(turn):
        for copy in shared[8 * turn:8 * turn + 8]:
            copy.wait_recv()
        if turn == 0:
            for g in others:
                given[g] = incoming[g] = nbr_counts[g, 8 - g:9 - g, :]
                kept[g] = outgoing[g] = counts_ref[g:g + 1, :]
        else:
            before = mine[turn - 1, 0:1, :]
            for g in others:
                theirs = loads[turn - 1, g, 0:1, :]
                come = jnp.floor((theirs - before) * (1.0 / 16.0))
                given[g] = jnp.clip(given[g] + come, 0.0, incoming[g])
                leave = jnp.floor((before - theirs) * (1.0 / 16.0))
                kept[g] = jnp.clip(kept[g] + leave, 0.0, outgoing[g])
        if turn < TURNS:
            load = counts_ref[4:5, :]
            for g in others:
                load = load + (outgoing[g] - kept[g]) + given[g]
            mine[turn] = jnp.broadcast_to(load, (8, TILE))
            share(turn + 1, mine.at[turn], loads.at[turn])

    for chunk in range(CHUNKS):
        balance(chunk)
        for g in (1, 7, 3, 5):
            straight[g, chunk].wait_recv()
            pass_on(g, chunk, lambda copy: copy.start())
    for turn in range(CHUNKS, TURNS + 1):
        balance(turn)
    blank = jnp.zeros((1, TILE), F32)
    rows = [given.get(g, blank) for g in range(9)] + [kept.get(g, blank) for g in range(9)]
    split_ref[...] = jnp.concatenate(rows + [blank] * 6, 0).astype(jnp.int32)
    for copy in shared:
        copy.wait_send()
    for chunk in range(CHUNKS):
        for g in (1, 7, 3, 5):
            straight[g, chunk].wait_send()
            pass_on(g, chunk, lambda copy: copy.wait_send())
        for g in (0, 2, 6, 8):
            piece(g, sites_ref, 8 - g, chunk).wait_recv()
    for copy in listed:
        copy.wait()
    own.wait()


def halo_exchange(sites, lists, counts):
    away = pl.BlockSpec(memory_space=pl.ANY)
    shapes = [jax.ShapeDtypeStruct(sites.shape, sites.dtype)] * 8
    shapes.append(jax.ShapeDtypeStruct((9,) + lists.shape, lists.dtype))
    shapes.append(jax.ShapeDtypeStruct((24, TILE), jnp.int32))
    vmem = pl.BlockSpec(memory_space=pltpu.VMEM)
    return pl.pallas_call(
        halo_kernel,
        out_shape=shapes,
        in_specs=[away, away, vmem],
        out_specs=[away] * 9 + [vmem],
        scratch_shapes=[
            pltpu.SemaphoreType.DMA((9, CHUNKS)),
            pltpu.SemaphoreType.DMA((9, CHUNKS)),
            pltpu.SemaphoreType.DMA((9,)),
            pltpu.SemaphoreType.DMA((9,)),
            pltpu.SemaphoreType.DMA,
            pltpu.VMEM((9, 16, TILE), F32),
            pltpu.VMEM((TURNS, 9, 8, TILE), F32),
            pltpu.VMEM((TURNS, 8, TILE), F32),
            pltpu.SemaphoreType.DMA((TURNS + 1, 9)),
            pltpu.SemaphoreType.DMA((TURNS + 1, 9)),
        ],
        compiler_params=pltpu.CompilerParams(collective_id=0, has_side_effects=True),
        name="halo",
    )(sites, lists, counts)


def shifted(value, axis, steps):
    count = lax.axis_size(axis)
    pairs = [(source, (source + steps) % count) for source in range(count)]
    return lax.ppermute(value, axis, pairs)


def local(positions, polarity, dipoles, perm_fields, pair_list, tile_counts):
    slot_total = pair_list.shape[3]
    sites = jnp.concatenate([dipoles, positions, polarity[None]], 0).reshape(10 * TILES, TILE)

    table = pair_list.reshape(2, slot_total)
    live = jnp.arange(slot_total, dtype=jnp.int32) < tile_counts.reshape(())
    far = jnp.where(live, table[1], 16 * TILES)
    far, near = lax.sort((far, table[0]), num_keys=1)
    bounds = jnp.arange(slot_total, dtype=jnp.int32)[:16] * TILES
    bounds = jnp.sum((far[None, :] < bounds[:, None]).astype(jnp.int32), 1)
    counts = (bounds[1:10] - bounds[:9]).astype(F32)
    counts = jnp.broadcast_to(jnp.pad(counts, (0, 7))[:, None], (16, TILE))
    bounds = jnp.concatenate([bounds, jnp.zeros((slot_total - 16,), jnp.int32)])
    lists = jnp.stack([far, near, bounds])
    *around_sites, lists, split = halo_exchange(sites, lists, counts)
    low, mid, high = field_kernel(
        lists.reshape(27, slot_total), split, *around_sites[:4], sites, *around_sites[4:]
    )
    column = mid + shifted(low, "gy", -1) + shifted(high, "gy", 1)
    field = column[1] + shifted(column[0], "gx", -1) + shifted(column[2], "gx", 1)
    field = field.reshape(6, 1, 1, TILES * TILE)
    induced = polarity[None] * (perm_fields + field)
    return (field, induced)


def solution(mesh):
    placed = (
        P(None, "gx", "gy", None),
        P("gx", "gy", None),
        P(None, "gx", "gy", None),
        P(None, "gx", "gy", None),
        P("gx", "gy", None, None),
        P("gx", "gy"),
    )
    return jax.shard_map(
        local,
        mesh=mesh,
        in_specs=placed,
        out_specs=(P(None, "gx", "gy", None), P(None, "gx", "gy", None)),
        check_vma=False,
    )
```

```python
import jax
import jax.numpy as jnp
from jax import lax
from jax.experimental import pallas as pl
from jax.experimental.pallas import tpu as pltpu
from jax.sharding import PartitionSpec as P

TILE = 128
TILES = 256
ROWS = 10 * TILES
UNROLL = 2
HALVES = 6
PARTS = 3
DUMMY = TILES
GRID = 2 * TILES

thole = 0.39
domain_edge = 16.0

F32 = jnp.float32
BF16 = jnp.bfloat16


def three_parts(value):
    high = value.astype(BF16)
    rest = value - high.astype(F32)
    middle = rest.astype(BF16)
    low = (rest - middle.astype(F32)).astype(BF16)
    return high, middle, low


def rows_of():
    sub = lax.broadcasted_iota(jnp.int32, (8, TILE), 0)
    second = (sub == 3) | (sub == 4) | (sub == 5) | (sub == 7)
    is_x = (sub == 0) | (sub == 3)
    is_y = (sub == 1) | (sub == 4)
    is_z = (sub == 2) | (sub == 5)
    return sub, second, is_x, is_y, is_z


def load_row(ref, row):
    return jnp.broadcast_to(ref[pl.ds(row, 1), :], (8, TILE))


def site_vectors(ref, base, centre):
    sub, second, is_x, is_y, is_z = rows_of()
    dips = [load_row(ref, base + k * TILES) for k in range(6)]
    pos = [load_row(ref, base + (6 + k) * TILES) - centre[k] for k in range(3)]
    pol = load_row(ref, base + 9 * TILES)
    mu = [jnp.where(second, dips[3 + j], dips[j]) for j in range(3)]
    mixed = jnp.where(is_x, pos[0], jnp.where(is_y, pos[1], jnp.where(is_z, pos[2], 1.0)))
    own = jnp.where(is_x, mu[0], jnp.where(is_y, mu[1], jnp.where(is_z, mu[2], 0.0)))
    return mu, pos, pol, mixed, own


def dipole_rows(mu, pos, mixed, own):
    dots = pos[0] * mu[0] + pos[1] * mu[1] + pos[2] * mu[2]
    tripled = 3.0 * mixed
    left = jnp.concatenate([tripled * mu[0], tripled * mu[1], tripled * mu[2], tripled * dots], 0)
    blank = jnp.zeros((16, TILE), BF16)
    right = jnp.concatenate([jnp.zeros((8, TILE), F32), -own], 0)
    out = []
    for l, r in zip(three_parts(left), three_parts(right)):
        out.append(jnp.concatenate([l, jnp.concatenate([blank, r], 0)], 1))
    return jnp.concatenate(out[:PARTS], 0)


def geometry_rows(first_three, fourth, fifth):
    sub = lax.broadcasted_iota(jnp.int32, (8, TILE), 0)
    rows = jnp.where(sub == 0, first_three[0], jnp.where(sub == 1, first_three[1], jnp.where(sub == 2, first_three[2], jnp.where(sub == 3, fourth, jnp.where(sub == 4, fifth, 0.0)))))
    return tuple(p.astype(F32) for p in three_parts(rows))


def scale_rows(scale, pattern):
    sub = lax.broadcasted_iota(jnp.int32, (8, TILE), 0)
    parts = [p.astype(F32) for p in three_parts(scale)]
    out = jnp.zeros((8, TILE), F32)
    for row, part in enumerate(pattern):
        out = jnp.where(sub == row, parts[part], out)
    return out


def squared(pos):
    return pos[0] * pos[0] + pos[1] * pos[1] + pos[2] * pos[2]


def assemble(parts, pos, mixed):
    sub, second, _, _, _ = rows_of()
    g = pos[0] * parts[0] + pos[1] * parts[1] + pos[2] * parts[2] - parts[3]
    s0 = jnp.broadcast_to(g[6:7], (8, TILE))
    s1 = jnp.broadcast_to(g[7:8], (8, TILE))
    s = jnp.where(second, s1, s0)
    return mixed * s - g


def kernel(
    lists_ref, split_ref, *refs
):
    sources, refs = refs[:9], refs[9:]
    outs, refs = refs[:3], refs[3:]
    (
    out_ref, copy_sem, out_sem, x_ref, geo_ref, dip_ref, acc_ref, eye_ref, near_ref, base_ref, target_ref, dist_even, dist_odd, coef_even, coef_odd,
    ) = refs
    eye = (
        lax.broadcasted_iota(jnp.int32, (TILE, TILE), 0) == lax.broadcasted_iota(jnp.int32, (TILE, TILE), 1)
    )
    eye16 = jnp.where(eye, 1.0, 0.0).astype(BF16)
    zero8 = jnp.zeros((8, TILE), F32)
    own_base = 4 * ROWS
    copies = []
    for g, source in enumerate(sources):
        place = x_ref.at[pl.ds(g * ROWS, ROWS), :]
        copies.append(pltpu.make_async_copy(source, place, copy_sem.at[g]))
        copies[-1].start()
    nt = (((1,), (1,)), ((), ()))
    eye_ref[0] = jnp.zeros((TILE, 2 * TILE), BF16)
    eye_ref[1] = jnp.concatenate(
        [jnp.where(eye, FAR_AWAY, 0.0).astype(BF16), jnp.zeros((TILE, TILE), BF16)], 1
    )

    eye_ref[2] = jnp.concatenate([eye16, eye16], 1)

    def clear(i, _):
        out_ref[pl.ds(pl.multiple_of(i * 64, 64), 64), :] = jnp.zeros((64, TILE), F32)
        return 0

    lax.fori_loop(0, out_ref.shape[0] // 64, clear, 0)
    copies[4].wait()

    def prepare(t, _):
        centre = (8.0, 8.0, (4 * t + 2).astype(F32))
        mu, pos, pol, mixed, own = site_vectors(x_ref, own_base + t, centre)
        dip_ref[t] = dipole_rows(mu, pos, mixed, own)
        hi, mid, lo = geometry_rows([-2.0 * p for p in pos], 1.0, squared(pos))
        scale = (-thole) * lax.rsqrt(pol)
        q = scale_rows(scale, (0, 1, 0, 1, 0, 2))
        stack = jnp.concatenate([hi, mid, hi, mid, hi, lo, q, zero8], 0).astype(BF16)
        moved = lax.dot_general(eye16, stack, nt, preferred_element_type=F32).astype(BF16)
        geo_ref[t] = moved
        acc_ref[t] = jnp.zeros((32, TILE), F32)
        return 0

    lax.fori_loop(0, TILES, prepare, 0, unroll=4)
    for g in range(9):
        if g != 4:
            copies[g].wait()
    geo_ref[DUMMY] = geo_ref[0]
    dip_ref[DUMMY] = dip_ref[0]

    def blank(at):
        near_ref[at] = DUMMY + 4 * GRID
        base_ref[at] = own_base
        target_ref[at] = UNUSED

    for k in range(2 * UNROLL):
        blank(k)
    total = jnp.int32(2 * UNROLL)
    def put(at, home, remote, g):
        target = remote + g * OUT_ROWS
        if g == 4:
            target = jnp.where(remote == home, UNUSED, target)
        near_ref[at] = home + g * GRID
        base_ref[at] = remote + g * ROWS
        target_ref[at] = target
        return at + 1

    for g in range(9):
        first = lists_ref[3 * g + 2, 8 - g]
        last = lists_ref[3 * g + 2, 9 - g]
        if g != 4:
            last = first + split_ref[g, 0]

        def incoming(p, at, g=g):
            return put(at, lists_ref[3 * g, p] & (TILES - 1), lists_ref[3 * g + 1, p], g)

        total = lax.fori_loop(first, last, incoming, total)
        if g != 4:
            first = lists_ref[14, g] + split_ref[9 + g, 0]
            last = lists_ref[14, g + 1]

            def kept(p, at, g=g):
                return put(at, lists_ref[13, p], lists_ref[12, p] & (TILES - 1), g)

            total = lax.fori_loop(first, last, kept, total)
    for k in range((HALVES + 2) * UNROLL):
        blank(total + k)
    groups = (total - 2 * UNROLL + UNROLL - 1) // UNROLL

    def home_of(at):
        return near_ref[at] & (GRID - 1)

    def origin(at):
        grid = near_ref[at] // GRID
        row = (grid * 11) // 32
        column = grid - 3 * row
        return (
            24.0 - domain_edge * row.astype(F32),
            24.0 - domain_edge * column.astype(F32),
            (4 * home_of(at) + 2).astype(F32),
        )

    def distances(dist_ref, u, at):
        base = base_ref[at]
        pos = [load_row(x_ref, base + (6 + k) * TILES) - c for k, c in enumerate(origin(at))]
        pol = load_row(x_ref, base + 9 * TILES)
        hi, mid, lo = geometry_rows(pos, squared(pos), 1.0)
        q = scale_rows(lax.rsqrt(pol), (0, 0, 1, 1, 2, 0))
        left = jnp.concatenate([hi, hi, mid, mid, lo, hi, zero8, zero8], 0).astype(BF16)
        right = jnp.concatenate([jnp.zeros((48, TILE), F32), q, zero8], 0).astype(BF16)
        same = (target_ref[at] == UNUSED).astype(jnp.int32)
        operand = jnp.concatenate([eye_ref[same], jnp.concatenate([left, right], 1)], 0)
        rows = jnp.concatenate([eye_ref[2, :, :TILE], geo_ref[home_of(at)]], 1)
        dist_ref[u] = jnp.dot(rows, operand, preferred_element_type=F32)

    def coefficients(dist_ref, coef_ref, u):
        dist_sq = dist_ref[u, :, :TILE]
        inv = lax.rsqrt(dist_sq)
        inv_sq = inv * inv
        inv_cube = inv_sq * inv
        cube = dist_sq * inv * dist_sq
        damp = cube * dist_ref[u, :, TILE:]
        decay = jnp.exp(damp)
        lam_three = 1.0 - decay
        lam_five = lam_three + damp * decay
        three = lam_three * inv_cube
        five = lam_five * inv_cube * inv_sq
        three_hi = three.astype(BF16)
        five_hi = five.astype(BF16)
        coef_ref[u, 0] = five_hi
        coef_ref[u, 1] = (five - five_hi.astype(F32)).astype(BF16)
        coef_ref[u, 2] = three_hi
        coef_ref[u, 3] = (three - three_hi.astype(F32)).astype(BF16)

    def folded(sums):
        total = sums[0:32, :TILE]
        for k in range(1, PARTS):
            total = total + (sums[32 * k:32 * k + 32, :TILE] + sums[32 * k - 32:32 * k, TILE:])
        return total

    def sums(coef_ref, u, at):
        mu, pos, pol, mixed, own = site_vectors(x_ref, base_ref[at], origin(at))
        rem = dipole_rows(mu, pos, mixed, own)
        five_hi, five_lo, three_hi, three_lo = [coef_ref[u, k] for k in range(4)]
        square = jnp.concatenate(
            [jnp.concatenate([five_hi, three_hi], 1), jnp.concatenate([five_lo, three_lo], 1)], 0
        )
        h = folded(lax.dot_general(rem, square, nt, preferred_element_type=F32))
        square = jnp.concatenate(
            [jnp.concatenate([five_hi, five_lo], 1), jnp.concatenate([three_hi, three_lo], 1)], 0
        )
        r = folded(jnp.dot(dip_ref[home_of(at)], square, preferred_element_type=F32))
        field = assemble([r[8 * j:8 * j + 8] for j in range(4)], pos, mixed)
        return home_of(at), target_ref[at], h, field

    def half(first, dist_now, dist_next, coef_now, coef_next):
        done = [sums(coef_now, u, first + u) for u in range(UNROLL)]
        for u in range(UNROLL):
            coefficients(dist_now, coef_next, u)
        for u in range(UNROLL):
            distances(dist_next, u, first + 2 * UNROLL + u)
        for home, target, h, field in done:
            acc_ref[home] += h
            out_ref[pl.ds(target, 8, stride=OUT_STRIDE), :] += field

    even = (dist_even, dist_odd, coef_even, coef_odd)
    odd = (dist_odd, dist_even, coef_odd, coef_even)

    def step(i, _):
        for k in range(HALVES):
            half((HALVES * i + k) * UNROLL, *(odd if k % 2 else even))
        return 0

    lax.fori_loop(0, (groups + 1 + HALVES) // HALVES, step, 0)

    sends = []
    for g in range(9):
        for k in range(6):
            source = out_ref.at[pl.ds(g * OUT_ROWS + k * OUT_STRIDE, TILES), :]
            place = outs[g % 3].at[k, g // 3]
            sends.append(pltpu.make_async_copy(source, place, out_sem.at[6 * g + k]))
    for k, send in enumerate(sends):
        if k // 6 != 4:
            send.start()

    def finish(t, _):
        centre = (8.0, 8.0, (4 * t + 2).astype(F32))
        mu, pos, pol, mixed, own = site_vectors(x_ref, own_base + t, centre)
        field = assemble([acc_ref[t, 8 * j:8 * j + 8] for j in range(4)], pos, mixed)
        out_ref[pl.ds(4 * OUT_ROWS + t, 8, stride=OUT_STRIDE), :] += field
        return 0

    lax.fori_loop(0, TILES, finish, 0, unroll=4)
    for send in sends[24:30]:
        send.start()
    for send in sends:
        send.wait()


FAR_AWAY = 2.0 ** 60
LIST = 9 * 2048 + (HALVES + 4) * UNROLL
OUT_STRIDE = TILES + 8
OUT_ROWS = 8 * OUT_STRIDE
UNUSED = 4 * OUT_ROWS + DUMMY


def field_kernel(lists, split, *sites):
    smem = pl.BlockSpec(memory_space=pltpu.SMEM)
    away = pl.BlockSpec(memory_space=pl.ANY)
    return pl.pallas_call(
        kernel,
        out_shape=[jax.ShapeDtypeStruct((6, 3, TILES, TILE), F32)] * 3,
        in_specs=[smem, smem] + [away] * 9,
        out_specs=[away] * 3,
        scratch_shapes=[
            pltpu.VMEM((9 * OUT_ROWS, TILE), F32),
            pltpu.SemaphoreType.DMA((9,)),
            pltpu.SemaphoreType.DMA((54,)),
            pltpu.VMEM((9 * ROWS, TILE), F32),
            pltpu.VMEM((TILES + 1, TILE, 64), BF16),
            pltpu.VMEM((TILES + 1, 32 * PARTS, 2 * TILE), BF16),
            pltpu.VMEM((TILES + 1, 32, TILE), F32),
            pltpu.VMEM((3, TILE, 2 * TILE), BF16),
            pltpu.SMEM((LIST,), jnp.int32),
            pltpu.SMEM((LIST,), jnp.int32),
            pltpu.SMEM((LIST,), jnp.int32),
            pltpu.VMEM((UNROLL, TILE, 2 * TILE), F32),
            pltpu.VMEM((UNROLL, TILE, 2 * TILE), F32),
            pltpu.VMEM((UNROLL, 4, TILE, TILE), BF16),
            pltpu.VMEM((UNROLL, 4, TILE, TILE), BF16),
        ],
        compiler_params=pltpu.CompilerParams(vmem_limit_bytes=63 * 1024 * 1024),
        name="pair_fields",
    )(lists, split, *sites)


CHUNKS = 4
TURNS = 5
EDGE = 8


def halo_kernel(sites_ref, lists_ref, counts_ref, *refs):
    outs, lists_out, split_ref = refs[:8], refs[8], refs[9]
    send_sem, recv_sem, list_send, list_recv, own_sem, *refs = refs[10:]
    nbr_counts, loads, mine, share_send, share_recv = refs
    outs = outs[:4] + (None,) + outs[4:]
    gx, gy = lax.axis_index("gx"), lax.axis_index("gy")
    n_gx, n_gy = lax.axis_size("gx"), lax.axis_size("gy")
    mesh_id = pl.DeviceIdType.MESH
    size = ROWS // CHUNKS

    def device(g):
        return (lax.rem(gx + g // 3 - 1 + n_gx, n_gx), lax.rem(gy + g % 3 - 1 + n_gy, n_gy))

    barrier = pltpu.get_barrier_semaphore()
    others = [g for g in range(9) if g != 4]
    for g in others:
        pl.semaphore_signal(barrier, inc=1, device_id=device(g), device_id_type=mesh_id)
    pl.semaphore_wait(barrier, 8)

    def piece(g, source, target, chunk):
        rows = pl.ds(chunk * size, size)
        return pltpu.make_async_remote_copy(
            src_ref=source.at[rows, :],
            dst_ref=outs[g].at[rows, :],
            send_sem=send_sem.at[g, chunk],
            recv_sem=recv_sem.at[g, chunk],
            device_id=device(target),
            device_id_type=mesh_id,
        )

    shared = []

    def share(turn, source, dest):
        for g in others:
            copy = pltpu.make_async_remote_copy(
                src_ref=source,
                dst_ref=dest.at[g],
                send_sem=share_send.at[turn, g],
                recv_sem=share_recv.at[turn, g],
                device_id=device(8 - g),
                device_id_type=mesh_id,
            )
            copy.start()
            shared.append(copy)

    share(0, counts_ref, nbr_counts)
    straight = {}
    for chunk in range(CHUNKS):
        for g in (1, 7, 3, 5):
            straight[g, chunk] = piece(g, sites_ref, 8 - g, chunk)
    for chunk in range(CHUNKS):
        for g in (1, 7, 3, 5):
            straight[g, chunk].start()
    listed = []
    for g in others:
        listed.append(
            pltpu.make_async_remote_copy(
                src_ref=lists_ref,
                dst_ref=lists_out.at[g],
                send_sem=list_send.at[g],
                recv_sem=list_recv.at[g],
                device_id=device(8 - g),
                device_id_type=mesh_id,
            )
        )
        listed[-1].start()
    own = pltpu.make_async_copy(lists_ref, lists_out.at[4], own_sem)
    own.start()
    first_edge = lax.rem(gy, EDGE) == 0
    last_edge = lax.rem(gy, EDGE) == EDGE - 1
    onward = {
        1: ((~last_edge, 0, 1, 5), (~first_edge, 2, 1, 3)),
        7: ((~last_edge, 6, 7, 5), (~first_edge, 8, 7, 3)),
        3: ((first_edge, 0, 3, 7), (first_edge, 6, 3, 1)),
        5: ((last_edge, 2, 5, 7), (last_edge, 8, 5, 1)),
    }

    def pass_on(g, chunk, action):
        for condition, slot, here, target in onward[g]:

            @pl.when(condition)
            def _(slot=slot, here=here, target=target):
                action(piece(slot, outs[here], target, chunk))

    incoming, outgoing, given, kept = {}, {}, {}, {}

    def balance(turn):
        for copy in shared[8 * turn:8 * turn + 8]:
            copy.wait_recv()
        if turn == 0:
            for g in others:
                given[g] = incoming[g] = nbr_counts[g, 8 - g:9 - g, :]
                kept[g] = outgoing[g] = counts_ref[g:g + 1, :]
        else:
            before = mine[turn - 1, 0:1, :]
            for g in others:
                theirs = loads[turn - 1, g, 0:1, :]
                come = jnp.floor((theirs - before) * (1.0 / 16.0))
                given[g] = jnp.clip(given[g] + come, 0.0, incoming[g])
                leave = jnp.floor((before - theirs) * (1.0 / 16.0))
                kept[g] = jnp.clip(kept[g] + leave, 0.0, outgoing[g])
        if turn < TURNS:
            load = counts_ref[4:5, :]
            for g in others:
                load = load + (outgoing[g] - kept[g]) + given[g]
            mine[turn] = jnp.broadcast_to(load, (8, TILE))
            share(turn + 1, mine.at[turn], loads.at[turn])

    for chunk in range(CHUNKS):
        balance(chunk)
        for g in (1, 7, 3, 5):
            straight[g, chunk].wait_recv()
            pass_on(g, chunk, lambda copy: copy.start())
    for turn in range(CHUNKS, TURNS + 1):
        balance(turn)
    blank = jnp.zeros((1, TILE), F32)
    rows = [given.get(g, blank) for g in range(9)] + [kept.get(g, blank) for g in range(9)]
    split_ref[...] = jnp.concatenate(rows + [blank] * 6, 0).astype(jnp.int32)
    for copy in shared:
        copy.wait_send()
    for chunk in range(CHUNKS):
        for g in (1, 7, 3, 5):
            straight[g, chunk].wait_send()
            pass_on(g, chunk, lambda copy: copy.wait_send())
        for g in (0, 2, 6, 8):
            piece(g, sites_ref, 8 - g, chunk).wait_recv()
    for copy in listed:
        copy.wait()
    own.wait()


def halo_exchange(sites, lists, counts):
    away = pl.BlockSpec(memory_space=pl.ANY)
    shapes = [jax.ShapeDtypeStruct(sites.shape, sites.dtype)] * 8
    shapes.append(jax.ShapeDtypeStruct((9,) + lists.shape, lists.dtype))
    shapes.append(jax.ShapeDtypeStruct((24, TILE), jnp.int32))
    vmem = pl.BlockSpec(memory_space=pltpu.VMEM)
    return pl.pallas_call(
        halo_kernel,
        out_shape=shapes,
        in_specs=[away, away, vmem],
        out_specs=[away] * 9 + [vmem],
        scratch_shapes=[
            pltpu.SemaphoreType.DMA((9, CHUNKS)),
            pltpu.SemaphoreType.DMA((9, CHUNKS)),
            pltpu.SemaphoreType.DMA((9,)),
            pltpu.SemaphoreType.DMA((9,)),
            pltpu.SemaphoreType.DMA,
            pltpu.VMEM((9, 16, TILE), F32),
            pltpu.VMEM((TURNS, 9, 8, TILE), F32),
            pltpu.VMEM((TURNS, 8, TILE), F32),
            pltpu.SemaphoreType.DMA((TURNS + 1, 9)),
            pltpu.SemaphoreType.DMA((TURNS + 1, 9)),
        ],
        compiler_params=pltpu.CompilerParams(collective_id=0, has_side_effects=True),
        name="halo",
    )(sites, lists, counts)


def return_kernel(
    low_ref, mid_ref, high_ref, perm_ref, pol_ref, field_ref, induced_ref,
    column, left, right, up, down, mid_sem, gy_send, gy_recv, gx_send, gx_recv,
):
    gx, gy = lax.axis_index("gx"), lax.axis_index("gy")
    n_gx, n_gy = lax.axis_size("gx"), lax.axis_size("gy")
    mesh_id = pl.DeviceIdType.MESH

    def device(row, col):
        return (lax.rem(gx + row + n_gx, n_gx), lax.rem(gy + col + n_gy, n_gy))

    barrier = pltpu.get_barrier_semaphore()
    for row, col in ((-1, 0), (1, 0), (0, -1), (0, 1)):
        pl.semaphore_signal(barrier, inc=1, device_id=device(row, col), device_id_type=mesh_id)
    pl.semaphore_wait(barrier, 4)

    def remote(source, dest, send, recv, way, k, target):
        return pltpu.make_async_remote_copy(
            src_ref=source.at[k],
            dst_ref=dest.at[k],
            send_sem=send.at[way, k],
            recv_sem=recv.at[way, k],
            device_id=target,
            device_id_type=mesh_id,
        )

    first, second, own = [], [], []
    for k in range(6):
        first.append(
            (
                remote(low_ref, right, gy_send, gy_recv, 0, k, device(0, -1)),
                remote(high_ref, left, gy_send, gy_recv, 1, k, device(0, 1)),
            )
        )
        own.append(pltpu.make_async_copy(mid_ref.at[k], column.at[k], mid_sem.at[k]))
        for copy in first[k]:
            copy.start()
        own[k].start()

    def finish(k):
        for copy in second[k]:
            copy.wait_recv()
        total = column[k, 1] + up[k] + down[k]
        field_ref[k] = total
        induced_ref[k] = pol_ref[...] * (perm_ref[k] + total)

    for k in range(6):
        own[k].wait()
        for copy in first[k]:
            copy.wait_recv()
        column[k] = column[k] + left[k] + right[k]
        second.append(
            (
                remote(column.at[:, 0], down, gx_send, gx_recv, 0, k, device(-1, 0)),
                remote(column.at[:, 2], up, gx_send, gx_recv, 1, k, device(1, 0)),
            )
        )
        for copy in second[k]:
            copy.start()
        if k >= 2:
            finish(k - 2)
    finish(4)
    finish(5)
    for pairs in first + second:
        for copy in pairs:
            copy.wait_send()


def return_terms(low, mid, high, perm, pol):
    away = pl.BlockSpec(memory_space=pl.ANY)
    vmem = pl.BlockSpec(memory_space=pltpu.VMEM)
    return pl.pallas_call(
        return_kernel,
        out_shape=[jax.ShapeDtypeStruct((6, TILES, TILE), F32)] * 2,
        in_specs=[away] * 3 + [vmem] * 2,
        out_specs=[vmem] * 2,
        scratch_shapes=[
            pltpu.VMEM((6, 3, TILES, TILE), F32),
            pltpu.VMEM((6, 3, TILES, TILE), F32),
            pltpu.VMEM((6, 3, TILES, TILE), F32),
            pltpu.VMEM((6, TILES, TILE), F32),
            pltpu.VMEM((6, TILES, TILE), F32),
            pltpu.SemaphoreType.DMA((6,)),
            pltpu.SemaphoreType.DMA((2, 6)),
            pltpu.SemaphoreType.DMA((2, 6)),
            pltpu.SemaphoreType.DMA((2, 6)),
            pltpu.SemaphoreType.DMA((2, 6)),
        ],
        compiler_params=pltpu.CompilerParams(
            collective_id=1, has_side_effects=True, vmem_limit_bytes=32 * 1024 * 1024
        ),
        name="return_terms",
    )(low, mid, high, perm, pol)


def local(positions, polarity, dipoles, perm_fields, pair_list, tile_counts):
    slot_total = pair_list.shape[3]
    sites = jnp.concatenate([dipoles, positions, polarity[None]], 0).reshape(10 * TILES, TILE)

    table = pair_list.reshape(2, slot_total)
    live = jnp.arange(slot_total, dtype=jnp.int32) < tile_counts.reshape(())
    far = jnp.where(live, table[1], 16 * TILES)
    far, near = lax.sort((far, table[0]), num_keys=1)
    bounds = jnp.arange(slot_total, dtype=jnp.int32)[:16] * TILES
    bounds = jnp.sum((far[None, :] < bounds[:, None]).astype(jnp.int32), 1)
    counts = (bounds[1:10] - bounds[:9]).astype(F32)
    counts = jnp.broadcast_to(jnp.pad(counts, (0, 7))[:, None], (16, TILE))
    bounds = jnp.concatenate([bounds, jnp.zeros((slot_total - 16,), jnp.int32)])
    lists = jnp.stack([far, near, bounds])
    *around_sites, lists, split = halo_exchange(sites, lists, counts)
    low, mid, high = field_kernel(
        lists.reshape(27, slot_total), split, *around_sites[:4], sites, *around_sites[4:]
    )
    perm = perm_fields.reshape(6, TILES, TILE)
    field, induced = return_terms(low, mid, high, perm, polarity.reshape(TILES, TILE))
    field = field.reshape(6, 1, 1, TILES * TILE)
    induced = induced.reshape(6, 1, 1, TILES * TILE)
    return (field, induced)


def solution(mesh):
    placed = (
        P(None, "gx", "gy", None),
        P("gx", "gy", None),
        P(None, "gx", "gy", None),
        P(None, "gx", "gy", None),
        P("gx", "gy", None, None),
        P("gx", "gy"),
    )
    return jax.shard_map(
        local,
        mesh=mesh,
        in_specs=placed,
        out_specs=(P(None, "gx", "gy", None), P(None, "gx", "gy", None)),
        check_vma=False,
    )
```

```python
import jax
import jax.numpy as jnp
from jax import lax
from jax.experimental import pallas as pl
from jax.experimental.pallas import tpu as pltpu
from jax.sharding import PartitionSpec as P

TILE = 128
TILES = 256
ROWS = 10 * TILES
UNROLL = 2
HALVES = 6
PARTS = 3
DUMMY = TILES
GRID = 2 * TILES

thole = 0.39
domain_edge = 16.0

F32 = jnp.float32
BF16 = jnp.bfloat16


def three_parts(value):
    high = value.astype(BF16)
    rest = value - high.astype(F32)
    middle = rest.astype(BF16)
    low = (rest - middle.astype(F32)).astype(BF16)
    return high, middle, low


def rows_of():
    sub = lax.broadcasted_iota(jnp.int32, (8, TILE), 0)
    second = (sub == 3) | (sub == 4) | (sub == 5) | (sub == 7)
    is_x = (sub == 0) | (sub == 3)
    is_y = (sub == 1) | (sub == 4)
    is_z = (sub == 2) | (sub == 5)
    return sub, second, is_x, is_y, is_z


def load_row(ref, row):
    return jnp.broadcast_to(ref[pl.ds(row, 1), :], (8, TILE))


def site_vectors(ref, base, centre):
    sub, second, is_x, is_y, is_z = rows_of()
    dips = [load_row(ref, base + k * TILES) for k in range(6)]
    pos = [load_row(ref, base + (6 + k) * TILES) - centre[k] for k in range(3)]
    pol = load_row(ref, base + 9 * TILES)
    mu = [jnp.where(second, dips[3 + j], dips[j]) for j in range(3)]
    mixed = jnp.where(is_x, pos[0], jnp.where(is_y, pos[1], jnp.where(is_z, pos[2], 1.0)))
    own = jnp.where(is_x, mu[0], jnp.where(is_y, mu[1], jnp.where(is_z, mu[2], 0.0)))
    return mu, pos, pol, mixed, own


def dipole_rows(mu, pos, mixed, own):
    dots = pos[0] * mu[0] + pos[1] * mu[1] + pos[2] * mu[2]
    tripled = 3.0 * mixed
    left = jnp.concatenate([tripled * mu[0], tripled * mu[1], tripled * mu[2], tripled * dots], 0)
    blank = jnp.zeros((16, TILE), BF16)
    right = jnp.concatenate([jnp.zeros((8, TILE), F32), -own], 0)
    out = []
    for l, r in zip(three_parts(left), three_parts(right)):
        out.append(jnp.concatenate([l, jnp.concatenate([blank, r], 0)], 1))
    return jnp.concatenate(out[:PARTS], 0)


def geometry_rows(first_three, fourth, fifth):
    sub = lax.broadcasted_iota(jnp.int32, (8, TILE), 0)
    rows = jnp.where(sub == 0, first_three[0], jnp.where(sub == 1, first_three[1], jnp.where(sub == 2, first_three[2], jnp.where(sub == 3, fourth, jnp.where(sub == 4, fifth, 0.0)))))
    return tuple(p.astype(F32) for p in three_parts(rows))


def scale_rows(scale, pattern):
    sub = lax.broadcasted_iota(jnp.int32, (8, TILE), 0)
    parts = [p.astype(F32) for p in three_parts(scale)]
    out = jnp.zeros((8, TILE), F32)
    for row, part in enumerate(pattern):
        out = jnp.where(sub == row, parts[part], out)
    return out


def squared(pos):
    return pos[0] * pos[0] + pos[1] * pos[1] + pos[2] * pos[2]


def assemble(parts, pos, mixed):
    sub, second, _, _, _ = rows_of()
    g = pos[0] * parts[0] + pos[1] * parts[1] + pos[2] * parts[2] - parts[3]
    s0 = jnp.broadcast_to(g[6:7], (8, TILE))
    s1 = jnp.broadcast_to(g[7:8], (8, TILE))
    s = jnp.where(second, s1, s0)
    return mixed * s - g


def kernel(
    lists_ref, split_ref, *refs
):
    sources, refs = refs[:9], refs[9:]
    outs, refs = refs[:3], refs[3:]
    (
    out_ref, copy_sem, out_sem, x_ref, geo_ref, dip_ref, acc_ref, eye_ref, near_ref, base_ref, target_ref, dist_even, dist_odd, coef_even, coef_odd,
    ) = refs
    eye = (
        lax.broadcasted_iota(jnp.int32, (TILE, TILE), 0) == lax.broadcasted_iota(jnp.int32, (TILE, TILE), 1)
    )
    eye16 = jnp.where(eye, 1.0, 0.0).astype(BF16)
    zero8 = jnp.zeros((8, TILE), F32)
    own_base = 4 * ROWS
    copies = []
    for g, source in enumerate(sources):
        place = x_ref.at[pl.ds(g * ROWS, ROWS), :]
        copies.append(pltpu.make_async_copy(source, place, copy_sem.at[g]))
        copies[-1].start()
    nt = (((1,), (1,)), ((), ()))
    eye_ref[0] = jnp.zeros((TILE, 2 * TILE), BF16)
    eye_ref[1] = jnp.concatenate(
        [jnp.where(eye, FAR_AWAY, 0.0).astype(BF16), jnp.zeros((TILE, TILE), BF16)], 1
    )

    eye_ref[2] = jnp.concatenate([eye16, eye16], 1)

    def clear(i, _):
        out_ref[pl.ds(pl.multiple_of(i * 64, 64), 64), :] = jnp.zeros((64, TILE), F32)
        return 0

    lax.fori_loop(0, out_ref.shape[0] // 64, clear, 0)
    copies[4].wait()

    def prepare(t, _):
        centre = (8.0, 8.0, (4 * t + 2).astype(F32))
        mu, pos, pol, mixed, own = site_vectors(x_ref, own_base + t, centre)
        dip_ref[t] = dipole_rows(mu, pos, mixed, own)
        hi, mid, lo = geometry_rows([-2.0 * p for p in pos], 1.0, squared(pos))
        scale = (-thole) * lax.rsqrt(pol)
        q = scale_rows(scale, (0, 1, 0, 1, 0, 2))
        stack = jnp.concatenate([hi, mid, hi, mid, hi, lo, q, zero8], 0).astype(BF16)
        moved = lax.dot_general(eye16, stack, nt, preferred_element_type=F32).astype(BF16)
        geo_ref[t] = moved
        acc_ref[t] = jnp.zeros((32, TILE), F32)
        return 0

    lax.fori_loop(0, TILES, prepare, 0, unroll=4)
    for g in range(9):
        if g != 4:
            copies[g].wait()
    geo_ref[DUMMY] = geo_ref[0]
    dip_ref[DUMMY] = dip_ref[0]

    def blank(at):
        near_ref[at] = DUMMY + 4 * GRID
        base_ref[at] = own_base
        target_ref[at] = UNUSED

    for k in range(2 * UNROLL):
        blank(k)
    total = jnp.int32(2 * UNROLL)
    def put(at, home, remote, g):
        target = remote + g * OUT_ROWS
        if g == 4:
            target = jnp.where(remote == home, UNUSED, target)
        near_ref[at] = home + g * GRID
        base_ref[at] = remote + g * ROWS
        target_ref[at] = target
        return at + 1

    for g in range(9):
        first = lists_ref[3 * g + 2, 8 - g]
        last = lists_ref[3 * g + 2, 9 - g]
        if g != 4:
            last = first + split_ref[g, 0]

        def incoming(p, at, g=g):
            return put(at, lists_ref[3 * g, p] & (TILES - 1), lists_ref[3 * g + 1, p], g)

        total = lax.fori_loop(first, last, incoming, total)
        if g != 4:
            first = lists_ref[14, g] + split_ref[9 + g, 0]
            last = lists_ref[14, g + 1]

            def kept(p, at, g=g):
                return put(at, lists_ref[13, p], lists_ref[12, p] & (TILES - 1), g)

            total = lax.fori_loop(first, last, kept, total)
    for k in range((HALVES + 2) * UNROLL):
        blank(total + k)
    groups = (total - 2 * UNROLL + UNROLL - 1) // UNROLL

    def home_of(at):
        return near_ref[at] & (GRID - 1)

    def origin(at):
        grid = near_ref[at] // GRID
        row = (grid * 11) // 32
        column = grid - 3 * row
        return (
            24.0 - domain_edge * row.astype(F32),
            24.0 - domain_edge * column.astype(F32),
            (4 * home_of(at) + 2).astype(F32),
        )

    def distances(dist_ref, u, at):
        base = base_ref[at]
        pos = [load_row(x_ref, base + (6 + k) * TILES) - c for k, c in enumerate(origin(at))]
        pol = load_row(x_ref, base + 9 * TILES)
        hi, mid, lo = geometry_rows(pos, squared(pos), 1.0)
        q = scale_rows(lax.rsqrt(pol), (0, 0, 1, 1, 2, 0))
        left = jnp.concatenate([hi, hi, mid, mid, lo, hi, zero8, zero8], 0).astype(BF16)
        right = jnp.concatenate([jnp.zeros((48, TILE), F32), q, zero8], 0).astype(BF16)
        same = (target_ref[at] == UNUSED).astype(jnp.int32)
        operand = jnp.concatenate([eye_ref[same], jnp.concatenate([left, right], 1)], 0)
        rows = jnp.concatenate([eye_ref[2, :, :TILE], geo_ref[home_of(at)]], 1)
        dist_ref[u] = jnp.dot(rows, operand, preferred_element_type=F32)

    def coefficients(dist_ref, coef_ref, u):
        dist_sq = dist_ref[u, :, :TILE]
        inv = lax.rsqrt(dist_sq)
        inv_sq = inv * inv
        inv_cube = inv_sq * inv
        cube = dist_sq * inv * dist_sq
        damp = cube * dist_ref[u, :, TILE:]
        decay = jnp.exp(damp)
        lam_three = 1.0 - decay
        lam_five = lam_three + damp * decay
        three = lam_three * inv_cube
        five = lam_five * inv_cube * inv_sq
        three_hi = three.astype(BF16)
        five_hi = five.astype(BF16)
        coef_ref[u, 0] = five_hi
        coef_ref[u, 1] = (five - five_hi.astype(F32)).astype(BF16)
        coef_ref[u, 2] = three_hi
        coef_ref[u, 3] = (three - three_hi.astype(F32)).astype(BF16)

    def folded(sums):
        total = sums[0:32, :TILE]
        for k in range(1, PARTS):
            total = total + (sums[32 * k:32 * k + 32, :TILE] + sums[32 * k - 32:32 * k, TILE:])
        return total

    def sums(coef_ref, u, at):
        mu, pos, pol, mixed, own = site_vectors(x_ref, base_ref[at], origin(at))
        rem = dipole_rows(mu, pos, mixed, own)
        five_hi, five_lo, three_hi, three_lo = [coef_ref[u, k] for k in range(4)]
        square = jnp.concatenate(
            [jnp.concatenate([five_hi, three_hi], 1), jnp.concatenate([five_lo, three_lo], 1)], 0
        )
        h = folded(lax.dot_general(rem, square, nt, preferred_element_type=F32))
        square = jnp.concatenate(
            [jnp.concatenate([five_hi, five_lo], 1), jnp.concatenate([three_hi, three_lo], 1)], 0
        )
        r = folded(jnp.dot(dip_ref[home_of(at)], square, preferred_element_type=F32))
        field = assemble([r[8 * j:8 * j + 8] for j in range(4)], pos, mixed)
        return home_of(at), target_ref[at], h, field

    def half(first, dist_now, dist_next, coef_now, coef_next):
        done = [sums(coef_now, u, first + u) for u in range(UNROLL)]
        for u in range(UNROLL):
            coefficients(dist_now, coef_next, u)
        for u in range(UNROLL):
            distances(dist_next, u, first + 2 * UNROLL + u)
        for home, target, h, field in done:
            acc_ref[home] += h
            out_ref[pl.ds(target, 8, stride=OUT_STRIDE), :] += field

    even = (dist_even, dist_odd, coef_even, coef_odd)
    odd = (dist_odd, dist_even, coef_odd, coef_even)

    def step(i, _):
        for k in range(HALVES):
            half((HALVES * i + k) * UNROLL, *(odd if k % 2 else even))
        return 0

    lax.fori_loop(0, (groups + 1 + HALVES) // HALVES, step, 0)

    sends = []
    for g in range(9):
        for k in range(6):
            source = out_ref.at[pl.ds(g * OUT_ROWS + k * OUT_STRIDE, TILES), :]
            place = outs[g % 3].at[k, g // 3]
            sends.append(pltpu.make_async_copy(source, place, out_sem.at[6 * g + k]))
    for k, send in enumerate(sends):
        if k // 6 != 4:
            send.start()

    def finish(t, _):
        centre = (8.0, 8.0, (4 * t + 2).astype(F32))
        mu, pos, pol, mixed, own = site_vectors(x_ref, own_base + t, centre)
        field = assemble([acc_ref[t, 8 * j:8 * j + 8] for j in range(4)], pos, mixed)
        out_ref[pl.ds(4 * OUT_ROWS + t, 8, stride=OUT_STRIDE), :] += field
        return 0

    lax.fori_loop(0, TILES, finish, 0, unroll=4)
    for send in sends[24:30]:
        send.start()
    for send in sends:
        send.wait()


FAR_AWAY = 2.0 ** 60
LIST = 9 * 2048 + (HALVES + 4) * UNROLL
OUT_STRIDE = TILES + 8
OUT_ROWS = 8 * OUT_STRIDE
UNUSED = 4 * OUT_ROWS + DUMMY


def field_kernel(lists, split, *sites):
    smem = pl.BlockSpec(memory_space=pltpu.SMEM)
    away = pl.BlockSpec(memory_space=pl.ANY)
    return pl.pallas_call(
        kernel,
        out_shape=[jax.ShapeDtypeStruct((6, 3, TILES, TILE), F32)] * 3,
        in_specs=[smem, smem] + [away] * 9,
        out_specs=[away] * 3,
        scratch_shapes=[
            pltpu.VMEM((9 * OUT_ROWS, TILE), F32),
            pltpu.SemaphoreType.DMA((9,)),
            pltpu.SemaphoreType.DMA((54,)),
            pltpu.VMEM((9 * ROWS, TILE), F32),
            pltpu.VMEM((TILES + 1, TILE, 64), BF16),
            pltpu.VMEM((TILES + 1, 32 * PARTS, 2 * TILE), BF16),
            pltpu.VMEM((TILES + 1, 32, TILE), F32),
            pltpu.VMEM((3, TILE, 2 * TILE), BF16),
            pltpu.SMEM((LIST,), jnp.int32),
            pltpu.SMEM((LIST,), jnp.int32),
            pltpu.SMEM((LIST,), jnp.int32),
            pltpu.VMEM((UNROLL, TILE, 2 * TILE), F32),
            pltpu.VMEM((UNROLL, TILE, 2 * TILE), F32),
            pltpu.VMEM((UNROLL, 4, TILE, TILE), BF16),
            pltpu.VMEM((UNROLL, 4, TILE, TILE), BF16),
        ],
        compiler_params=pltpu.CompilerParams(vmem_limit_bytes=63 * 1024 * 1024),
        name="pair_fields",
    )(lists, split, *sites)


CHUNKS = 4
TURNS = 3
AHEAD = 2
EDGE = 8


def halo_kernel(sites_ref, lists_ref, counts_ref, *refs):
    outs, lists_out, split_ref = refs[:8], refs[8], refs[9]
    send_sem, recv_sem, list_send, list_recv, own_sem, *refs = refs[10:]
    nbr_counts, loads, mine, share_send, share_recv = refs
    outs = outs[:4] + (None,) + outs[4:]
    gx, gy = lax.axis_index("gx"), lax.axis_index("gy")
    n_gx, n_gy = lax.axis_size("gx"), lax.axis_size("gy")
    mesh_id = pl.DeviceIdType.MESH
    size = ROWS // CHUNKS

    def device(g):
        return (lax.rem(gx + g // 3 - 1 + n_gx, n_gx), lax.rem(gy + g % 3 - 1 + n_gy, n_gy))

    barrier = pltpu.get_barrier_semaphore()
    others = [g for g in range(9) if g != 4]
    for g in others:
        pl.semaphore_signal(barrier, inc=1, device_id=device(g), device_id_type=mesh_id)
    pl.semaphore_wait(barrier, 8)

    def piece(g, source, target, chunk):
        rows = pl.ds(chunk * size, size)
        return pltpu.make_async_remote_copy(
            src_ref=source.at[rows, :],
            dst_ref=outs[g].at[rows, :],
            send_sem=send_sem.at[g, chunk],
            recv_sem=recv_sem.at[g, chunk],
            device_id=device(target),
            device_id_type=mesh_id,
        )

    shared = []

    def share(turn, source, dest):
        for g in others:
            copy = pltpu.make_async_remote_copy(
                src_ref=source,
                dst_ref=dest.at[g],
                send_sem=share_send.at[turn, g],
                recv_sem=share_recv.at[turn, g],
                device_id=device(8 - g),
                device_id_type=mesh_id,
            )
            copy.start()
            shared.append(copy)

    share(0, counts_ref, nbr_counts)
    straight = {}
    for chunk in range(CHUNKS):
        for g in (1, 7, 3, 5):
            straight[g, chunk] = piece(g, sites_ref, 8 - g, chunk)
    def begin(chunk):
        for g in (1, 7, 3, 5):
            straight[g, chunk].start()

    for chunk in range(AHEAD):
        begin(chunk)
    listed = []
    for g in others:
        listed.append(
            pltpu.make_async_remote_copy(
                src_ref=lists_ref,
                dst_ref=lists_out.at[g],
                send_sem=list_send.at[g],
                recv_sem=list_recv.at[g],
                device_id=device(8 - g),
                device_id_type=mesh_id,
            )
        )
        listed[-1].start()
    own = pltpu.make_async_copy(lists_ref, lists_out.at[4], own_sem)
    own.start()
    first_edge = lax.rem(gy, EDGE) == 0
    last_edge = lax.rem(gy, EDGE) == EDGE - 1
    onward = {
        1: ((~last_edge, 0, 1, 5), (~first_edge, 2, 1, 3)),
        7: ((~last_edge, 6, 7, 5), (~first_edge, 8, 7, 3)),
        3: ((first_edge, 0, 3, 7), (first_edge, 6, 3, 1)),
        5: ((last_edge, 2, 5, 7), (last_edge, 8, 5, 1)),
    }

    def pass_on(g, chunk, action):
        for condition, slot, here, target in onward[g]:

            @pl.when(condition)
            def _(slot=slot, here=here, target=target):
                action(piece(slot, outs[here], target, chunk))

    incoming, outgoing, given, kept = {}, {}, {}, {}

    def balance(turn):
        for copy in shared[8 * turn:8 * turn + 8]:
            copy.wait_recv()
        if turn == 0:
            for g in others:
                given[g] = incoming[g] = nbr_counts[g, 8 - g:9 - g, :]
                kept[g] = outgoing[g] = counts_ref[g:g + 1, :]
        else:
            before = mine[turn - 1, 0:1, :]
            for g in others:
                theirs = loads[turn - 1, g, 0:1, :]
                come = jnp.floor((theirs - before) * (1.0 / 16.0))
                given[g] = jnp.clip(given[g] + come, 0.0, incoming[g])
                leave = jnp.floor((before - theirs) * (1.0 / 16.0))
                kept[g] = jnp.clip(kept[g] + leave, 0.0, outgoing[g])
        if turn < TURNS:
            load = counts_ref[4:5, :]
            for g in others:
                load = load + (outgoing[g] - kept[g]) + given[g]
            mine[turn] = jnp.broadcast_to(load, (8, TILE))
            share(turn + 1, mine.at[turn], loads.at[turn])

    for chunk in range(CHUNKS):
        balance(chunk)
        for g in (1, 7, 3, 5):
            straight[g, chunk].wait_recv()
            pass_on(g, chunk, lambda copy: copy.start())
        if chunk + AHEAD < CHUNKS:
            begin(chunk + AHEAD)
    for turn in range(CHUNKS, TURNS + 1):
        balance(turn)
    blank = jnp.zeros((1, TILE), F32)
    rows = [given.get(g, blank) for g in range(9)] + [kept.get(g, blank) for g in range(9)]
    split_ref[...] = jnp.concatenate(rows + [blank] * 6, 0).astype(jnp.int32)
    for copy in shared:
        copy.wait_send()
    for chunk in range(CHUNKS):
        for g in (1, 7, 3, 5):
            straight[g, chunk].wait_send()
            pass_on(g, chunk, lambda copy: copy.wait_send())
        for g in (0, 2, 6, 8):
            piece(g, sites_ref, 8 - g, chunk).wait_recv()
    for copy in listed:
        copy.wait()
    own.wait()


def halo_exchange(sites, lists, counts):
    away = pl.BlockSpec(memory_space=pl.ANY)
    shapes = [jax.ShapeDtypeStruct(sites.shape, sites.dtype)] * 8
    shapes.append(jax.ShapeDtypeStruct((9,) + lists.shape, lists.dtype))
    shapes.append(jax.ShapeDtypeStruct((24, TILE), jnp.int32))
    vmem = pl.BlockSpec(memory_space=pltpu.VMEM)
    return pl.pallas_call(
        halo_kernel,
        out_shape=shapes,
        in_specs=[away, away, vmem],
        out_specs=[away] * 9 + [vmem],
        scratch_shapes=[
            pltpu.SemaphoreType.DMA((9, CHUNKS)),
            pltpu.SemaphoreType.DMA((9, CHUNKS)),
            pltpu.SemaphoreType.DMA((9,)),
            pltpu.SemaphoreType.DMA((9,)),
            pltpu.SemaphoreType.DMA,
            pltpu.VMEM((9, 16, TILE), F32),
            pltpu.VMEM((TURNS, 9, 8, TILE), F32),
            pltpu.VMEM((TURNS, 8, TILE), F32),
            pltpu.SemaphoreType.DMA((TURNS + 1, 9)),
            pltpu.SemaphoreType.DMA((TURNS + 1, 9)),
        ],
        compiler_params=pltpu.CompilerParams(collective_id=0, has_side_effects=True),
        name="halo",
    )(sites, lists, counts)


def return_kernel(
    low_ref, mid_ref, high_ref, perm_ref, pol_ref, field_ref, induced_ref,
    column, left, right, up, down, mid_sem, gy_send, gy_recv, gx_send, gx_recv,
):
    gx, gy = lax.axis_index("gx"), lax.axis_index("gy")
    n_gx, n_gy = lax.axis_size("gx"), lax.axis_size("gy")
    mesh_id = pl.DeviceIdType.MESH

    def device(row, col):
        return (lax.rem(gx + row + n_gx, n_gx), lax.rem(gy + col + n_gy, n_gy))

    barrier = pltpu.get_barrier_semaphore()
    for row, col in ((-1, 0), (1, 0), (0, -1), (0, 1)):
        pl.semaphore_signal(barrier, inc=1, device_id=device(row, col), device_id_type=mesh_id)
    pl.semaphore_wait(barrier, 4)

    def remote(source, dest, send, recv, way, k, target):
        return pltpu.make_async_remote_copy(
            src_ref=source.at[k],
            dst_ref=dest.at[k],
            send_sem=send.at[way, k],
            recv_sem=recv.at[way, k],
            device_id=target,
            device_id_type=mesh_id,
        )

    first, second, own = [], [], []
    for k in range(6):
        first.append(
            (
                remote(low_ref, right, gy_send, gy_recv, 0, k, device(0, -1)),
                remote(high_ref, left, gy_send, gy_recv, 1, k, device(0, 1)),
            )
        )
        own.append(pltpu.make_async_copy(mid_ref.at[k], column.at[k], mid_sem.at[k]))
        for copy in first[k]:
            copy.start()
        own[k].start()

    def finish(k):
        for copy in second[k]:
            copy.wait_recv()
        total = column[k, 1] + up[k] + down[k]
        field_ref[k] = total
        induced_ref[k] = pol_ref[...] * (perm_ref[k] + total)

    for k in range(6):
        own[k].wait()
        for copy in first[k]:
            copy.wait_recv()
        column[k] = column[k] + left[k] + right[k]
        second.append(
            (
                remote(column.at[:, 0], down, gx_send, gx_recv, 0, k, device(-1, 0)),
                remote(column.at[:, 2], up, gx_send, gx_recv, 1, k, device(1, 0)),
            )
        )
        for copy in second[k]:
            copy.start()
        if k >= 2:
            finish(k - 2)
    finish(4)
    finish(5)
    for pairs in first + second:
        for copy in pairs:
            copy.wait_send()


def return_terms(low, mid, high, perm, pol):
    away = pl.BlockSpec(memory_space=pl.ANY)
    vmem = pl.BlockSpec(memory_space=pltpu.VMEM)
    return pl.pallas_call(
        return_kernel,
        out_shape=[jax.ShapeDtypeStruct((6, TILES, TILE), F32)] * 2,
        in_specs=[away] * 3 + [vmem] * 2,
        out_specs=[vmem] * 2,
        scratch_shapes=[
            pltpu.VMEM((6, 3, TILES, TILE), F32),
            pltpu.VMEM((6, 3, TILES, TILE), F32),
            pltpu.VMEM((6, 3, TILES, TILE), F32),
            pltpu.VMEM((6, TILES, TILE), F32),
            pltpu.VMEM((6, TILES, TILE), F32),
            pltpu.SemaphoreType.DMA((6,)),
            pltpu.SemaphoreType.DMA((2, 6)),
            pltpu.SemaphoreType.DMA((2, 6)),
            pltpu.SemaphoreType.DMA((2, 6)),
            pltpu.SemaphoreType.DMA((2, 6)),
        ],
        compiler_params=pltpu.CompilerParams(
            collective_id=1, has_side_effects=True, vmem_limit_bytes=63 * 1024 * 1024
        ),
        name="return_terms",
    )(low, mid, high, perm, pol)


def local(positions, polarity, dipoles, perm_fields, pair_list, tile_counts):
    slot_total = pair_list.shape[3]
    sites = jnp.concatenate([dipoles, positions, polarity[None]], 0).reshape(10 * TILES, TILE)

    table = pair_list.reshape(2, slot_total)
    live = jnp.arange(slot_total, dtype=jnp.int32) < tile_counts.reshape(())
    far = jnp.where(live, table[1], 16 * TILES)
    far, near = lax.sort((far, table[0]), num_keys=1)
    bounds = jnp.arange(slot_total, dtype=jnp.int32)[:16] * TILES
    bounds = jnp.sum((far[None, :] < bounds[:, None]).astype(jnp.int32), 1)
    counts = (bounds[1:10] - bounds[:9]).astype(F32)
    counts = jnp.broadcast_to(jnp.pad(counts, (0, 7))[:, None], (16, TILE))
    bounds = jnp.concatenate([bounds, jnp.zeros((slot_total - 16,), jnp.int32)])
    lists = jnp.stack([far, near, bounds])
    *around_sites, lists, split = halo_exchange(sites, lists, counts)
    low, mid, high = field_kernel(
        lists.reshape(27, slot_total), split, *around_sites[:4], sites, *around_sites[4:]
    )
    perm = perm_fields.reshape(6, TILES, TILE)
    field, induced = return_terms(low, mid, high, perm, polarity.reshape(TILES, TILE))
    field = field.reshape(6, 1, 1, TILES * TILE)
    induced = induced.reshape(6, 1, 1, TILES * TILE)
    return (field, induced)


def solution(mesh):
    placed = (
        P(None, "gx", "gy", None),
        P("gx", "gy", None),
        P(None, "gx", "gy", None),
        P(None, "gx", "gy", None),
        P("gx", "gy", None, None),
        P("gx", "gy"),
    )
    return jax.shard_map(
        local,
        mesh=mesh,
        in_specs=placed,
        out_specs=(P(None, "gx", "gy", None), P(None, "gx", "gy", None)),
        check_vma=False,
    )
```

```python
import jax
import jax.numpy as jnp
from jax import lax
from jax.experimental import pallas as pl
from jax.experimental.pallas import tpu as pltpu
from jax.sharding import PartitionSpec as P

TILE = 128
TILES = 256
ROWS = 10 * TILES
UNROLL = 2
HALVES = 6
PARTS = 3
DUMMY = TILES
GRID = 2 * TILES

thole = 0.39
domain_edge = 16.0

F32 = jnp.float32
BF16 = jnp.bfloat16


def three_parts(value):
    high = value.astype(BF16)
    rest = value - high.astype(F32)
    middle = rest.astype(BF16)
    low = (rest - middle.astype(F32)).astype(BF16)
    return high, middle, low


def rows_of():
    sub = lax.broadcasted_iota(jnp.int32, (8, TILE), 0)
    second = (sub == 3) | (sub == 4) | (sub == 5) | (sub == 7)
    is_x = (sub == 0) | (sub == 3)
    is_y = (sub == 1) | (sub == 4)
    is_z = (sub == 2) | (sub == 5)
    return sub, second, is_x, is_y, is_z


def load_row(ref, row):
    return jnp.broadcast_to(ref[pl.ds(row, 1), :], (8, TILE))


def site_vectors(ref, base, centre):
    sub, second, is_x, is_y, is_z = rows_of()
    dips = [load_row(ref, base + k * TILES) for k in range(6)]
    pos = [load_row(ref, base + (6 + k) * TILES) - centre[k] for k in range(3)]
    pol = load_row(ref, base + 9 * TILES)
    mu = [jnp.where(second, dips[3 + j], dips[j]) for j in range(3)]
    mixed = jnp.where(is_x, pos[0], jnp.where(is_y, pos[1], jnp.where(is_z, pos[2], 1.0)))
    own = jnp.where(is_x, mu[0], jnp.where(is_y, mu[1], jnp.where(is_z, mu[2], 0.0)))
    return mu, pos, pol, mixed, own


def dipole_rows(mu, pos, mixed, own):
    dots = pos[0] * mu[0] + pos[1] * mu[1] + pos[2] * mu[2]
    tripled = 3.0 * mixed
    left = jnp.concatenate([tripled * mu[0], tripled * mu[1], tripled * mu[2], tripled * dots], 0)
    blank = jnp.zeros((16, TILE), BF16)
    right = jnp.concatenate([jnp.zeros((8, TILE), F32), -own], 0)
    out = []
    for l, r in zip(three_parts(left), three_parts(right)):
        out.append(jnp.concatenate([l, jnp.concatenate([blank, r], 0)], 1))
    return jnp.concatenate(out[:PARTS], 0)


def geometry_rows(first_three, fourth, fifth):
    sub = lax.broadcasted_iota(jnp.int32, (8, TILE), 0)
    rows = jnp.where(sub == 0, first_three[0], jnp.where(sub == 1, first_three[1], jnp.where(sub == 2, first_three[2], jnp.where(sub == 3, fourth, jnp.where(sub == 4, fifth, 0.0)))))
    return tuple(p.astype(F32) for p in three_parts(rows))


def scale_rows(scale, pattern):
    sub = lax.broadcasted_iota(jnp.int32, (8, TILE), 0)
    parts = [p.astype(F32) for p in three_parts(scale)]
    out = jnp.zeros((8, TILE), F32)
    for row, part in enumerate(pattern):
        out = jnp.where(sub == row, parts[part], out)
    return out


def squared(pos):
    return pos[0] * pos[0] + pos[1] * pos[1] + pos[2] * pos[2]


def assemble(parts, pos, mixed):
    sub, second, _, _, _ = rows_of()
    g = pos[0] * parts[0] + pos[1] * parts[1] + pos[2] * parts[2] - parts[3]
    s0 = jnp.broadcast_to(g[6:7], (8, TILE))
    s1 = jnp.broadcast_to(g[7:8], (8, TILE))
    s = jnp.where(second, s1, s0)
    return mixed * s - g


def kernel(
    lists_ref, split_ref, *refs
):
    sources, refs = refs[:9], refs[9:]
    outs, refs = refs[:3], refs[3:]
    (
    out_ref, copy_sem, out_sem, x_ref, geo_ref, dip_ref, acc_ref, eye_ref, near_ref, base_ref, target_ref, dist_even, dist_odd, coef_even, coef_odd,
    ) = refs
    eye = (
        lax.broadcasted_iota(jnp.int32, (TILE, TILE), 0) == lax.broadcasted_iota(jnp.int32, (TILE, TILE), 1)
    )
    eye16 = jnp.where(eye, 1.0, 0.0).astype(BF16)
    zero8 = jnp.zeros((8, TILE), F32)
    own_base = 4 * ROWS
    copies = []
    for g, source in enumerate(sources):
        place = x_ref.at[pl.ds(g * ROWS, ROWS), :]
        copies.append(pltpu.make_async_copy(source, place, copy_sem.at[g]))
        copies[-1].start()
    nt = (((1,), (1,)), ((), ()))
    eye_ref[0] = jnp.zeros((TILE, 2 * TILE), BF16)
    eye_ref[1] = jnp.concatenate(
        [jnp.where(eye, FAR_AWAY, 0.0).astype(BF16), jnp.zeros((TILE, TILE), BF16)], 1
    )

    eye_ref[2] = jnp.concatenate([eye16, eye16], 1)

    def clear(i, _):
        out_ref[pl.ds(pl.multiple_of(i * 64, 64), 64), :] = jnp.zeros((64, TILE), F32)
        return 0

    lax.fori_loop(0, out_ref.shape[0] // 64, clear, 0)
    copies[4].wait()

    def prepare(t, _):
        centre = (8.0, 8.0, (4 * t + 2).astype(F32))
        mu, pos, pol, mixed, own = site_vectors(x_ref, own_base + t, centre)
        dip_ref[t] = dipole_rows(mu, pos, mixed, own)
        hi, mid, lo = geometry_rows([-2.0 * p for p in pos], 1.0, squared(pos))
        scale = (-thole) * lax.rsqrt(pol)
        q = scale_rows(scale, (0, 1, 0, 1, 0, 2))
        stack = jnp.concatenate([hi, mid, hi, mid, hi, lo, q, zero8], 0).astype(BF16)
        moved = lax.dot_general(eye16, stack, nt, preferred_element_type=F32).astype(BF16)
        geo_ref[t] = moved
        acc_ref[t] = jnp.zeros((32, TILE), F32)
        return 0

    lax.fori_loop(0, TILES, prepare, 0, unroll=4)
    for g in range(9):
        if g != 4:
            copies[g].wait()
    geo_ref[DUMMY] = geo_ref[0]
    dip_ref[DUMMY] = dip_ref[0]

    def blank(at):
        near_ref[at] = DUMMY + 4 * GRID
        base_ref[at] = own_base
        target_ref[at] = UNUSED

    for k in range(2 * UNROLL):
        blank(k)
    total = jnp.int32(2 * UNROLL)
    def put(at, home, remote, g):
        target = remote + g * OUT_ROWS
        if g == 4:
            target = jnp.where(remote == home, UNUSED, target)
        near_ref[at] = home + g * GRID
        base_ref[at] = remote + g * ROWS
        target_ref[at] = target
        return at + 1

    for g in range(9):
        first = lists_ref[3 * g + 2, 8 - g]
        last = lists_ref[3 * g + 2, 9 - g]
        if g != 4:
            last = first + split_ref[g, 0]

        def incoming(p, at, g=g):
            return put(at, lists_ref[3 * g, p] & (TILES - 1), lists_ref[3 * g + 1, p], g)

        total = lax.fori_loop(first, last, incoming, total)
        if g != 4:
            first = lists_ref[14, g] + split_ref[9 + g, 0]
            last = lists_ref[14, g + 1]

            def kept(p, at, g=g):
                return put(at, lists_ref[13, p], lists_ref[12, p] & (TILES - 1), g)

            total = lax.fori_loop(first, last, kept, total)
    for k in range((HALVES + 2) * UNROLL):
        blank(total + k)
    groups = (total - 2 * UNROLL + UNROLL - 1) // UNROLL

    def home_of(at):
        return near_ref[at] & (GRID - 1)

    def origin(at):
        grid = near_ref[at] // GRID
        row = (grid * 11) // 32
        column = grid - 3 * row
        return (
            24.0 - domain_edge * row.astype(F32),
            24.0 - domain_edge * column.astype(F32),
            (4 * home_of(at) + 2).astype(F32),
        )

    def distances(dist_ref, u, at):
        base = base_ref[at]
        pos = [load_row(x_ref, base + (6 + k) * TILES) - c for k, c in enumerate(origin(at))]
        pol = load_row(x_ref, base + 9 * TILES)
        hi, mid, lo = geometry_rows(pos, squared(pos), 1.0)
        q = scale_rows(lax.rsqrt(pol), (0, 0, 1, 1, 2, 0))
        left = jnp.concatenate([hi, hi, mid, mid, lo, hi, zero8, zero8], 0).astype(BF16)
        right = jnp.concatenate([jnp.zeros((48, TILE), F32), q, zero8], 0).astype(BF16)
        same = (target_ref[at] == UNUSED).astype(jnp.int32)
        operand = jnp.concatenate([eye_ref[same], jnp.concatenate([left, right], 1)], 0)
        rows = jnp.concatenate([eye_ref[2, :, :TILE], geo_ref[home_of(at)]], 1)
        dist_ref[u] = jnp.dot(rows, operand, preferred_element_type=F32)

    def coefficients(dist_ref, coef_ref, u):
        dist_sq = dist_ref[u, :, :TILE]
        inv = lax.rsqrt(dist_sq)
        inv_sq = inv * inv
        inv_cube = inv_sq * inv
        cube = dist_sq * inv * dist_sq
        damp = cube * dist_ref[u, :, TILE:]
        decay = jnp.exp(damp)
        lam_three = 1.0 - decay
        lam_five = lam_three + damp * decay
        three = lam_three * inv_cube
        five = lam_five * inv_cube * inv_sq
        three_hi = three.astype(BF16)
        five_hi = five.astype(BF16)
        coef_ref[u, 0] = five_hi
        coef_ref[u, 1] = (five - five_hi.astype(F32)).astype(BF16)
        coef_ref[u, 2] = three_hi
        coef_ref[u, 3] = (three - three_hi.astype(F32)).astype(BF16)

    def folded(sums):
        total = sums[0:32, :TILE]
        for k in range(1, PARTS):
            total = total + (sums[32 * k:32 * k + 32, :TILE] + sums[32 * k - 32:32 * k, TILE:])
        return total

    def sums(coef_ref, u, at):
        mu, pos, pol, mixed, own = site_vectors(x_ref, base_ref[at], origin(at))
        rem = dipole_rows(mu, pos, mixed, own)
        five_hi, five_lo, three_hi, three_lo = [coef_ref[u, k] for k in range(4)]
        square = jnp.concatenate(
            [jnp.concatenate([five_hi, three_hi], 1), jnp.concatenate([five_lo, three_lo], 1)], 0
        )
        h = folded(lax.dot_general(rem, square, nt, preferred_element_type=F32))
        square = jnp.concatenate(
            [jnp.concatenate([five_hi, five_lo], 1), jnp.concatenate([three_hi, three_lo], 1)], 0
        )
        r = folded(jnp.dot(dip_ref[home_of(at)], square, preferred_element_type=F32))
        field = assemble([r[8 * j:8 * j + 8] for j in range(4)], pos, mixed)
        return home_of(at), target_ref[at], h, field

    def half(first, dist_now, dist_next, coef_now, coef_next):
        done = [sums(coef_now, u, first + u) for u in range(UNROLL)]
        for u in range(UNROLL):
            coefficients(dist_now, coef_next, u)
        for u in range(UNROLL):
            distances(dist_next, u, first + 2 * UNROLL + u)
        for home, target, h, field in done:
            acc_ref[home] += h
            out_ref[pl.ds(target, 8, stride=OUT_STRIDE), :] += field

    even = (dist_even, dist_odd, coef_even, coef_odd)
    odd = (dist_odd, dist_even, coef_odd, coef_even)

    def step(i, _):
        for k in range(HALVES):
            half((HALVES * i + k) * UNROLL, *(odd if k % 2 else even))
        return 0

    lax.fori_loop(0, (groups + 1 + HALVES) // HALVES, step, 0)

    sends = []
    for g in range(9):
        for k in range(6):
            source = out_ref.at[pl.ds(g * OUT_ROWS + k * OUT_STRIDE, TILES), :]
            place = outs[g % 3].at[k, g // 3]
            sends.append(pltpu.make_async_copy(source, place, out_sem.at[6 * g + k]))
    for k, send in enumerate(sends):
        if k // 6 != 4:
            send.start()

    def finish(t, _):
        centre = (8.0, 8.0, (4 * t + 2).astype(F32))
        mu, pos, pol, mixed, own = site_vectors(x_ref, own_base + t, centre)
        field = assemble([acc_ref[t, 8 * j:8 * j + 8] for j in range(4)], pos, mixed)
        out_ref[pl.ds(4 * OUT_ROWS + t, 8, stride=OUT_STRIDE), :] += field
        return 0

    lax.fori_loop(0, TILES, finish, 0, unroll=4)
    for send in sends[24:30]:
        send.start()
    for send in sends:
        send.wait()


FAR_AWAY = 2.0 ** 60
LIST = 9 * 2048 + (HALVES + 4) * UNROLL
OUT_STRIDE = TILES + 8
OUT_ROWS = 8 * OUT_STRIDE
UNUSED = 4 * OUT_ROWS + DUMMY


def field_kernel(lists, split, *sites):
    smem = pl.BlockSpec(memory_space=pltpu.SMEM)
    away = pl.BlockSpec(memory_space=pl.ANY)
    return pl.pallas_call(
        kernel,
        out_shape=[jax.ShapeDtypeStruct((6, 3, TILES, TILE), F32)] * 3,
        in_specs=[smem, smem] + [away] * 9,
        out_specs=[away] * 3,
        scratch_shapes=[
            pltpu.VMEM((9 * OUT_ROWS, TILE), F32),
            pltpu.SemaphoreType.DMA((9,)),
            pltpu.SemaphoreType.DMA((54,)),
            pltpu.VMEM((9 * ROWS, TILE), F32),
            pltpu.VMEM((TILES + 1, TILE, 64), BF16),
            pltpu.VMEM((TILES + 1, 32 * PARTS, 2 * TILE), BF16),
            pltpu.VMEM((TILES + 1, 32, TILE), F32),
            pltpu.VMEM((3, TILE, 2 * TILE), BF16),
            pltpu.SMEM((LIST,), jnp.int32),
            pltpu.SMEM((LIST,), jnp.int32),
            pltpu.SMEM((LIST,), jnp.int32),
            pltpu.VMEM((UNROLL, TILE, 2 * TILE), F32),
            pltpu.VMEM((UNROLL, TILE, 2 * TILE), F32),
            pltpu.VMEM((UNROLL, 4, TILE, TILE), BF16),
            pltpu.VMEM((UNROLL, 4, TILE, TILE), BF16),
        ],
        compiler_params=pltpu.CompilerParams(vmem_limit_bytes=63 * 1024 * 1024),
        name="pair_fields",
    )(lists, split, *sites)


CHUNKS = 4
TURNS = 3
AHEAD = 2
EDGE = 8


def halo_kernel(sites_ref, lists_ref, counts_ref, *refs):
    outs, lists_out, split_ref = refs[:8], refs[8], refs[9]
    send_sem, recv_sem, list_send, list_recv, own_sem, *refs = refs[10:]
    nbr_counts, loads, mine, share_send, share_recv = refs
    outs = outs[:4] + (None,) + outs[4:]
    gx, gy = lax.axis_index("gx"), lax.axis_index("gy")
    n_gx, n_gy = lax.axis_size("gx"), lax.axis_size("gy")
    mesh_id = pl.DeviceIdType.MESH
    size = ROWS // CHUNKS

    def device(g):
        return (lax.rem(gx + g // 3 - 1 + n_gx, n_gx), lax.rem(gy + g % 3 - 1 + n_gy, n_gy))

    barrier = pltpu.get_barrier_semaphore()
    others = [g for g in range(9) if g != 4]
    for g in others:
        pl.semaphore_signal(barrier, inc=1, device_id=device(g), device_id_type=mesh_id)
    pl.semaphore_wait(barrier, 8)

    def piece(g, source, target, chunk):
        rows = pl.ds(chunk * size, size)
        return pltpu.make_async_remote_copy(
            src_ref=source.at[rows, :],
            dst_ref=outs[g].at[rows, :],
            send_sem=send_sem.at[g, chunk],
            recv_sem=recv_sem.at[g, chunk],
            device_id=device(target),
            device_id_type=mesh_id,
        )

    shared = []

    def share(turn, source, dest):
        for g in others:
            copy = pltpu.make_async_remote_copy(
                src_ref=source,
                dst_ref=dest.at[g],
                send_sem=share_send.at[turn, g],
                recv_sem=share_recv.at[turn, g],
                device_id=device(8 - g),
                device_id_type=mesh_id,
            )
            copy.start()
            shared.append(copy)

    share(0, counts_ref, nbr_counts)
    straight = {}
    for chunk in range(CHUNKS):
        for g in (1, 7, 3, 5):
            straight[g, chunk] = piece(g, sites_ref, 8 - g, chunk)
    def begin(chunk):
        for g in (1, 7, 3, 5):
            straight[g, chunk].start()

    for chunk in range(AHEAD):
        begin(chunk)
    listed = []
    for g in others:
        listed.append(
            pltpu.make_async_remote_copy(
                src_ref=lists_ref,
                dst_ref=lists_out.at[g],
                send_sem=list_send.at[g],
                recv_sem=list_recv.at[g],
                device_id=device(8 - g),
                device_id_type=mesh_id,
            )
        )
        listed[-1].start()
    own = pltpu.make_async_copy(lists_ref, lists_out.at[4], own_sem)
    own.start()
    first_edge = lax.rem(gy, EDGE) == 0
    last_edge = lax.rem(gy, EDGE) == EDGE - 1
    onward = {
        1: ((~last_edge, 0, 1, 5), (~first_edge, 2, 1, 3)),
        7: ((~last_edge, 6, 7, 5), (~first_edge, 8, 7, 3)),
        3: ((first_edge, 0, 3, 7), (first_edge, 6, 3, 1)),
        5: ((last_edge, 2, 5, 7), (last_edge, 8, 5, 1)),
    }

    def pass_on(g, chunk, action):
        for condition, slot, here, target in onward[g]:

            @pl.when(condition)
            def _(slot=slot, here=here, target=target):
                action(piece(slot, outs[here], target, chunk))

    incoming, outgoing, given, kept = {}, {}, {}, {}

    def balance(turn):
        for copy in shared[8 * turn:8 * turn + 8]:
            copy.wait_recv()
        if turn == 0:
            for g in others:
                given[g] = incoming[g] = nbr_counts[g, 8 - g:9 - g, :]
                kept[g] = outgoing[g] = counts_ref[g:g + 1, :]
        else:
            before = mine[turn - 1, 0:1, :]
            for g in others:
                theirs = loads[turn - 1, g, 0:1, :]
                come = jnp.floor((theirs - before) * (1.0 / 16.0))
                given[g] = jnp.clip(given[g] + come, 0.0, incoming[g])
                leave = jnp.floor((before - theirs) * (1.0 / 16.0))
                kept[g] = jnp.clip(kept[g] + leave, 0.0, outgoing[g])
        if turn < TURNS:
            load = counts_ref[4:5, :]
            for g in others:
                load = load + (outgoing[g] - kept[g]) + given[g]
            mine[turn] = jnp.broadcast_to(load, (8, TILE))
            share(turn + 1, mine.at[turn], loads.at[turn])

    for chunk in range(CHUNKS):
        balance(chunk)
        for g in (1, 7, 3, 5):
            straight[g, chunk].wait_recv()
            pass_on(g, chunk, lambda copy: copy.start())
        if chunk + AHEAD < CHUNKS:
            begin(chunk + AHEAD)
    for turn in range(CHUNKS, TURNS + 1):
        balance(turn)
    blank = jnp.zeros((1, TILE), F32)
    rows = [given.get(g, blank) for g in range(9)] + [kept.get(g, blank) for g in range(9)]
    split_ref[...] = jnp.concatenate(rows + [blank] * 6, 0).astype(jnp.int32)
    for copy in shared:
        copy.wait_send()
    for chunk in range(CHUNKS):
        for g in (1, 7, 3, 5):
            straight[g, chunk].wait_send()
            pass_on(g, chunk, lambda copy: copy.wait_send())
        for g in (0, 2, 6, 8):
            piece(g, sites_ref, 8 - g, chunk).wait_recv()
    for copy in listed:
        copy.wait()
    own.wait()


def halo_exchange(sites, lists, counts):
    away = pl.BlockSpec(memory_space=pl.ANY)
    shapes = [jax.ShapeDtypeStruct(sites.shape, sites.dtype)] * 8
    shapes.append(jax.ShapeDtypeStruct((9,) + lists.shape, lists.dtype))
    shapes.append(jax.ShapeDtypeStruct((24, TILE), jnp.int32))
    vmem = pl.BlockSpec(memory_space=pltpu.VMEM)
    return pl.pallas_call(
        halo_kernel,
        out_shape=shapes,
        in_specs=[away, away, vmem],
        out_specs=[away] * 9 + [vmem],
        scratch_shapes=[
            pltpu.SemaphoreType.DMA((9, CHUNKS)),
            pltpu.SemaphoreType.DMA((9, CHUNKS)),
            pltpu.SemaphoreType.DMA((9,)),
            pltpu.SemaphoreType.DMA((9,)),
            pltpu.SemaphoreType.DMA,
            pltpu.VMEM((9, 16, TILE), F32),
            pltpu.VMEM((TURNS, 9, 8, TILE), F32),
            pltpu.VMEM((TURNS, 8, TILE), F32),
            pltpu.SemaphoreType.DMA((TURNS + 1, 9)),
            pltpu.SemaphoreType.DMA((TURNS + 1, 9)),
        ],
        compiler_params=pltpu.CompilerParams(collective_id=0, has_side_effects=True),
        name="halo",
    )(sites, lists, counts)


def return_kernel(
    low_ref, mid_ref, high_ref, perm_ref, pol_ref, field_ref, induced_ref,
    column, left, right, up, down, edge_in, edge_own, edge_sum,
    mid_sem, gy_send, gy_recv, gx_send, gx_recv, edge_send, edge_recv, edge_sem,
):
    gx, gy = lax.axis_index("gx"), lax.axis_index("gy")
    n_gx, n_gy = lax.axis_size("gx"), lax.axis_size("gy")
    mesh_id = pl.DeviceIdType.MESH

    def device(row, col):
        return (lax.rem(gx + row + n_gx, n_gx), lax.rem(gy + col + n_gy, n_gy))

    barrier = pltpu.get_barrier_semaphore()
    for row, col in ((-1, 0), (1, 0), (0, -1), (0, 1)):
        pl.semaphore_signal(barrier, inc=1, device_id=device(row, col), device_id_type=mesh_id)
    pl.semaphore_wait(barrier, 4)

    def remote(source, dest, send, recv, way, k, target):
        return pltpu.make_async_remote_copy(
            src_ref=source.at[k],
            dst_ref=dest.at[k],
            send_sem=send.at[way, k],
            recv_sem=recv.at[way, k],
            device_id=target,
            device_id_type=mesh_id,
        )

    edges = (lax.rem(gy, EDGE) == 0, lax.rem(gy, EDGE) == EDGE - 1)
    sources, dests = (low_ref, high_ref), (right, left)
    targets = (device(0, -1), device(0, 1))
    second, own = [], []

    def either(condition, yes, no):
        pl.when(condition)(yes)
        pl.when(jnp.logical_not(condition))(no)

    def whole(way, k):
        return remote(sources[way], dests[way], gy_send, gy_recv, way, k, targets[way])

    def summed(way, k):
        return pltpu.make_async_remote_copy(
            src_ref=edge_sum.at[k],
            dst_ref=dests[way].at[k, 1],
            send_sem=gy_send.at[way, k],
            recv_sem=gy_recv.at[way, k],
            device_id=targets[way],
            device_id_type=mesh_id,
        )

    def along(way, k, slot):
        return pltpu.make_async_remote_copy(
            src_ref=sources[way].at[k, 2 - 2 * slot],
            dst_ref=edge_in.at[slot, k],
            send_sem=edge_send.at[slot, k],
            recv_sem=edge_recv.at[slot, k],
            device_id=device(1 - 2 * slot, 0),
            device_id_type=mesh_id,
        )

    def centre(way, k):
        return pltpu.make_async_copy(sources[way].at[k, 1], edge_own.at[k], edge_sem.at[k])

    for k in range(6):
        for way in range(2):

            def start_edge(way=way, k=k):
                along(way, k, 0).start()
                along(way, k, 1).start()
                centre(way, k).start()

            either(edges[way], start_edge, lambda way=way, k=k: whole(way, k).start())
        own.append(pltpu.make_async_copy(mid_ref.at[k], column.at[k], mid_sem.at[k]))
        own[k].start()

    for way in range(2):

        @pl.when(edges[1 - way])
        def _(way=way):
            for k in range(6):
                for row in (0, 2):
                    dests[way][k, row] = jnp.zeros((TILES, TILE), F32)

    def edge_stage(k):
        for way in range(2):

            @pl.when(edges[way])
            def _(way=way):
                centre(way, k).wait()
                along(way, k, 0).wait_recv()
                along(way, k, 1).wait_recv()
                edge_sum[k] = edge_own[k] + edge_in[0, k] + edge_in[1, k]
                summed(way, k).start()

    def finish(k):
        for copy in second[k]:
            copy.wait_recv()
        total = column[k, 1] + up[k] + down[k]
        field_ref[k] = total
        induced_ref[k] = pol_ref[...] * (perm_ref[k] + total)

    edge_stage(0)
    edge_stage(1)
    for k in range(6):
        own[k].wait()
        for way in range(2):
            either(
                edges[1 - way],
                lambda way=way: summed(way, k).wait_recv(),
                lambda way=way: whole(way, k).wait_recv(),
            )
        column[k] = column[k] + left[k] + right[k]
        second.append(
            (
                remote(column.at[:, 0], down, gx_send, gx_recv, 0, k, device(-1, 0)),
                remote(column.at[:, 2], up, gx_send, gx_recv, 1, k, device(1, 0)),
            )
        )
        for copy in second[k]:
            copy.start()
        if k + 2 < 6:
            edge_stage(k + 2)
        if k >= 2:
            finish(k - 2)
    finish(4)
    finish(5)
    for k in range(6):
        for way in range(2):

            def end_edge(way=way, k=k):
                along(way, k, 0).wait_send()
                along(way, k, 1).wait_send()
                summed(way, k).wait_send()

            either(edges[way], end_edge, lambda way=way, k=k: whole(way, k).wait_send())
        for copy in second[k]:
            copy.wait_send()


def return_terms(low, mid, high, perm, pol):
    away = pl.BlockSpec(memory_space=pl.ANY)
    vmem = pl.BlockSpec(memory_space=pltpu.VMEM)
    return pl.pallas_call(
        return_kernel,
        out_shape=[jax.ShapeDtypeStruct((6, TILES, TILE), F32)] * 2,
        in_specs=[away] * 3 + [vmem] * 2,
        out_specs=[vmem] * 2,
        scratch_shapes=[
            pltpu.VMEM((6, 3, TILES, TILE), F32),
            pltpu.VMEM((6, 3, TILES, TILE), F32),
            pltpu.VMEM((6, 3, TILES, TILE), F32),
            pltpu.VMEM((6, TILES, TILE), F32),
            pltpu.VMEM((6, TILES, TILE), F32),
            pltpu.VMEM((2, 6, TILES, TILE), F32),
            pltpu.VMEM((6, TILES, TILE), F32),
            pltpu.VMEM((6, TILES, TILE), F32),
            pltpu.SemaphoreType.DMA((6,)),
            pltpu.SemaphoreType.DMA((2, 6)),
            pltpu.SemaphoreType.DMA((2, 6)),
            pltpu.SemaphoreType.DMA((2, 6)),
            pltpu.SemaphoreType.DMA((2, 6)),
            pltpu.SemaphoreType.DMA((2, 6)),
            pltpu.SemaphoreType.DMA((2, 6)),
            pltpu.SemaphoreType.DMA((6,)),
        ],
        compiler_params=pltpu.CompilerParams(
            collective_id=1, has_side_effects=True, vmem_limit_bytes=63 * 1024 * 1024
        ),
        name="return_terms",
    )(low, mid, high, perm, pol)


def local(positions, polarity, dipoles, perm_fields, pair_list, tile_counts):
    slot_total = pair_list.shape[3]
    sites = jnp.concatenate([dipoles, positions, polarity[None]], 0).reshape(10 * TILES, TILE)

    table = pair_list.reshape(2, slot_total)
    live = jnp.arange(slot_total, dtype=jnp.int32) < tile_counts.reshape(())
    far = jnp.where(live, table[1], 16 * TILES)
    far, near = lax.sort((far, table[0]), num_keys=1)
    bounds = jnp.arange(slot_total, dtype=jnp.int32)[:16] * TILES
    bounds = jnp.sum((far[None, :] < bounds[:, None]).astype(jnp.int32), 1)
    counts = (bounds[1:10] - bounds[:9]).astype(F32)
    counts = jnp.broadcast_to(jnp.pad(counts, (0, 7))[:, None], (16, TILE))
    bounds = jnp.concatenate([bounds, jnp.zeros((slot_total - 16,), jnp.int32)])
    lists = jnp.stack([far, near, bounds])
    *around_sites, lists, split = halo_exchange(sites, lists, counts)
    low, mid, high = field_kernel(
        lists.reshape(27, slot_total), split, *around_sites[:4], sites, *around_sites[4:]
    )
    perm = perm_fields.reshape(6, TILES, TILE)
    field, induced = return_terms(low, mid, high, perm, polarity.reshape(TILES, TILE))
    field = field.reshape(6, 1, 1, TILES * TILE)
    induced = induced.reshape(6, 1, 1, TILES * TILE)
    return (field, induced)


def solution(mesh):
    placed = (
        P(None, "gx", "gy", None),
        P("gx", "gy", None),
        P(None, "gx", "gy", None),
        P(None, "gx", "gy", None),
        P("gx", "gy", None, None),
        P("gx", "gy"),
    )
    return jax.shard_map(
        local,
        mesh=mesh,
        in_specs=placed,
        out_specs=(P(None, "gx", "gy", None), P(None, "gx", "gy", None)),
        check_vma=False,
    )
```

```python
import jax
import jax.numpy as jnp
from jax import lax
from jax.experimental import pallas as pl
from jax.experimental.pallas import tpu as pltpu
from jax.sharding import PartitionSpec as P

TILE = 128
TILES = 256
ROWS = 10 * TILES
UNROLL = 2
HALVES = 6
PARTS = 3
DUMMY = TILES
GRID = 2 * TILES

thole = 0.39
domain_edge = 16.0

F32 = jnp.float32
BF16 = jnp.bfloat16


def three_parts(value):
    high = value.astype(BF16)
    rest = value - high.astype(F32)
    middle = rest.astype(BF16)
    low = (rest - middle.astype(F32)).astype(BF16)
    return high, middle, low


def rows_of():
    sub = lax.broadcasted_iota(jnp.int32, (8, TILE), 0)
    second = (sub == 3) | (sub == 4) | (sub == 5) | (sub == 7)
    is_x = (sub == 0) | (sub == 3)
    is_y = (sub == 1) | (sub == 4)
    is_z = (sub == 2) | (sub == 5)
    return sub, second, is_x, is_y, is_z


def load_row(ref, row):
    return jnp.broadcast_to(ref[pl.ds(row, 1), :], (8, TILE))


def site_vectors(ref, base, centre):
    sub, second, is_x, is_y, is_z = rows_of()
    dips = [load_row(ref, base + k * TILES) for k in range(6)]
    pos = [load_row(ref, base + (6 + k) * TILES) - centre[k] for k in range(3)]
    pol = load_row(ref, base + 9 * TILES)
    mu = [jnp.where(second, dips[3 + j], dips[j]) for j in range(3)]
    mixed = jnp.where(is_x, pos[0], jnp.where(is_y, pos[1], jnp.where(is_z, pos[2], 1.0)))
    own = jnp.where(is_x, mu[0], jnp.where(is_y, mu[1], jnp.where(is_z, mu[2], 0.0)))
    return mu, pos, pol, mixed, own


def dipole_rows(mu, pos, mixed, own):
    dots = pos[0] * mu[0] + pos[1] * mu[1] + pos[2] * mu[2]
    tripled = 3.0 * mixed
    left = jnp.concatenate([tripled * mu[0], tripled * mu[1], tripled * mu[2], tripled * dots], 0)
    blank = jnp.zeros((16, TILE), BF16)
    right = jnp.concatenate([jnp.zeros((8, TILE), F32), -own], 0)
    out = []
    for l, r in zip(three_parts(left), three_parts(right)):
        out.append(jnp.concatenate([l, jnp.concatenate([blank, r], 0)], 1))
    return jnp.concatenate(out[:PARTS], 0)


def geometry_rows(first_three, fourth, fifth):
    sub = lax.broadcasted_iota(jnp.int32, (8, TILE), 0)
    rows = jnp.where(sub == 0, first_three[0], jnp.where(sub == 1, first_three[1], jnp.where(sub == 2, first_three[2], jnp.where(sub == 3, fourth, jnp.where(sub == 4, fifth, 0.0)))))
    return tuple(p.astype(F32) for p in three_parts(rows))


def scale_rows(scale, pattern):
    sub = lax.broadcasted_iota(jnp.int32, (8, TILE), 0)
    parts = [p.astype(F32) for p in three_parts(scale)]
    out = jnp.zeros((8, TILE), F32)
    for row, part in enumerate(pattern):
        out = jnp.where(sub == row, parts[part], out)
    return out


def squared(pos):
    return pos[0] * pos[0] + pos[1] * pos[1] + pos[2] * pos[2]


def assemble(parts, pos, mixed):
    sub, second, _, _, _ = rows_of()
    g = pos[0] * parts[0] + pos[1] * parts[1] + pos[2] * parts[2] - parts[3]
    s0 = jnp.broadcast_to(g[6:7], (8, TILE))
    s1 = jnp.broadcast_to(g[7:8], (8, TILE))
    s = jnp.where(second, s1, s0)
    return mixed * s - g


def kernel(
    lists_ref, split_ref, *refs
):
    sources, refs = refs[:9], refs[9:]
    outs, refs = refs[:3], refs[3:]
    (
    out_ref, copy_sem, out_sem, x_ref, geo_ref, dip_ref, acc_ref, eye_ref, near_ref, base_ref, target_ref, dist_even, dist_odd, coef_even, coef_odd,
    ) = refs
    eye = (
        lax.broadcasted_iota(jnp.int32, (TILE, TILE), 0) == lax.broadcasted_iota(jnp.int32, (TILE, TILE), 1)
    )
    eye16 = jnp.where(eye, 1.0, 0.0).astype(BF16)
    zero8 = jnp.zeros((8, TILE), F32)
    own_base = 4 * ROWS
    copies = []
    for g, source in enumerate(sources):
        place = x_ref.at[pl.ds(g * ROWS, ROWS), :]
        copies.append(pltpu.make_async_copy(source, place, copy_sem.at[g]))
        copies[-1].start()
    nt = (((1,), (1,)), ((), ()))
    eye_ref[0] = jnp.zeros((TILE, 2 * TILE), BF16)
    eye_ref[1] = jnp.concatenate(
        [jnp.where(eye, FAR_AWAY, 0.0).astype(BF16), jnp.zeros((TILE, TILE), BF16)], 1
    )

    eye_ref[2] = jnp.concatenate([eye16, eye16], 1)

    def clear(i, _):
        out_ref[pl.ds(pl.multiple_of(i * 64, 64), 64), :] = jnp.zeros((64, TILE), F32)
        return 0

    lax.fori_loop(0, out_ref.shape[0] // 64, clear, 0)
    copies[4].wait()

    def prepare(t, _):
        centre = (8.0, 8.0, (4 * t + 2).astype(F32))
        mu, pos, pol, mixed, own = site_vectors(x_ref, own_base + t, centre)
        dip_ref[t] = dipole_rows(mu, pos, mixed, own)
        hi, mid, lo = geometry_rows([-2.0 * p for p in pos], 1.0, squared(pos))
        scale = (-thole) * lax.rsqrt(pol)
        q = scale_rows(scale, (0, 1, 0, 1, 0, 2))
        stack = jnp.concatenate([hi, mid, hi, mid, hi, lo, q, zero8], 0).astype(BF16)
        moved = lax.dot_general(eye16, stack, nt, preferred_element_type=F32).astype(BF16)
        geo_ref[t] = moved
        acc_ref[t] = jnp.zeros((32, TILE), F32)
        return 0

    lax.fori_loop(0, TILES, prepare, 0, unroll=4)
    for g in range(9):
        if g != 4:
            copies[g].wait()
    geo_ref[DUMMY] = geo_ref[0]
    dip_ref[DUMMY] = dip_ref[0]

    def blank(at):
        near_ref[at] = DUMMY + 4 * GRID
        base_ref[at] = own_base
        target_ref[at] = UNUSED

    for k in range(2 * UNROLL):
        blank(k)
    total = jnp.int32(2 * UNROLL)
    def put(at, home, remote, g):
        target = remote + g * OUT_ROWS
        if g == 4:
            target = jnp.where(remote == home, UNUSED, target)
        near_ref[at] = home + g * GRID
        base_ref[at] = remote + g * ROWS
        target_ref[at] = target
        return at + 1

    for g in range(9):
        first = lists_ref[3 * g + 2, 8 - g]
        last = lists_ref[3 * g + 2, 9 - g]
        if g != 4:
            last = first + split_ref[g, 0]

        def incoming(p, at, g=g):
            return put(at, lists_ref[3 * g, p] & (TILES - 1), lists_ref[3 * g + 1, p], g)

        total = lax.fori_loop(first, last, incoming, total)
        if g != 4:
            first = lists_ref[14, g] + split_ref[9 + g, 0]
            last = lists_ref[14, g + 1]

            def kept(p, at, g=g):
                return put(at, lists_ref[13, p], lists_ref[12, p] & (TILES - 1), g)

            total = lax.fori_loop(first, last, kept, total)
    for k in range((HALVES + 2) * UNROLL):
        blank(total + k)
    groups = (total - 2 * UNROLL + UNROLL - 1) // UNROLL

    def home_of(at):
        return near_ref[at] & (GRID - 1)

    def origin(at):
        grid = near_ref[at] // GRID
        row = (grid * 11) // 32
        column = grid - 3 * row
        return (
            24.0 - domain_edge * row.astype(F32),
            24.0 - domain_edge * column.astype(F32),
            (4 * home_of(at) + 2).astype(F32),
        )

    def distances(dist_ref, u, at):
        base = base_ref[at]
        pos = [load_row(x_ref, base + (6 + k) * TILES) - c for k, c in enumerate(origin(at))]
        pol = load_row(x_ref, base + 9 * TILES)
        hi, mid, lo = geometry_rows(pos, squared(pos), 1.0)
        q = scale_rows(lax.rsqrt(pol), (0, 0, 1, 1, 2, 0))
        left = jnp.concatenate([hi, hi, mid, mid, lo, hi, zero8, zero8], 0).astype(BF16)
        right = jnp.concatenate([jnp.zeros((48, TILE), F32), q, zero8], 0).astype(BF16)
        same = (target_ref[at] == UNUSED).astype(jnp.int32)
        operand = jnp.concatenate([eye_ref[same], jnp.concatenate([left, right], 1)], 0)
        rows = jnp.concatenate([eye_ref[2, :, :TILE], geo_ref[home_of(at)]], 1)
        dist_ref[u] = jnp.dot(rows, operand, preferred_element_type=F32)

    def coefficients(dist_ref, coef_ref, u):
        dist_sq = dist_ref[u, :, :TILE]
        inv = lax.rsqrt(dist_sq)
        inv_sq = inv * inv
        inv_cube = inv_sq * inv
        cube = dist_sq * inv * dist_sq
        damp = cube * dist_ref[u, :, TILE:]
        decay = jnp.exp(damp)
        lam_three = 1.0 - decay
        lam_five = lam_three + damp * decay
        three = lam_three * inv_cube
        five = lam_five * inv_cube * inv_sq
        three_hi = three.astype(BF16)
        five_hi = five.astype(BF16)
        coef_ref[u, 0] = five_hi
        coef_ref[u, 1] = (five - five_hi.astype(F32)).astype(BF16)
        coef_ref[u, 2] = three_hi
        coef_ref[u, 3] = (three - three_hi.astype(F32)).astype(BF16)

    def folded(sums):
        total = sums[0:32, :TILE]
        for k in range(1, PARTS):
            total = total + (sums[32 * k:32 * k + 32, :TILE] + sums[32 * k - 32:32 * k, TILE:])
        return total

    def sums(coef_ref, u, at):
        mu, pos, pol, mixed, own = site_vectors(x_ref, base_ref[at], origin(at))
        rem = dipole_rows(mu, pos, mixed, own)
        five_hi, five_lo, three_hi, three_lo = [coef_ref[u, k] for k in range(4)]
        square = jnp.concatenate(
            [jnp.concatenate([five_hi, three_hi], 1), jnp.concatenate([five_lo, three_lo], 1)], 0
        )
        h = folded(lax.dot_general(rem, square, nt, preferred_element_type=F32))
        square = jnp.concatenate(
            [jnp.concatenate([five_hi, five_lo], 1), jnp.concatenate([three_hi, three_lo], 1)], 0
        )
        r = folded(jnp.dot(dip_ref[home_of(at)], square, preferred_element_type=F32))
        field = assemble([r[8 * j:8 * j + 8] for j in range(4)], pos, mixed)
        return home_of(at), target_ref[at], h, field

    def half(first, dist_now, dist_next, coef_now, coef_next):
        done = [sums(coef_now, u, first + u) for u in range(UNROLL)]
        for u in range(UNROLL):
            coefficients(dist_now, coef_next, u)
        for u in range(UNROLL):
            distances(dist_next, u, first + 2 * UNROLL + u)
        for home, target, h, field in done:
            acc_ref[home] += h
            out_ref[pl.ds(target, 8, stride=OUT_STRIDE), :] += field

    even = (dist_even, dist_odd, coef_even, coef_odd)
    odd = (dist_odd, dist_even, coef_odd, coef_even)

    def step(i, _):
        for k in range(HALVES):
            half((HALVES * i + k) * UNROLL, *(odd if k % 2 else even))
        return 0

    lax.fori_loop(0, (groups + 1 + HALVES) // HALVES, step, 0)

    sends = []
    for g in range(9):
        for k in range(6):
            source = out_ref.at[pl.ds(g * OUT_ROWS + k * OUT_STRIDE, TILES), :]
            place = outs[g % 3].at[k, g // 3]
            sends.append(pltpu.make_async_copy(source, place, out_sem.at[6 * g + k]))
    for k, send in enumerate(sends):
        if k // 6 != 4:
            send.start()

    def finish(t, _):
        centre = (8.0, 8.0, (4 * t + 2).astype(F32))
        mu, pos, pol, mixed, own = site_vectors(x_ref, own_base + t, centre)
        field = assemble([acc_ref[t, 8 * j:8 * j + 8] for j in range(4)], pos, mixed)
        out_ref[pl.ds(4 * OUT_ROWS + t, 8, stride=OUT_STRIDE), :] += field
        return 0

    lax.fori_loop(0, TILES, finish, 0, unroll=4)
    for send in sends[24:30]:
        send.start()
    for send in sends:
        send.wait()


FAR_AWAY = 2.0 ** 60
LIST = 9 * 2048 + (HALVES + 4) * UNROLL
OUT_STRIDE = TILES + 8
OUT_ROWS = 8 * OUT_STRIDE
UNUSED = 4 * OUT_ROWS + DUMMY


def field_kernel(lists, split, *sites):
    smem = pl.BlockSpec(memory_space=pltpu.SMEM)
    away = pl.BlockSpec(memory_space=pl.ANY)
    return pl.pallas_call(
        kernel,
        out_shape=[jax.ShapeDtypeStruct((6, 3, TILES, TILE), F32)] * 3,
        in_specs=[smem, smem] + [away] * 9,
        out_specs=[away] * 3,
        scratch_shapes=[
            pltpu.VMEM((9 * OUT_ROWS, TILE), F32),
            pltpu.SemaphoreType.DMA((9,)),
            pltpu.SemaphoreType.DMA((54,)),
            pltpu.VMEM((9 * ROWS, TILE), F32),
            pltpu.VMEM((TILES + 1, TILE, 64), BF16),
            pltpu.VMEM((TILES + 1, 32 * PARTS, 2 * TILE), BF16),
            pltpu.VMEM((TILES + 1, 32, TILE), F32),
            pltpu.VMEM((3, TILE, 2 * TILE), BF16),
            pltpu.SMEM((LIST,), jnp.int32),
            pltpu.SMEM((LIST,), jnp.int32),
            pltpu.SMEM((LIST,), jnp.int32),
            pltpu.VMEM((UNROLL, TILE, 2 * TILE), F32),
            pltpu.VMEM((UNROLL, TILE, 2 * TILE), F32),
            pltpu.VMEM((UNROLL, 4, TILE, TILE), BF16),
            pltpu.VMEM((UNROLL, 4, TILE, TILE), BF16),
        ],
        compiler_params=pltpu.CompilerParams(vmem_limit_bytes=63 * 1024 * 1024),
        name="pair_fields",
    )(lists, split, *sites)


CHUNKS = 8
TURNS = 3
AHEAD = 2
EDGE = 8


def halo_kernel(sites_ref, lists_ref, counts_ref, *refs):
    outs, lists_out, split_ref = refs[:8], refs[8], refs[9]
    send_sem, recv_sem, list_send, list_recv, own_sem, *refs = refs[10:]
    nbr_counts, loads, mine, share_send, share_recv = refs
    outs = outs[:4] + (None,) + outs[4:]
    gx, gy = lax.axis_index("gx"), lax.axis_index("gy")
    n_gx, n_gy = lax.axis_size("gx"), lax.axis_size("gy")
    mesh_id = pl.DeviceIdType.MESH
    size = ROWS // CHUNKS

    def device(g):
        return (lax.rem(gx + g // 3 - 1 + n_gx, n_gx), lax.rem(gy + g % 3 - 1 + n_gy, n_gy))

    barrier = pltpu.get_barrier_semaphore()
    others = [g for g in range(9) if g != 4]
    for g in others:
        pl.semaphore_signal(barrier, inc=1, device_id=device(g), device_id_type=mesh_id)
    pl.semaphore_wait(barrier, 8)

    def piece(g, source, target, chunk):
        rows = pl.ds(chunk * size, size)
        return pltpu.make_async_remote_copy(
            src_ref=source.at[rows, :],
            dst_ref=outs[g].at[rows, :],
            send_sem=send_sem.at[g, chunk],
            recv_sem=recv_sem.at[g, chunk],
            device_id=device(target),
            device_id_type=mesh_id,
        )

    shared = []

    def share(turn, source, dest):
        for g in others:
            copy = pltpu.make_async_remote_copy(
                src_ref=source,
                dst_ref=dest.at[g],
                send_sem=share_send.at[turn, g],
                recv_sem=share_recv.at[turn, g],
                device_id=device(8 - g),
                device_id_type=mesh_id,
            )
            copy.start()
            shared.append(copy)

    share(0, counts_ref, nbr_counts)
    straight = {}
    for chunk in range(CHUNKS):
        for g in (1, 7, 3, 5):
            straight[g, chunk] = piece(g, sites_ref, 8 - g, chunk)
    def begin(chunk):
        for g in (1, 7, 3, 5):
            straight[g, chunk].start()

    for chunk in range(AHEAD):
        begin(chunk)
    listed = []
    for g in others:
        listed.append(
            pltpu.make_async_remote_copy(
                src_ref=lists_ref,
                dst_ref=lists_out.at[g],
                send_sem=list_send.at[g],
                recv_sem=list_recv.at[g],
                device_id=device(8 - g),
                device_id_type=mesh_id,
            )
        )
        listed[-1].start()
    own = pltpu.make_async_copy(lists_ref, lists_out.at[4], own_sem)
    own.start()
    first_edge = lax.rem(gy, EDGE) == 0
    last_edge = lax.rem(gy, EDGE) == EDGE - 1
    onward = {
        1: ((~last_edge, 0, 1, 5), (~first_edge, 2, 1, 3)),
        7: ((~last_edge, 6, 7, 5), (~first_edge, 8, 7, 3)),
        3: ((first_edge, 0, 3, 7), (first_edge, 6, 3, 1)),
        5: ((last_edge, 2, 5, 7), (last_edge, 8, 5, 1)),
    }

    def pass_on(g, chunk, action):
        for condition, slot, here, target in onward[g]:

            @pl.when(condition)
            def _(slot=slot, here=here, target=target):
                action(piece(slot, outs[here], target, chunk))

    incoming, outgoing, given, kept = {}, {}, {}, {}

    def balance(turn):
        for copy in shared[8 * turn:8 * turn + 8]:
            copy.wait_recv()
        if turn == 0:
            for g in others:
                given[g] = incoming[g] = nbr_counts[g, 8 - g:9 - g, :]
                kept[g] = outgoing[g] = counts_ref[g:g + 1, :]
        else:
            before = mine[turn - 1, 0:1, :]
            for g in others:
                theirs = loads[turn - 1, g, 0:1, :]
                come = jnp.floor((theirs - before) * (1.0 / 16.0))
                given[g] = jnp.clip(given[g] + come, 0.0, incoming[g])
                leave = jnp.floor((before - theirs) * (1.0 / 16.0))
                kept[g] = jnp.clip(kept[g] + leave, 0.0, outgoing[g])
        if turn < TURNS:
            load = counts_ref[4:5, :]
            for g in others:
                load = load + (outgoing[g] - kept[g]) + given[g]
            mine[turn] = jnp.broadcast_to(load, (8, TILE))
            share(turn + 1, mine.at[turn], loads.at[turn])

    for chunk in range(CHUNKS):
        if chunk <= TURNS:
            balance(chunk)
        for g in (1, 7, 3, 5):
            straight[g, chunk].wait_recv()
            pass_on(g, chunk, lambda copy: copy.start())
        if chunk + AHEAD < CHUNKS:
            begin(chunk + AHEAD)
    for turn in range(CHUNKS, TURNS + 1):
        balance(turn)
    blank = jnp.zeros((1, TILE), F32)
    rows = [given.get(g, blank) for g in range(9)] + [kept.get(g, blank) for g in range(9)]
    split_ref[...] = jnp.concatenate(rows + [blank] * 6, 0).astype(jnp.int32)
    for copy in shared:
        copy.wait_send()
    for chunk in range(CHUNKS):
        for g in (1, 7, 3, 5):
            straight[g, chunk].wait_send()
            pass_on(g, chunk, lambda copy: copy.wait_send())
        for g in (0, 2, 6, 8):
            piece(g, sites_ref, 8 - g, chunk).wait_recv()
    for copy in listed:
        copy.wait()
    own.wait()


def halo_exchange(sites, lists, counts):
    away = pl.BlockSpec(memory_space=pl.ANY)
    shapes = [jax.ShapeDtypeStruct(sites.shape, sites.dtype)] * 8
    shapes.append(jax.ShapeDtypeStruct((9,) + lists.shape, lists.dtype))
    shapes.append(jax.ShapeDtypeStruct((24, TILE), jnp.int32))
    vmem = pl.BlockSpec(memory_space=pltpu.VMEM)
    return pl.pallas_call(
        halo_kernel,
        out_shape=shapes,
        in_specs=[away, away, vmem],
        out_specs=[away] * 9 + [vmem],
        scratch_shapes=[
            pltpu.SemaphoreType.DMA((9, CHUNKS)),
            pltpu.SemaphoreType.DMA((9, CHUNKS)),
            pltpu.SemaphoreType.DMA((9,)),
            pltpu.SemaphoreType.DMA((9,)),
            pltpu.SemaphoreType.DMA,
            pltpu.VMEM((9, 16, TILE), F32),
            pltpu.VMEM((TURNS, 9, 8, TILE), F32),
            pltpu.VMEM((TURNS, 8, TILE), F32),
            pltpu.SemaphoreType.DMA((TURNS + 1, 9)),
            pltpu.SemaphoreType.DMA((TURNS + 1, 9)),
        ],
        compiler_params=pltpu.CompilerParams(collective_id=0, has_side_effects=True),
        name="halo",
    )(sites, lists, counts)


def return_kernel(
    low_ref, mid_ref, high_ref, perm_ref, pol_ref, field_ref, induced_ref,
    column, left, right, up, down, edge_in, edge_own, edge_sum,
    mid_sem, gy_send, gy_recv, gx_send, gx_recv, edge_send, edge_recv, edge_sem,
):
    gx, gy = lax.axis_index("gx"), lax.axis_index("gy")
    n_gx, n_gy = lax.axis_size("gx"), lax.axis_size("gy")
    mesh_id = pl.DeviceIdType.MESH

    def device(row, col):
        return (lax.rem(gx + row + n_gx, n_gx), lax.rem(gy + col + n_gy, n_gy))

    barrier = pltpu.get_barrier_semaphore()
    for row, col in ((-1, 0), (1, 0), (0, -1), (0, 1)):
        pl.semaphore_signal(barrier, inc=1, device_id=device(row, col), device_id_type=mesh_id)
    pl.semaphore_wait(barrier, 4)

    def remote(source, dest, send, recv, way, k, target):
        return pltpu.make_async_remote_copy(
            src_ref=source.at[k],
            dst_ref=dest.at[k],
            send_sem=send.at[way, k],
            recv_sem=recv.at[way, k],
            device_id=target,
            device_id_type=mesh_id,
        )

    edges = (lax.rem(gy, EDGE) == 0, lax.rem(gy, EDGE) == EDGE - 1)
    sources, dests = (low_ref, high_ref), (right, left)
    targets = (device(0, -1), device(0, 1))
    second, own = [], []

    def either(condition, yes, no):
        pl.when(condition)(yes)
        pl.when(jnp.logical_not(condition))(no)

    def whole(way, k):
        return remote(sources[way], dests[way], gy_send, gy_recv, way, k, targets[way])

    def summed(way, k):
        return pltpu.make_async_remote_copy(
            src_ref=edge_sum.at[k],
            dst_ref=dests[way].at[k, 1],
            send_sem=gy_send.at[way, k],
            recv_sem=gy_recv.at[way, k],
            device_id=targets[way],
            device_id_type=mesh_id,
        )

    def along(way, k, slot):
        return pltpu.make_async_remote_copy(
            src_ref=sources[way].at[k, 2 - 2 * slot],
            dst_ref=edge_in.at[slot, k],
            send_sem=edge_send.at[slot, k],
            recv_sem=edge_recv.at[slot, k],
            device_id=device(1 - 2 * slot, 0),
            device_id_type=mesh_id,
        )

    def centre(way, k):
        return pltpu.make_async_copy(sources[way].at[k, 1], edge_own.at[k], edge_sem.at[k])

    for k in range(6):
        for way in range(2):

            def start_edge(way=way, k=k):
                along(way, k, 0).start()
                along(way, k, 1).start()
                centre(way, k).start()

            either(edges[way], start_edge, lambda way=way, k=k: whole(way, k).start())
        own.append(pltpu.make_async_copy(mid_ref.at[k], column.at[k], mid_sem.at[k]))
        own[k].start()

    for way in range(2):

        @pl.when(edges[1 - way])
        def _(way=way):
            for k in range(6):
                for row in (0, 2):
                    dests[way][k, row] = jnp.zeros((TILES, TILE), F32)

    def edge_stage(k):
        for way in range(2):

            @pl.when(edges[way])
            def _(way=way):
                centre(way, k).wait()
                along(way, k, 0).wait_recv()
                along(way, k, 1).wait_recv()
                edge_sum[k] = edge_own[k] + edge_in[0, k] + edge_in[1, k]
                summed(way, k).start()

    def finish(k):
        for copy in second[k]:
            copy.wait_recv()
        total = column[k, 1] + up[k] + down[k]
        field_ref[k] = total
        induced_ref[k] = pol_ref[...] * (perm_ref[k] + total)

    edge_stage(0)
    edge_stage(1)
    for k in range(6):
        own[k].wait()
        for way in range(2):
            either(
                edges[1 - way],
                lambda way=way: summed(way, k).wait_recv(),
                lambda way=way: whole(way, k).wait_recv(),
            )
        column[k] = column[k] + left[k] + right[k]
        second.append(
            (
                remote(column.at[:, 0], down, gx_send, gx_recv, 0, k, device(-1, 0)),
                remote(column.at[:, 2], up, gx_send, gx_recv, 1, k, device(1, 0)),
            )
        )
        for copy in second[k]:
            copy.start()
        if k + 2 < 6:
            edge_stage(k + 2)
        if k >= 2:
            finish(k - 2)
    finish(4)
    finish(5)
    for k in range(6):
        for way in range(2):

            def end_edge(way=way, k=k):
                along(way, k, 0).wait_send()
                along(way, k, 1).wait_send()
                summed(way, k).wait_send()

            either(edges[way], end_edge, lambda way=way, k=k: whole(way, k).wait_send())
        for copy in second[k]:
            copy.wait_send()


def return_terms(low, mid, high, perm, pol):
    away = pl.BlockSpec(memory_space=pl.ANY)
    vmem = pl.BlockSpec(memory_space=pltpu.VMEM)
    return pl.pallas_call(
        return_kernel,
        out_shape=[jax.ShapeDtypeStruct((6, TILES, TILE), F32)] * 2,
        in_specs=[away] * 3 + [vmem] * 2,
        out_specs=[vmem] * 2,
        scratch_shapes=[
            pltpu.VMEM((6, 3, TILES, TILE), F32),
            pltpu.VMEM((6, 3, TILES, TILE), F32),
            pltpu.VMEM((6, 3, TILES, TILE), F32),
            pltpu.VMEM((6, TILES, TILE), F32),
            pltpu.VMEM((6, TILES, TILE), F32),
            pltpu.VMEM((2, 6, TILES, TILE), F32),
            pltpu.VMEM((6, TILES, TILE), F32),
            pltpu.VMEM((6, TILES, TILE), F32),
            pltpu.SemaphoreType.DMA((6,)),
            pltpu.SemaphoreType.DMA((2, 6)),
            pltpu.SemaphoreType.DMA((2, 6)),
            pltpu.SemaphoreType.DMA((2, 6)),
            pltpu.SemaphoreType.DMA((2, 6)),
            pltpu.SemaphoreType.DMA((2, 6)),
            pltpu.SemaphoreType.DMA((2, 6)),
            pltpu.SemaphoreType.DMA((6,)),
        ],
        compiler_params=pltpu.CompilerParams(
            collective_id=1, has_side_effects=True, vmem_limit_bytes=63 * 1024 * 1024
        ),
        name="return_terms",
    )(low, mid, high, perm, pol)


def local(positions, polarity, dipoles, perm_fields, pair_list, tile_counts):
    slot_total = pair_list.shape[3]
    sites = jnp.concatenate([dipoles, positions, polarity[None]], 0).reshape(10 * TILES, TILE)

    table = pair_list.reshape(2, slot_total)
    live = jnp.arange(slot_total, dtype=jnp.int32) < tile_counts.reshape(())
    far = jnp.where(live, table[1], 16 * TILES)
    far, near = lax.sort((far, table[0]), num_keys=1)
    bounds = jnp.arange(slot_total, dtype=jnp.int32)[:16] * TILES
    bounds = jnp.sum((far[None, :] < bounds[:, None]).astype(jnp.int32), 1)
    counts = (bounds[1:10] - bounds[:9]).astype(F32)
    counts = jnp.broadcast_to(jnp.pad(counts, (0, 7))[:, None], (16, TILE))
    bounds = jnp.concatenate([bounds, jnp.zeros((slot_total - 16,), jnp.int32)])
    lists = jnp.stack([far, near, bounds])
    *around_sites, lists, split = halo_exchange(sites, lists, counts)
    low, mid, high = field_kernel(
        lists.reshape(27, slot_total), split, *around_sites[:4], sites, *around_sites[4:]
    )
    perm = perm_fields.reshape(6, TILES, TILE)
    field, induced = return_terms(low, mid, high, perm, polarity.reshape(TILES, TILE))
    field = field.reshape(6, 1, 1, TILES * TILE)
    induced = induced.reshape(6, 1, 1, TILES * TILE)
    return (field, induced)


def solution(mesh):
    placed = (
        P(None, "gx", "gy", None),
        P("gx", "gy", None),
        P(None, "gx", "gy", None),
        P(None, "gx", "gy", None),
        P("gx", "gy", None, None),
        P("gx", "gy"),
    )
    return jax.shard_map(
        local,
        mesh=mesh,
        in_specs=placed,
        out_specs=(P(None, "gx", "gy", None), P(None, "gx", "gy", None)),
        check_vma=False,
    )
```

```python
import jax
import jax.numpy as jnp
from jax import lax
from jax.experimental import pallas as pl
from jax.experimental.pallas import tpu as pltpu
from jax.sharding import PartitionSpec as P

TILE = 128
TILES = 256
ROWS = 10 * TILES
UNROLL = 2
HALVES = 6
PARTS = 3
DUMMY = TILES
GRID = 2 * TILES

thole = 0.39
domain_edge = 16.0

F32 = jnp.float32
BF16 = jnp.bfloat16


def three_parts(value):
    high = value.astype(BF16)
    rest = value - high.astype(F32)
    middle = rest.astype(BF16)
    low = (rest - middle.astype(F32)).astype(BF16)
    return high, middle, low


def rows_of():
    sub = lax.broadcasted_iota(jnp.int32, (8, TILE), 0)
    second = (sub == 3) | (sub == 4) | (sub == 5) | (sub == 7)
    is_x = (sub == 0) | (sub == 3)
    is_y = (sub == 1) | (sub == 4)
    is_z = (sub == 2) | (sub == 5)
    return sub, second, is_x, is_y, is_z


def load_row(ref, row):
    return jnp.broadcast_to(ref[pl.ds(row, 1), :], (8, TILE))


def site_vectors(ref, base, centre):
    sub, second, is_x, is_y, is_z = rows_of()
    dips = [load_row(ref, base + k * TILES) for k in range(6)]
    pos = [load_row(ref, base + (6 + k) * TILES) - centre[k] for k in range(3)]
    pol = load_row(ref, base + 9 * TILES)
    mu = [jnp.where(second, dips[3 + j], dips[j]) for j in range(3)]
    mixed = jnp.where(is_x, pos[0], jnp.where(is_y, pos[1], jnp.where(is_z, pos[2], 1.0)))
    own = jnp.where(is_x, mu[0], jnp.where(is_y, mu[1], jnp.where(is_z, mu[2], 0.0)))
    return mu, pos, pol, mixed, own


def dipole_rows(mu, pos, mixed, own):
    dots = pos[0] * mu[0] + pos[1] * mu[1] + pos[2] * mu[2]
    tripled = 3.0 * mixed
    left = jnp.concatenate([tripled * mu[0], tripled * mu[1], tripled * mu[2], tripled * dots], 0)
    blank = jnp.zeros((16, TILE), BF16)
    right = jnp.concatenate([jnp.zeros((8, TILE), F32), -own], 0)
    out = []
    for l, r in zip(three_parts(left), three_parts(right)):
        out.append(jnp.concatenate([l, jnp.concatenate([blank, r], 0)], 1))
    return jnp.concatenate(out[:PARTS], 0)


def geometry_rows(first_three, fourth, fifth):
    sub = lax.broadcasted_iota(jnp.int32, (8, TILE), 0)
    rows = jnp.where(sub == 0, first_three[0], jnp.where(sub == 1, first_three[1], jnp.where(sub == 2, first_three[2], jnp.where(sub == 3, fourth, jnp.where(sub == 4, fifth, 0.0)))))
    return tuple(p.astype(F32) for p in three_parts(rows))


def scale_rows(scale, pattern):
    sub = lax.broadcasted_iota(jnp.int32, (8, TILE), 0)
    parts = [p.astype(F32) for p in three_parts(scale)]
    out = jnp.zeros((8, TILE), F32)
    for row, part in enumerate(pattern):
        out = jnp.where(sub == row, parts[part], out)
    return out


def squared(pos):
    return pos[0] * pos[0] + pos[1] * pos[1] + pos[2] * pos[2]


def assemble(parts, pos, mixed):
    sub, second, _, _, _ = rows_of()
    g = pos[0] * parts[0] + pos[1] * parts[1] + pos[2] * parts[2] - parts[3]
    s0 = jnp.broadcast_to(g[6:7], (8, TILE))
    s1 = jnp.broadcast_to(g[7:8], (8, TILE))
    s = jnp.where(second, s1, s0)
    return mixed * s - g


def kernel(
    lists_ref, split_ref, *refs
):
    sources, refs = refs[:9], refs[9:]
    outs, refs = refs[:3], refs[3:]
    (
    out_ref, copy_sem, out_sem, x_ref, geo_ref, dip_ref, acc_ref, eye_ref, near_ref, base_ref, target_ref, dist_even, dist_odd, coef_even, coef_odd,
    ) = refs
    eye = (
        lax.broadcasted_iota(jnp.int32, (TILE, TILE), 0) == lax.broadcasted_iota(jnp.int32, (TILE, TILE), 1)
    )
    eye16 = jnp.where(eye, 1.0, 0.0).astype(BF16)
    zero8 = jnp.zeros((8, TILE), F32)
    own_base = 4 * ROWS
    copies = []
    for g, source in enumerate(sources):
        place = x_ref.at[pl.ds(g * ROWS, ROWS), :]
        copies.append(pltpu.make_async_copy(source, place, copy_sem.at[g]))
        copies[-1].start()
    nt = (((1,), (1,)), ((), ()))
    eye_ref[0] = jnp.zeros((TILE, 2 * TILE), BF16)
    eye_ref[1] = jnp.concatenate(
        [jnp.where(eye, FAR_AWAY, 0.0).astype(BF16), jnp.zeros((TILE, TILE), BF16)], 1
    )

    eye_ref[2] = jnp.concatenate([eye16, eye16], 1)

    def clear(i, _):
        out_ref[pl.ds(pl.multiple_of(i * 64, 64), 64), :] = jnp.zeros((64, TILE), F32)
        return 0

    lax.fori_loop(0, out_ref.shape[0] // 64, clear, 0)
    copies[4].wait()

    def prepare(t, _):
        centre = (8.0, 8.0, (4 * t + 2).astype(F32))
        mu, pos, pol, mixed, own = site_vectors(x_ref, own_base + t, centre)
        dip_ref[t] = dipole_rows(mu, pos, mixed, own)
        hi, mid, lo = geometry_rows([-2.0 * p for p in pos], 1.0, squared(pos))
        scale = (-thole) * lax.rsqrt(pol)
        q = scale_rows(scale, (0, 1, 0, 1, 0, 2))
        stack = jnp.concatenate([hi, mid, hi, mid, hi, lo, q, zero8], 0).astype(BF16)
        moved = lax.dot_general(eye16, stack, nt, preferred_element_type=F32).astype(BF16)
        geo_ref[t] = moved
        acc_ref[t] = jnp.zeros((32, TILE), F32)
        return 0

    lax.fori_loop(0, TILES, prepare, 0, unroll=4)
    for g in range(9):
        if g != 4:
            copies[g].wait()
    geo_ref[DUMMY] = geo_ref[0]
    dip_ref[DUMMY] = dip_ref[0]

    def blank(at):
        near_ref[at] = DUMMY + 4 * GRID
        base_ref[at] = own_base
        target_ref[at] = UNUSED

    for k in range(2 * UNROLL):
        blank(k)
    total = jnp.int32(2 * UNROLL)
    def put(at, home, remote, g):
        target = remote + g * OUT_ROWS
        if g == 4:
            target = jnp.where(remote == home, UNUSED, target)
        near_ref[at] = home + g * GRID
        base_ref[at] = remote + g * ROWS
        target_ref[at] = target
        return at + 1

    for g in range(9):
        first = lists_ref[3 * g + 2, 8 - g]
        last = lists_ref[3 * g + 2, 9 - g]
        if g != 4:
            last = first + split_ref[g, 0]

        def incoming(p, at, g=g):
            return put(at, lists_ref[3 * g, p] & (TILES - 1), lists_ref[3 * g + 1, p], g)

        total = lax.fori_loop(first, last, incoming, total)
        if g != 4:
            first = lists_ref[14, g] + split_ref[9 + g, 0]
            last = lists_ref[14, g + 1]

            def kept(p, at, g=g):
                return put(at, lists_ref[13, p], lists_ref[12, p] & (TILES - 1), g)

            total = lax.fori_loop(first, last, kept, total)
    for k in range((HALVES + 2) * UNROLL):
        blank(total + k)
    groups = (total - 2 * UNROLL + UNROLL - 1) // UNROLL

    def home_of(at):
        return near_ref[at] & (GRID - 1)

    def origin(at):
        grid = near_ref[at] // GRID
        row = (grid * 11) // 32
        column = grid - 3 * row
        return (
            24.0 - domain_edge * row.astype(F32),
            24.0 - domain_edge * column.astype(F32),
            (4 * home_of(at) + 2).astype(F32),
        )

    def distances(dist_ref, u, at):
        base = base_ref[at]
        pos = [load_row(x_ref, base + (6 + k) * TILES) - c for k, c in enumerate(origin(at))]
        pol = load_row(x_ref, base + 9 * TILES)
        hi, mid, lo = geometry_rows(pos, squared(pos), 1.0)
        q = scale_rows(lax.rsqrt(pol), (0, 0, 1, 1, 2, 0))
        left = jnp.concatenate([hi, hi, mid, mid, lo, hi, zero8, zero8], 0).astype(BF16)
        right = jnp.concatenate([jnp.zeros((48, TILE), F32), q, zero8], 0).astype(BF16)
        same = (target_ref[at] == UNUSED).astype(jnp.int32)
        operand = jnp.concatenate([eye_ref[same], jnp.concatenate([left, right], 1)], 0)
        rows = jnp.concatenate([eye_ref[2, :, :TILE], geo_ref[home_of(at)]], 1)
        dist_ref[u] = jnp.dot(rows, operand, preferred_element_type=F32)

    def coefficients(dist_ref, coef_ref, u):
        dist_sq = dist_ref[u, :, :TILE]
        inv = lax.rsqrt(dist_sq)
        inv_sq = inv * inv
        inv_cube = inv_sq * inv
        cube = dist_sq * inv * dist_sq
        damp = cube * dist_ref[u, :, TILE:]
        decay = jnp.exp(damp)
        lam_three = 1.0 - decay
        lam_five = lam_three + damp * decay
        three = lam_three * inv_cube
        five = lam_five * inv_cube * inv_sq
        three_hi = three.astype(BF16)
        five_hi = five.astype(BF16)
        coef_ref[u, 0] = five_hi
        coef_ref[u, 1] = (five - five_hi.astype(F32)).astype(BF16)
        coef_ref[u, 2] = three_hi
        coef_ref[u, 3] = (three - three_hi.astype(F32)).astype(BF16)

    def folded(sums):
        total = sums[0:32, :TILE]
        for k in range(1, PARTS):
            total = total + (sums[32 * k:32 * k + 32, :TILE] + sums[32 * k - 32:32 * k, TILE:])
        return total

    def sums(coef_ref, u, at):
        mu, pos, pol, mixed, own = site_vectors(x_ref, base_ref[at], origin(at))
        rem = dipole_rows(mu, pos, mixed, own)
        five_hi, five_lo, three_hi, three_lo = [coef_ref[u, k] for k in range(4)]
        square = jnp.concatenate(
            [jnp.concatenate([five_hi, three_hi], 1), jnp.concatenate([five_lo, three_lo], 1)], 0
        )
        h = folded(lax.dot_general(rem, square, nt, preferred_element_type=F32))
        square = jnp.concatenate(
            [jnp.concatenate([five_hi, five_lo], 1), jnp.concatenate([three_hi, three_lo], 1)], 0
        )
        r = folded(jnp.dot(dip_ref[home_of(at)], square, preferred_element_type=F32))
        field = assemble([r[8 * j:8 * j + 8] for j in range(4)], pos, mixed)
        return home_of(at), target_ref[at], h, field

    def half(first, dist_now, dist_next, coef_now, coef_next):
        done = [sums(coef_now, u, first + u) for u in range(UNROLL)]
        for u in range(UNROLL):
            coefficients(dist_now, coef_next, u)
        for u in range(UNROLL):
            distances(dist_next, u, first + 2 * UNROLL + u)
        for home, target, h, field in done:
            acc_ref[home] += h
            out_ref[pl.ds(target, 8, stride=OUT_STRIDE), :] += field

    even = (dist_even, dist_odd, coef_even, coef_odd)
    odd = (dist_odd, dist_even, coef_odd, coef_even)

    def step(i, _):
        for k in range(HALVES):
            half((HALVES * i + k) * UNROLL, *(odd if k % 2 else even))
        return 0

    lax.fori_loop(0, (groups + 1 + HALVES) // HALVES, step, 0)

    sends = []
    for g in range(9):
        for k in range(6):
            source = out_ref.at[pl.ds(g * OUT_ROWS + k * OUT_STRIDE, TILES), :]
            place = outs[g % 3].at[k, g // 3]
            sends.append(pltpu.make_async_copy(source, place, out_sem.at[6 * g + k]))
    for k, send in enumerate(sends):
        if k // 6 != 4:
            send.start()

    def finish(t, _):
        centre = (8.0, 8.0, (4 * t + 2).astype(F32))
        mu, pos, pol, mixed, own = site_vectors(x_ref, own_base + t, centre)
        field = assemble([acc_ref[t, 8 * j:8 * j + 8] for j in range(4)], pos, mixed)
        out_ref[pl.ds(4 * OUT_ROWS + t, 8, stride=OUT_STRIDE), :] += field
        return 0

    lax.fori_loop(0, TILES, finish, 0, unroll=4)
    for send in sends[24:30]:
        send.start()
    for send in sends:
        send.wait()


FAR_AWAY = 2.0 ** 60
LIST = 9 * 2048 + (HALVES + 4) * UNROLL
OUT_STRIDE = TILES + 8
OUT_ROWS = 8 * OUT_STRIDE
UNUSED = 4 * OUT_ROWS + DUMMY


def field_kernel(lists, split, *sites):
    smem = pl.BlockSpec(memory_space=pltpu.SMEM)
    away = pl.BlockSpec(memory_space=pl.ANY)
    return pl.pallas_call(
        kernel,
        out_shape=[jax.ShapeDtypeStruct((6, 3, TILES, TILE), F32)] * 3,
        in_specs=[smem, smem] + [away] * 9,
        out_specs=[away] * 3,
        scratch_shapes=[
            pltpu.VMEM((9 * OUT_ROWS, TILE), F32),
            pltpu.SemaphoreType.DMA((9,)),
            pltpu.SemaphoreType.DMA((54,)),
            pltpu.VMEM((9 * ROWS, TILE), F32),
            pltpu.VMEM((TILES + 1, TILE, 64), BF16),
            pltpu.VMEM((TILES + 1, 32 * PARTS, 2 * TILE), BF16),
            pltpu.VMEM((TILES + 1, 32, TILE), F32),
            pltpu.VMEM((3, TILE, 2 * TILE), BF16),
            pltpu.SMEM((LIST,), jnp.int32),
            pltpu.SMEM((LIST,), jnp.int32),
            pltpu.SMEM((LIST,), jnp.int32),
            pltpu.VMEM((UNROLL, TILE, 2 * TILE), F32),
            pltpu.VMEM((UNROLL, TILE, 2 * TILE), F32),
            pltpu.VMEM((UNROLL, 4, TILE, TILE), BF16),
            pltpu.VMEM((UNROLL, 4, TILE, TILE), BF16),
        ],
        compiler_params=pltpu.CompilerParams(vmem_limit_bytes=63 * 1024 * 1024),
        name="pair_fields",
    )(lists, split, *sites)


CHUNKS = 8
TURNS = 2
AHEAD = 4
EDGE = 8


def halo_kernel(sites_ref, lists_ref, counts_ref, *refs):
    outs, lists_out, split_ref = refs[:8], refs[8], refs[9]
    send_sem, recv_sem, list_send, list_recv, own_sem, *refs = refs[10:]
    nbr_counts, loads, mine, share_send, share_recv = refs
    outs = outs[:4] + (None,) + outs[4:]
    gx, gy = lax.axis_index("gx"), lax.axis_index("gy")
    n_gx, n_gy = lax.axis_size("gx"), lax.axis_size("gy")
    mesh_id = pl.DeviceIdType.MESH
    size = ROWS // CHUNKS

    def device(g):
        return (lax.rem(gx + g // 3 - 1 + n_gx, n_gx), lax.rem(gy + g % 3 - 1 + n_gy, n_gy))

    barrier = pltpu.get_barrier_semaphore()
    others = [g for g in range(9) if g != 4]
    for g in others:
        pl.semaphore_signal(barrier, inc=1, device_id=device(g), device_id_type=mesh_id)
    pl.semaphore_wait(barrier, 8)

    def piece(g, source, target, chunk):
        rows = pl.ds(chunk * size, size)
        return pltpu.make_async_remote_copy(
            src_ref=source.at[rows, :],
            dst_ref=outs[g].at[rows, :],
            send_sem=send_sem.at[g, chunk],
            recv_sem=recv_sem.at[g, chunk],
            device_id=device(target),
            device_id_type=mesh_id,
        )

    shared = []

    def share(turn, source, dest):
        for g in others:
            copy = pltpu.make_async_remote_copy(
                src_ref=source,
                dst_ref=dest.at[g],
                send_sem=share_send.at[turn, g],
                recv_sem=share_recv.at[turn, g],
                device_id=device(8 - g),
                device_id_type=mesh_id,
            )
            copy.start()
            shared.append(copy)

    share(0, counts_ref, nbr_counts)
    straight = {}
    for chunk in range(CHUNKS):
        for g in (1, 7, 3, 5):
            straight[g, chunk] = piece(g, sites_ref, 8 - g, chunk)
    def begin(chunk):
        for g in (1, 7, 3, 5):
            straight[g, chunk].start()

    for chunk in range(AHEAD):
        begin(chunk)
    listed = []
    for g in others:
        listed.append(
            pltpu.make_async_remote_copy(
                src_ref=lists_ref,
                dst_ref=lists_out.at[g],
                send_sem=list_send.at[g],
                recv_sem=list_recv.at[g],
                device_id=device(8 - g),
                device_id_type=mesh_id,
            )
        )
        listed[-1].start()
    own = pltpu.make_async_copy(lists_ref, lists_out.at[4], own_sem)
    own.start()
    first_edge = lax.rem(gy, EDGE) == 0
    last_edge = lax.rem(gy, EDGE) == EDGE - 1
    onward = {
        1: ((~last_edge, 0, 1, 5), (~first_edge, 2, 1, 3)),
        7: ((~last_edge, 6, 7, 5), (~first_edge, 8, 7, 3)),
        3: ((first_edge, 0, 3, 7), (first_edge, 6, 3, 1)),
        5: ((last_edge, 2, 5, 7), (last_edge, 8, 5, 1)),
    }

    def pass_on(g, chunk, action):
        for condition, slot, here, target in onward[g]:

            @pl.when(condition)
            def _(slot=slot, here=here, target=target):
                action(piece(slot, outs[here], target, chunk))

    incoming, outgoing, given, kept = {}, {}, {}, {}

    def balance(turn):
        for copy in shared[8 * turn:8 * turn + 8]:
            copy.wait_recv()
        if turn == 0:
            for g in others:
                given[g] = incoming[g] = nbr_counts[g, 8 - g:9 - g, :]
                kept[g] = outgoing[g] = counts_ref[g:g + 1, :]
        else:
            before = mine[turn - 1, 0:1, :]
            for g in others:
                theirs = loads[turn - 1, g, 0:1, :]
                come = jnp.floor((theirs - before) * (1.0 / 16.0))
                given[g] = jnp.clip(given[g] + come, 0.0, incoming[g])
                leave = jnp.floor((before - theirs) * (1.0 / 16.0))
                kept[g] = jnp.clip(kept[g] + leave, 0.0, outgoing[g])
        if turn < TURNS:
            load = counts_ref[4:5, :]
            for g in others:
                load = load + (outgoing[g] - kept[g]) + given[g]
            mine[turn] = jnp.broadcast_to(load, (8, TILE))
            share(turn + 1, mine.at[turn], loads.at[turn])

    for chunk in range(CHUNKS):
        if chunk <= TURNS:
            balance(chunk)
        for g in (1, 7, 3, 5):
            straight[g, chunk].wait_recv()
            pass_on(g, chunk, lambda copy: copy.start())
        if chunk + AHEAD < CHUNKS:
            begin(chunk + AHEAD)
    for turn in range(CHUNKS, TURNS + 1):
        balance(turn)
    blank = jnp.zeros((1, TILE), F32)
    rows = [given.get(g, blank) for g in range(9)] + [kept.get(g, blank) for g in range(9)]
    split_ref[...] = jnp.concatenate(rows + [blank] * 6, 0).astype(jnp.int32)
    for copy in shared:
        copy.wait_send()
    for chunk in range(CHUNKS):
        for g in (1, 7, 3, 5):
            straight[g, chunk].wait_send()
            pass_on(g, chunk, lambda copy: copy.wait_send())
        for g in (0, 2, 6, 8):
            piece(g, sites_ref, 8 - g, chunk).wait_recv()
    for copy in listed:
        copy.wait()
    own.wait()


def halo_exchange(sites, lists, counts):
    away = pl.BlockSpec(memory_space=pl.ANY)
    shapes = [jax.ShapeDtypeStruct(sites.shape, sites.dtype)] * 8
    shapes.append(jax.ShapeDtypeStruct((9,) + lists.shape, lists.dtype))
    shapes.append(jax.ShapeDtypeStruct((24, TILE), jnp.int32))
    vmem = pl.BlockSpec(memory_space=pltpu.VMEM)
    return pl.pallas_call(
        halo_kernel,
        out_shape=shapes,
        in_specs=[away, away, vmem],
        out_specs=[away] * 9 + [vmem],
        scratch_shapes=[
            pltpu.SemaphoreType.DMA((9, CHUNKS)),
            pltpu.SemaphoreType.DMA((9, CHUNKS)),
            pltpu.SemaphoreType.DMA((9,)),
            pltpu.SemaphoreType.DMA((9,)),
            pltpu.SemaphoreType.DMA,
            pltpu.VMEM((9, 16, TILE), F32),
            pltpu.VMEM((TURNS, 9, 8, TILE), F32),
            pltpu.VMEM((TURNS, 8, TILE), F32),
            pltpu.SemaphoreType.DMA((TURNS + 1, 9)),
            pltpu.SemaphoreType.DMA((TURNS + 1, 9)),
        ],
        compiler_params=pltpu.CompilerParams(collective_id=0, has_side_effects=True),
        name="halo",
    )(sites, lists, counts)


def return_kernel(
    low_ref, mid_ref, high_ref, perm_ref, pol_ref, field_ref, induced_ref,
    column, left, right, up, down, edge_in, edge_own, edge_sum,
    mid_sem, gy_send, gy_recv, gx_send, gx_recv, edge_send, edge_recv, edge_sem,
):
    gx, gy = lax.axis_index("gx"), lax.axis_index("gy")
    n_gx, n_gy = lax.axis_size("gx"), lax.axis_size("gy")
    mesh_id = pl.DeviceIdType.MESH

    def device(row, col):
        return (lax.rem(gx + row + n_gx, n_gx), lax.rem(gy + col + n_gy, n_gy))

    barrier = pltpu.get_barrier_semaphore()
    for row, col in ((-1, 0), (1, 0), (0, -1), (0, 1)):
        pl.semaphore_signal(barrier, inc=1, device_id=device(row, col), device_id_type=mesh_id)
    pl.semaphore_wait(barrier, 4)

    def remote(source, dest, send, recv, way, k, target):
        return pltpu.make_async_remote_copy(
            src_ref=source.at[k],
            dst_ref=dest.at[k],
            send_sem=send.at[way, k],
            recv_sem=recv.at[way, k],
            device_id=target,
            device_id_type=mesh_id,
        )

    edges = (lax.rem(gy, EDGE) == 0, lax.rem(gy, EDGE) == EDGE - 1)
    sources, dests = (low_ref, high_ref), (right, left)
    targets = (device(0, -1), device(0, 1))
    second, own = [], []

    def either(condition, yes, no):
        pl.when(condition)(yes)
        pl.when(jnp.logical_not(condition))(no)

    def whole(way, k):
        return remote(sources[way], dests[way], gy_send, gy_recv, way, k, targets[way])

    def summed(way, k):
        return pltpu.make_async_remote_copy(
            src_ref=edge_sum.at[k],
            dst_ref=dests[way].at[k, 1],
            send_sem=gy_send.at[way, k],
            recv_sem=gy_recv.at[way, k],
            device_id=targets[way],
            device_id_type=mesh_id,
        )

    def along(way, k, slot):
        return pltpu.make_async_remote_copy(
            src_ref=sources[way].at[k, 2 - 2 * slot],
            dst_ref=edge_in.at[slot, k],
            send_sem=edge_send.at[slot, k],
            recv_sem=edge_recv.at[slot, k],
            device_id=device(1 - 2 * slot, 0),
            device_id_type=mesh_id,
        )

    def centre(way, k):
        return pltpu.make_async_copy(sources[way].at[k, 1], edge_own.at[k], edge_sem.at[k])

    for k in range(6):
        for way in range(2):

            def start_edge(way=way, k=k):
                along(way, k, 0).start()
                along(way, k, 1).start()
                centre(way, k).start()

            either(edges[way], start_edge, lambda way=way, k=k: whole(way, k).start())
        own.append(pltpu.make_async_copy(mid_ref.at[k], column.at[k], mid_sem.at[k]))
        own[k].start()

    for way in range(2):

        @pl.when(edges[1 - way])
        def _(way=way):
            for k in range(6):
                for row in (0, 2):
                    dests[way][k, row] = jnp.zeros((TILES, TILE), F32)

    def edge_stage(k):
        for way in range(2):

            @pl.when(edges[way])
            def _(way=way):
                centre(way, k).wait()
                along(way, k, 0).wait_recv()
                along(way, k, 1).wait_recv()
                edge_sum[k] = edge_own[k] + edge_in[0, k] + edge_in[1, k]
                summed(way, k).start()

    def finish(k):
        for copy in second[k]:
            copy.wait_recv()
        total = column[k, 1] + up[k] + down[k]
        field_ref[k] = total
        induced_ref[k] = pol_ref[...] * (perm_ref[k] + total)

    edge_stage(0)
    edge_stage(1)
    for k in range(6):
        own[k].wait()
        for way in range(2):
            either(
                edges[1 - way],
                lambda way=way: summed(way, k).wait_recv(),
                lambda way=way: whole(way, k).wait_recv(),
            )
        column[k] = column[k] + left[k] + right[k]
        second.append(
            (
                remote(column.at[:, 0], down, gx_send, gx_recv, 0, k, device(-1, 0)),
                remote(column.at[:, 2], up, gx_send, gx_recv, 1, k, device(1, 0)),
            )
        )
        for copy in second[k]:
            copy.start()
        if k + 2 < 6:
            edge_stage(k + 2)
        if k >= 2:
            finish(k - 2)
    finish(4)
    finish(5)
    for k in range(6):
        for way in range(2):

            def end_edge(way=way, k=k):
                along(way, k, 0).wait_send()
                along(way, k, 1).wait_send()
                summed(way, k).wait_send()

            either(edges[way], end_edge, lambda way=way, k=k: whole(way, k).wait_send())
        for copy in second[k]:
            copy.wait_send()


def return_terms(low, mid, high, perm, pol):
    away = pl.BlockSpec(memory_space=pl.ANY)
    vmem = pl.BlockSpec(memory_space=pltpu.VMEM)
    return pl.pallas_call(
        return_kernel,
        out_shape=[jax.ShapeDtypeStruct((6, TILES, TILE), F32)] * 2,
        in_specs=[away] * 3 + [vmem] * 2,
        out_specs=[vmem] * 2,
        scratch_shapes=[
            pltpu.VMEM((6, 3, TILES, TILE), F32),
            pltpu.VMEM((6, 3, TILES, TILE), F32),
            pltpu.VMEM((6, 3, TILES, TILE), F32),
            pltpu.VMEM((6, TILES, TILE), F32),
            pltpu.VMEM((6, TILES, TILE), F32),
            pltpu.VMEM((2, 6, TILES, TILE), F32),
            pltpu.VMEM((6, TILES, TILE), F32),
            pltpu.VMEM((6, TILES, TILE), F32),
            pltpu.SemaphoreType.DMA((6,)),
            pltpu.SemaphoreType.DMA((2, 6)),
            pltpu.SemaphoreType.DMA((2, 6)),
            pltpu.SemaphoreType.DMA((2, 6)),
            pltpu.SemaphoreType.DMA((2, 6)),
            pltpu.SemaphoreType.DMA((2, 6)),
            pltpu.SemaphoreType.DMA((2, 6)),
            pltpu.SemaphoreType.DMA((6,)),
        ],
        compiler_params=pltpu.CompilerParams(
            collective_id=1, has_side_effects=True, vmem_limit_bytes=63 * 1024 * 1024
        ),
        name="return_terms",
    )(low, mid, high, perm, pol)


def local(positions, polarity, dipoles, perm_fields, pair_list, tile_counts):
    slot_total = pair_list.shape[3]
    sites = jnp.concatenate([dipoles, positions, polarity[None]], 0).reshape(10 * TILES, TILE)

    table = pair_list.reshape(2, slot_total)
    live = jnp.arange(slot_total, dtype=jnp.int32) < tile_counts.reshape(())
    far = jnp.where(live, table[1], 16 * TILES)
    far, near = lax.sort((far, table[0]), num_keys=1)
    bounds = jnp.arange(slot_total, dtype=jnp.int32)[:16] * TILES
    bounds = jnp.sum((far[None, :] < bounds[:, None]).astype(jnp.int32), 1)
    counts = (bounds[1:10] - bounds[:9]).astype(F32)
    counts = jnp.broadcast_to(jnp.pad(counts, (0, 7))[:, None], (16, TILE))
    bounds = jnp.concatenate([bounds, jnp.zeros((slot_total - 16,), jnp.int32)])
    lists = jnp.stack([far, near, bounds])
    *around_sites, lists, split = halo_exchange(sites, lists, counts)
    low, mid, high = field_kernel(
        lists.reshape(27, slot_total), split, *around_sites[:4], sites, *around_sites[4:]
    )
    perm = perm_fields.reshape(6, TILES, TILE)
    field, induced = return_terms(low, mid, high, perm, polarity.reshape(TILES, TILE))
    field = field.reshape(6, 1, 1, TILES * TILE)
    induced = induced.reshape(6, 1, 1, TILES * TILE)
    return (field, induced)


def solution(mesh):
    placed = (
        P(None, "gx", "gy", None),
        P("gx", "gy", None),
        P(None, "gx", "gy", None),
        P(None, "gx", "gy", None),
        P("gx", "gy", None, None),
        P("gx", "gy"),
    )
    return jax.shard_map(
        local,
        mesh=mesh,
        in_specs=placed,
        out_specs=(P(None, "gx", "gy", None), P(None, "gx", "gy", None)),
        check_vma=False,
    )
```

```python
import jax
import jax.numpy as jnp
from jax import lax
from jax.experimental import pallas as pl
from jax.experimental.pallas import tpu as pltpu
from jax.sharding import PartitionSpec as P

TILE = 128
TILES = 256
ROWS = 10 * TILES
UNROLL = 2
HALVES = 6
PARTS = 3
DUMMY = TILES
GRID = 2 * TILES

thole = 0.39
domain_edge = 16.0

F32 = jnp.float32
BF16 = jnp.bfloat16


def three_parts(value):
    high = value.astype(BF16)
    rest = value - high.astype(F32)
    middle = rest.astype(BF16)
    low = (rest - middle.astype(F32)).astype(BF16)
    return high, middle, low


def rows_of():
    sub = lax.broadcasted_iota(jnp.int32, (8, TILE), 0)
    second = (sub == 3) | (sub == 4) | (sub == 5) | (sub == 7)
    is_x = (sub == 0) | (sub == 3)
    is_y = (sub == 1) | (sub == 4)
    is_z = (sub == 2) | (sub == 5)
    return sub, second, is_x, is_y, is_z


def load_row(ref, row):
    return jnp.broadcast_to(ref[pl.ds(row, 1), :], (8, TILE))


def site_vectors(ref, base, centre):
    sub, second, is_x, is_y, is_z = rows_of()
    dips = [load_row(ref, base + k * TILES) for k in range(6)]
    pos = [load_row(ref, base + (6 + k) * TILES) - centre[k] for k in range(3)]
    pol = load_row(ref, base + 9 * TILES)
    mu = [jnp.where(second, dips[3 + j], dips[j]) for j in range(3)]
    mixed = jnp.where(is_x, pos[0], jnp.where(is_y, pos[1], jnp.where(is_z, pos[2], 1.0)))
    own = jnp.where(is_x, mu[0], jnp.where(is_y, mu[1], jnp.where(is_z, mu[2], 0.0)))
    return mu, pos, pol, mixed, own


def dipole_rows(mu, pos, mixed, own):
    dots = pos[0] * mu[0] + pos[1] * mu[1] + pos[2] * mu[2]
    tripled = 3.0 * mixed
    left = jnp.concatenate([tripled * mu[0], tripled * mu[1], tripled * mu[2], tripled * dots], 0)
    blank = jnp.zeros((16, TILE), BF16)
    right = jnp.concatenate([jnp.zeros((8, TILE), F32), -own], 0)
    out = []
    for l, r in zip(three_parts(left), three_parts(right)):
        out.append(jnp.concatenate([l, jnp.concatenate([blank, r], 0)], 1))
    return jnp.concatenate(out[:PARTS], 0)


def geometry_rows(first_three, fourth, fifth):
    sub = lax.broadcasted_iota(jnp.int32, (8, TILE), 0)
    rows = jnp.where(sub == 0, first_three[0], jnp.where(sub == 1, first_three[1], jnp.where(sub == 2, first_three[2], jnp.where(sub == 3, fourth, jnp.where(sub == 4, fifth, 0.0)))))
    return tuple(p.astype(F32) for p in three_parts(rows))


def scale_rows(scale, pattern):
    sub = lax.broadcasted_iota(jnp.int32, (8, TILE), 0)
    parts = [p.astype(F32) for p in three_parts(scale)]
    out = jnp.zeros((8, TILE), F32)
    for row, part in enumerate(pattern):
        out = jnp.where(sub == row, parts[part], out)
    return out


def squared(pos):
    return pos[0] * pos[0] + pos[1] * pos[1] + pos[2] * pos[2]


def assemble(parts, pos, mixed):
    sub, second, _, _, _ = rows_of()
    g = pos[0] * parts[0] + pos[1] * parts[1] + pos[2] * parts[2] - parts[3]
    s0 = jnp.broadcast_to(g[6:7], (8, TILE))
    s1 = jnp.broadcast_to(g[7:8], (8, TILE))
    s = jnp.where(second, s1, s0)
    return mixed * s - g


def kernel(
    lists_ref, split_ref, *refs
):
    sources, refs = refs[:9], refs[9:]
    outs, refs = refs[:3], refs[3:]
    (
    out_ref, copy_sem, out_sem, x_ref, geo_ref, dip_ref, acc_ref, eye_ref, near_ref, base_ref, target_ref, dist_even, dist_odd, coef_even, coef_odd,
    ) = refs
    eye = (
        lax.broadcasted_iota(jnp.int32, (TILE, TILE), 0) == lax.broadcasted_iota(jnp.int32, (TILE, TILE), 1)
    )
    eye16 = jnp.where(eye, 1.0, 0.0).astype(BF16)
    zero8 = jnp.zeros((8, TILE), F32)
    own_base = 4 * ROWS
    copies = []
    for g, source in enumerate(sources):
        place = x_ref.at[pl.ds(g * ROWS, ROWS), :]
        copies.append(pltpu.make_async_copy(source, place, copy_sem.at[g]))
        copies[-1].start()
    nt = (((1,), (1,)), ((), ()))
    eye_ref[0] = jnp.zeros((TILE, 2 * TILE), BF16)
    eye_ref[1] = jnp.concatenate(
        [jnp.where(eye, FAR_AWAY, 0.0).astype(BF16), jnp.zeros((TILE, TILE), BF16)], 1
    )

    eye_ref[2] = jnp.concatenate([eye16, eye16], 1)

    def clear(i, _):
        out_ref[pl.ds(pl.multiple_of(i * 64, 64), 64), :] = jnp.zeros((64, TILE), F32)
        return 0

    lax.fori_loop(0, out_ref.shape[0] // 64, clear, 0)
    copies[4].wait()

    def prepare(t, _):
        centre = (8.0, 8.0, (4 * t + 2).astype(F32))
        mu, pos, pol, mixed, own = site_vectors(x_ref, own_base + t, centre)
        dip_ref[t] = dipole_rows(mu, pos, mixed, own)
        hi, mid, lo = geometry_rows([-2.0 * p for p in pos], 1.0, squared(pos))
        scale = (-thole) * lax.rsqrt(pol)
        q = scale_rows(scale, (0, 1, 0, 1, 0, 2))
        stack = jnp.concatenate([hi, mid, hi, mid, hi, lo, q, zero8], 0).astype(BF16)
        moved = lax.dot_general(eye16, stack, nt, preferred_element_type=F32).astype(BF16)
        geo_ref[t] = moved
        acc_ref[t] = jnp.zeros((32, TILE), F32)
        return 0

    lax.fori_loop(0, TILES, prepare, 0, unroll=4)
    for g in range(9):
        if g != 4:
            copies[g].wait()
    geo_ref[DUMMY] = geo_ref[0]
    dip_ref[DUMMY] = dip_ref[0]

    def blank(at):
        near_ref[at] = DUMMY + 4 * GRID
        base_ref[at] = own_base
        target_ref[at] = UNUSED

    for k in range(2 * UNROLL):
        blank(k)
    total = jnp.int32(2 * UNROLL)
    def put(at, home, remote, g):
        target = remote + g * OUT_ROWS
        if g == 4:
            target = jnp.where(remote == home, UNUSED, target)
        near_ref[at] = home + g * GRID
        base_ref[at] = remote + g * ROWS
        target_ref[at] = target
        return at + 1

    for g in range(9):
        first = lists_ref[3 * g + 2, 8 - g]
        last = lists_ref[3 * g + 2, 9 - g]
        if g != 4:
            last = first + split_ref[g, 0]

        def incoming(p, at, g=g):
            return put(at, lists_ref[3 * g, p] & (TILES - 1), lists_ref[3 * g + 1, p], g)

        total = lax.fori_loop(first, last, incoming, total)
        if g != 4:
            first = lists_ref[14, g] + split_ref[9 + g, 0]
            last = lists_ref[14, g + 1]

            def kept(p, at, g=g):
                return put(at, lists_ref[13, p], lists_ref[12, p] & (TILES - 1), g)

            total = lax.fori_loop(first, last, kept, total)
    for k in range((HALVES + 2) * UNROLL):
        blank(total + k)
    groups = (total - 2 * UNROLL + UNROLL - 1) // UNROLL

    def home_of(at):
        return near_ref[at] & (GRID - 1)

    def origin(at):
        grid = near_ref[at] // GRID
        row = (grid * 11) // 32
        column = grid - 3 * row
        return (
            24.0 - domain_edge * row.astype(F32),
            24.0 - domain_edge * column.astype(F32),
            (4 * home_of(at) + 2).astype(F32),
        )

    def distances(dist_ref, u, at):
        base = base_ref[at]
        pos = [load_row(x_ref, base + (6 + k) * TILES) - c for k, c in enumerate(origin(at))]
        pol = load_row(x_ref, base + 9 * TILES)
        hi, mid, lo = geometry_rows(pos, squared(pos), 1.0)
        q = scale_rows(lax.rsqrt(pol), (0, 0, 1, 1, 2, 0))
        left = jnp.concatenate([hi, hi, mid, mid, lo, hi, zero8, zero8], 0).astype(BF16)
        right = jnp.concatenate([jnp.zeros((48, TILE), F32), q, zero8], 0).astype(BF16)
        same = (target_ref[at] == UNUSED).astype(jnp.int32)
        operand = jnp.concatenate([eye_ref[same], jnp.concatenate([left, right], 1)], 0)
        rows = jnp.concatenate([eye_ref[2, :, :TILE], geo_ref[home_of(at)]], 1)
        dist_ref[u] = jnp.dot(rows, operand, preferred_element_type=F32)

    def coefficients(dist_ref, coef_ref, u):
        dist_sq = dist_ref[u, :, :TILE]
        inv = lax.rsqrt(dist_sq)
        inv_sq = inv * inv
        inv_cube = inv_sq * inv
        cube = dist_sq * inv * dist_sq
        damp = cube * dist_ref[u, :, TILE:]
        decay = jnp.exp(damp)
        lam_three = 1.0 - decay
        lam_five = lam_three + damp * decay
        three = lam_three * inv_cube
        five = lam_five * inv_cube * inv_sq
        three_hi = three.astype(BF16)
        five_hi = five.astype(BF16)
        coef_ref[u, 0] = five_hi
        coef_ref[u, 1] = (five - five_hi.astype(F32)).astype(BF16)
        coef_ref[u, 2] = three_hi
        coef_ref[u, 3] = (three - three_hi.astype(F32)).astype(BF16)

    def folded(sums):
        total = sums[0:32, :TILE]
        for k in range(1, PARTS):
            total = total + (sums[32 * k:32 * k + 32, :TILE] + sums[32 * k - 32:32 * k, TILE:])
        return total

    def sums(coef_ref, u, at):
        mu, pos, pol, mixed, own = site_vectors(x_ref, base_ref[at], origin(at))
        rem = dipole_rows(mu, pos, mixed, own)
        five_hi, five_lo, three_hi, three_lo = [coef_ref[u, k] for k in range(4)]
        square = jnp.concatenate(
            [jnp.concatenate([five_hi, three_hi], 1), jnp.concatenate([five_lo, three_lo], 1)], 0
        )
        h = folded(lax.dot_general(rem, square, nt, preferred_element_type=F32))
        square = jnp.concatenate(
            [jnp.concatenate([five_hi, five_lo], 1), jnp.concatenate([three_hi, three_lo], 1)], 0
        )
        r = folded(jnp.dot(dip_ref[home_of(at)], square, preferred_element_type=F32))
        field = assemble([r[8 * j:8 * j + 8] for j in range(4)], pos, mixed)
        return home_of(at), target_ref[at], h, field

    def half(first, dist_now, dist_next, coef_now, coef_next):
        done = [sums(coef_now, u, first + u) for u in range(UNROLL)]
        for u in range(UNROLL):
            coefficients(dist_now, coef_next, u)
        for u in range(UNROLL):
            distances(dist_next, u, first + 2 * UNROLL + u)
        for home, target, h, field in done:
            acc_ref[home] += h
            out_ref[pl.ds(target, 8, stride=OUT_STRIDE), :] += field

    even = (dist_even, dist_odd, coef_even, coef_odd)
    odd = (dist_odd, dist_even, coef_odd, coef_even)

    def step(i, _):
        for k in range(HALVES):
            half((HALVES * i + k) * UNROLL, *(odd if k % 2 else even))
        return 0

    lax.fori_loop(0, (groups + 1 + HALVES) // HALVES, step, 0)

    sends = []
    for g in range(9):
        for k in range(6):
            source = out_ref.at[pl.ds(g * OUT_ROWS + k * OUT_STRIDE, TILES), :]
            place = outs[g % 3].at[k, g // 3]
            sends.append(pltpu.make_async_copy(source, place, out_sem.at[6 * g + k]))
    for k, send in enumerate(sends):
        if k // 6 != 4:
            send.start()

    def finish(t, _):
        centre = (8.0, 8.0, (4 * t + 2).astype(F32))
        mu, pos, pol, mixed, own = site_vectors(x_ref, own_base + t, centre)
        field = assemble([acc_ref[t, 8 * j:8 * j + 8] for j in range(4)], pos, mixed)
        out_ref[pl.ds(4 * OUT_ROWS + t, 8, stride=OUT_STRIDE), :] += field
        return 0

    lax.fori_loop(0, TILES, finish, 0, unroll=4)
    for send in sends[24:30]:
        send.start()
    for send in sends:
        send.wait()


FAR_AWAY = 2.0 ** 60
LIST = 9 * 2048 + (HALVES + 4) * UNROLL
OUT_STRIDE = TILES + 8
OUT_ROWS = 8 * OUT_STRIDE
UNUSED = 4 * OUT_ROWS + DUMMY


def field_kernel(lists, split, *sites):
    smem = pl.BlockSpec(memory_space=pltpu.SMEM)
    away = pl.BlockSpec(memory_space=pl.ANY)
    return pl.pallas_call(
        kernel,
        out_shape=[jax.ShapeDtypeStruct((6, 3, TILES, TILE), F32)] * 3,
        in_specs=[smem, smem] + [away] * 9,
        out_specs=[away] * 3,
        scratch_shapes=[
            pltpu.VMEM((9 * OUT_ROWS, TILE), F32),
            pltpu.SemaphoreType.DMA((9,)),
            pltpu.SemaphoreType.DMA((54,)),
            pltpu.VMEM((9 * ROWS, TILE), F32),
            pltpu.VMEM((TILES + 1, TILE, 64), BF16),
            pltpu.VMEM((TILES + 1, 32 * PARTS, 2 * TILE), BF16),
            pltpu.VMEM((TILES + 1, 32, TILE), F32),
            pltpu.VMEM((3, TILE, 2 * TILE), BF16),
            pltpu.SMEM((LIST,), jnp.int32),
            pltpu.SMEM((LIST,), jnp.int32),
            pltpu.SMEM((LIST,), jnp.int32),
            pltpu.VMEM((UNROLL, TILE, 2 * TILE), F32),
            pltpu.VMEM((UNROLL, TILE, 2 * TILE), F32),
            pltpu.VMEM((UNROLL, 4, TILE, TILE), BF16),
            pltpu.VMEM((UNROLL, 4, TILE, TILE), BF16),
        ],
        compiler_params=pltpu.CompilerParams(vmem_limit_bytes=63 * 1024 * 1024),
        name="pair_fields",
    )(lists, split, *sites)


CHUNKS = 4
TURNS = 3
AHEAD = 2
EDGE = 8


def halo_kernel(sites_ref, lists_ref, counts_ref, *refs):
    outs, lists_out, split_ref = refs[:8], refs[8], refs[9]
    send_sem, recv_sem, list_send, list_recv, own_sem, *refs = refs[10:]
    nbr_counts, loads, mine, share_send, share_recv = refs
    outs = outs[:4] + (None,) + outs[4:]
    gx, gy = lax.axis_index("gx"), lax.axis_index("gy")
    n_gx, n_gy = lax.axis_size("gx"), lax.axis_size("gy")
    mesh_id = pl.DeviceIdType.MESH
    size = ROWS // CHUNKS

    def device(g):
        return (lax.rem(gx + g // 3 - 1 + n_gx, n_gx), lax.rem(gy + g % 3 - 1 + n_gy, n_gy))

    barrier = pltpu.get_barrier_semaphore()
    others = [g for g in range(9) if g != 4]
    for g in others:
        pl.semaphore_signal(barrier, inc=1, device_id=device(g), device_id_type=mesh_id)
    pl.semaphore_wait(barrier, 8)

    def piece(g, source, target, chunk):
        rows = pl.ds(chunk * size, size)
        return pltpu.make_async_remote_copy(
            src_ref=source.at[rows, :],
            dst_ref=outs[g].at[rows, :],
            send_sem=send_sem.at[g, chunk],
            recv_sem=recv_sem.at[g, chunk],
            device_id=device(target),
            device_id_type=mesh_id,
        )

    shared = []

    def share(turn, source, dest):
        for g in others:
            copy = pltpu.make_async_remote_copy(
                src_ref=source,
                dst_ref=dest.at[g],
                send_sem=share_send.at[turn, g],
                recv_sem=share_recv.at[turn, g],
                device_id=device(8 - g),
                device_id_type=mesh_id,
            )
            copy.start()
            shared.append(copy)

    share(0, counts_ref, nbr_counts)
    straight = {}
    for chunk in range(CHUNKS):
        for g in (1, 7, 3, 5):
            straight[g, chunk] = piece(g, sites_ref, 8 - g, chunk)
    def begin(chunk):
        for g in (3, 5, 1, 7):
            straight[g, chunk].start()

    for chunk in range(AHEAD):
        begin(chunk)
    listed = []
    for g in others:
        listed.append(
            pltpu.make_async_remote_copy(
                src_ref=lists_ref,
                dst_ref=lists_out.at[g],
                send_sem=list_send.at[g],
                recv_sem=list_recv.at[g],
                device_id=device(8 - g),
                device_id_type=mesh_id,
            )
        )
        listed[-1].start()
    own = pltpu.make_async_copy(lists_ref, lists_out.at[4], own_sem)
    own.start()
    first_edge = lax.rem(gy, EDGE) == 0
    last_edge = lax.rem(gy, EDGE) == EDGE - 1
    onward = {
        1: ((~last_edge, 0, 1, 5), (~first_edge, 2, 1, 3)),
        7: ((~last_edge, 6, 7, 5), (~first_edge, 8, 7, 3)),
        3: ((first_edge, 0, 3, 7), (first_edge, 6, 3, 1)),
        5: ((last_edge, 2, 5, 7), (last_edge, 8, 5, 1)),
    }

    def pass_on(g, chunk, action):
        for condition, slot, here, target in onward[g]:

            @pl.when(condition)
            def _(slot=slot, here=here, target=target):
                action(piece(slot, outs[here], target, chunk))

    incoming, outgoing, given, kept = {}, {}, {}, {}

    def balance(turn):
        for copy in shared[8 * turn:8 * turn + 8]:
            copy.wait_recv()
        if turn == 0:
            for g in others:
                given[g] = incoming[g] = nbr_counts[g, 8 - g:9 - g, :]
                kept[g] = outgoing[g] = counts_ref[g:g + 1, :]
        else:
            before = mine[turn - 1, 0:1, :]
            for g in others:
                theirs = loads[turn - 1, g, 0:1, :]
                come = jnp.floor((theirs - before) * (1.0 / 16.0))
                given[g] = jnp.clip(given[g] + come, 0.0, incoming[g])
                leave = jnp.floor((before - theirs) * (1.0 / 16.0))
                kept[g] = jnp.clip(kept[g] + leave, 0.0, outgoing[g])
        if turn < TURNS:
            load = counts_ref[4:5, :]
            for g in others:
                load = load + (outgoing[g] - kept[g]) + given[g]
            mine[turn] = jnp.broadcast_to(load, (8, TILE))
            share(turn + 1, mine.at[turn], loads.at[turn])

    for chunk in range(CHUNKS):
        balance(chunk)
        for g in (1, 7, 3, 5):
            straight[g, chunk].wait_recv()
            pass_on(g, chunk, lambda copy: copy.start())
        if chunk + AHEAD < CHUNKS:
            begin(chunk + AHEAD)
    for turn in range(CHUNKS, TURNS + 1):
        balance(turn)
    blank = jnp.zeros((1, TILE), F32)
    rows = [given.get(g, blank) for g in range(9)] + [kept.get(g, blank) for g in range(9)]
    split_ref[...] = jnp.concatenate(rows + [blank] * 6, 0).astype(jnp.int32)
    for copy in shared:
        copy.wait_send()
    for chunk in range(CHUNKS):
        for g in (1, 7, 3, 5):
            straight[g, chunk].wait_send()
            pass_on(g, chunk, lambda copy: copy.wait_send())
        for g in (0, 2, 6, 8):
            piece(g, sites_ref, 8 - g, chunk).wait_recv()
    for copy in listed:
        copy.wait()
    own.wait()


def halo_exchange(sites, lists, counts):
    away = pl.BlockSpec(memory_space=pl.ANY)
    shapes = [jax.ShapeDtypeStruct(sites.shape, sites.dtype)] * 8
    shapes.append(jax.ShapeDtypeStruct((9,) + lists.shape, lists.dtype))
    shapes.append(jax.ShapeDtypeStruct((24, TILE), jnp.int32))
    vmem = pl.BlockSpec(memory_space=pltpu.VMEM)
    return pl.pallas_call(
        halo_kernel,
        out_shape=shapes,
        in_specs=[away, away, vmem],
        out_specs=[away] * 9 + [vmem],
        scratch_shapes=[
            pltpu.SemaphoreType.DMA((9, CHUNKS)),
            pltpu.SemaphoreType.DMA((9, CHUNKS)),
            pltpu.SemaphoreType.DMA((9,)),
            pltpu.SemaphoreType.DMA((9,)),
            pltpu.SemaphoreType.DMA,
            pltpu.VMEM((9, 16, TILE), F32),
            pltpu.VMEM((TURNS, 9, 8, TILE), F32),
            pltpu.VMEM((TURNS, 8, TILE), F32),
            pltpu.SemaphoreType.DMA((TURNS + 1, 9)),
            pltpu.SemaphoreType.DMA((TURNS + 1, 9)),
        ],
        compiler_params=pltpu.CompilerParams(collective_id=0, has_side_effects=True),
        name="halo",
    )(sites, lists, counts)


def return_kernel(
    low_ref, mid_ref, high_ref, perm_ref, pol_ref, field_ref, induced_ref,
    column, left, right, up, down, edge_in, edge_own, edge_sum,
    mid_sem, gy_send, gy_recv, gx_send, gx_recv, edge_send, edge_recv, edge_sem,
):
    gx, gy = lax.axis_index("gx"), lax.axis_index("gy")
    n_gx, n_gy = lax.axis_size("gx"), lax.axis_size("gy")
    mesh_id = pl.DeviceIdType.MESH

    def device(row, col):
        return (lax.rem(gx + row + n_gx, n_gx), lax.rem(gy + col + n_gy, n_gy))

    barrier = pltpu.get_barrier_semaphore()
    for row, col in ((-1, 0), (1, 0), (0, -1), (0, 1)):
        pl.semaphore_signal(barrier, inc=1, device_id=device(row, col), device_id_type=mesh_id)
    pl.semaphore_wait(barrier, 4)

    def remote(source, dest, send, recv, way, k, target):
        return pltpu.make_async_remote_copy(
            src_ref=source.at[k],
            dst_ref=dest.at[k],
            send_sem=send.at[way, k],
            recv_sem=recv.at[way, k],
            device_id=target,
            device_id_type=mesh_id,
        )

    edges = (lax.rem(gy, EDGE) == 0, lax.rem(gy, EDGE) == EDGE - 1)
    sources, dests = (low_ref, high_ref), (right, left)
    targets = (device(0, -1), device(0, 1))
    second, own = [], []

    def either(condition, yes, no):
        pl.when(condition)(yes)
        pl.when(jnp.logical_not(condition))(no)

    def whole(way, k):
        return remote(sources[way], dests[way], gy_send, gy_recv, way, k, targets[way])

    def summed(way, k):
        return pltpu.make_async_remote_copy(
            src_ref=edge_sum.at[k],
            dst_ref=dests[way].at[k, 1],
            send_sem=gy_send.at[way, k],
            recv_sem=gy_recv.at[way, k],
            device_id=targets[way],
            device_id_type=mesh_id,
        )

    def along(way, k, slot):
        return pltpu.make_async_remote_copy(
            src_ref=sources[way].at[k, 2 - 2 * slot],
            dst_ref=edge_in.at[slot, k],
            send_sem=edge_send.at[slot, k],
            recv_sem=edge_recv.at[slot, k],
            device_id=device(1 - 2 * slot, 0),
            device_id_type=mesh_id,
        )

    def centre(way, k):
        return pltpu.make_async_copy(sources[way].at[k, 1], edge_own.at[k], edge_sem.at[k])

    for k in range(6):
        for way in range(2):

            def start_edge(way=way, k=k):
                along(way, k, 0).start()
                along(way, k, 1).start()
                centre(way, k).start()

            either(edges[way], start_edge, lambda way=way, k=k: whole(way, k).start())
        own.append(pltpu.make_async_copy(mid_ref.at[k], column.at[k], mid_sem.at[k]))
        own[k].start()

    for way in range(2):

        @pl.when(edges[1 - way])
        def _(way=way):
            for k in range(6):
                for row in (0, 2):
                    dests[way][k, row] = jnp.zeros((TILES, TILE), F32)

    def edge_stage(k):
        for way in range(2):

            @pl.when(edges[way])
            def _(way=way):
                centre(way, k).wait()
                along(way, k, 0).wait_recv()
                along(way, k, 1).wait_recv()
                edge_sum[k] = edge_own[k] + edge_in[0, k] + edge_in[1, k]
                summed(way, k).start()

    def finish(k):
        for copy in second[k]:
            copy.wait_recv()
        total = column[k, 1] + up[k] + down[k]
        field_ref[k] = total
        induced_ref[k] = pol_ref[...] * (perm_ref[k] + total)

    edge_stage(0)
    edge_stage(1)
    for k in range(6):
        own[k].wait()
        for way in range(2):
            either(
                edges[1 - way],
                lambda way=way: summed(way, k).wait_recv(),
                lambda way=way: whole(way, k).wait_recv(),
            )
        column[k] = column[k] + left[k] + right[k]
        second.append(
            (
                remote(column.at[:, 0], down, gx_send, gx_recv, 0, k, device(-1, 0)),
                remote(column.at[:, 2], up, gx_send, gx_recv, 1, k, device(1, 0)),
            )
        )
        for copy in second[k]:
            copy.start()
        if k + 2 < 6:
            edge_stage(k + 2)
        if k >= 2:
            finish(k - 2)
    finish(4)
    finish(5)
    for k in range(6):
        for way in range(2):

            def end_edge(way=way, k=k):
                along(way, k, 0).wait_send()
                along(way, k, 1).wait_send()
                summed(way, k).wait_send()

            either(edges[way], end_edge, lambda way=way, k=k: whole(way, k).wait_send())
        for copy in second[k]:
            copy.wait_send()


def return_terms(low, mid, high, perm, pol):
    away = pl.BlockSpec(memory_space=pl.ANY)
    vmem = pl.BlockSpec(memory_space=pltpu.VMEM)
    return pl.pallas_call(
        return_kernel,
        out_shape=[jax.ShapeDtypeStruct((6, TILES, TILE), F32)] * 2,
        in_specs=[away] * 3 + [vmem] * 2,
        out_specs=[vmem] * 2,
        scratch_shapes=[
            pltpu.VMEM((6, 3, TILES, TILE), F32),
            pltpu.VMEM((6, 3, TILES, TILE), F32),
            pltpu.VMEM((6, 3, TILES, TILE), F32),
            pltpu.VMEM((6, TILES, TILE), F32),
            pltpu.VMEM((6, TILES, TILE), F32),
            pltpu.VMEM((2, 6, TILES, TILE), F32),
            pltpu.VMEM((6, TILES, TILE), F32),
            pltpu.VMEM((6, TILES, TILE), F32),
            pltpu.SemaphoreType.DMA((6,)),
            pltpu.SemaphoreType.DMA((2, 6)),
            pltpu.SemaphoreType.DMA((2, 6)),
            pltpu.SemaphoreType.DMA((2, 6)),
            pltpu.SemaphoreType.DMA((2, 6)),
            pltpu.SemaphoreType.DMA((2, 6)),
            pltpu.SemaphoreType.DMA((2, 6)),
            pltpu.SemaphoreType.DMA((6,)),
        ],
        compiler_params=pltpu.CompilerParams(
            collective_id=1, has_side_effects=True, vmem_limit_bytes=63 * 1024 * 1024
        ),
        name="return_terms",
    )(low, mid, high, perm, pol)


def local(positions, polarity, dipoles, perm_fields, pair_list, tile_counts):
    slot_total = pair_list.shape[3]
    sites = jnp.concatenate([dipoles, positions, polarity[None]], 0).reshape(10 * TILES, TILE)

    table = pair_list.reshape(2, slot_total)
    live = jnp.arange(slot_total, dtype=jnp.int32) < tile_counts.reshape(())
    far = jnp.where(live, table[1], 16 * TILES)
    far, near = lax.sort((far, table[0]), num_keys=1)
    bounds = jnp.arange(slot_total, dtype=jnp.int32)[:16] * TILES
    bounds = jnp.sum((far[None, :] < bounds[:, None]).astype(jnp.int32), 1)
    counts = (bounds[1:10] - bounds[:9]).astype(F32)
    counts = jnp.broadcast_to(jnp.pad(counts, (0, 7))[:, None], (16, TILE))
    bounds = jnp.concatenate([bounds, jnp.zeros((slot_total - 16,), jnp.int32)])
    lists = jnp.stack([far, near, bounds])
    *around_sites, lists, split = halo_exchange(sites, lists, counts)
    low, mid, high = field_kernel(
        lists.reshape(27, slot_total), split, *around_sites[:4], sites, *around_sites[4:]
    )
    perm = perm_fields.reshape(6, TILES, TILE)
    field, induced = return_terms(low, mid, high, perm, polarity.reshape(TILES, TILE))
    field = field.reshape(6, 1, 1, TILES * TILE)
    induced = induced.reshape(6, 1, 1, TILES * TILE)
    return (field, induced)


def solution(mesh):
    placed = (
        P(None, "gx", "gy", None),
        P("gx", "gy", None),
        P(None, "gx", "gy", None),
        P(None, "gx", "gy", None),
        P("gx", "gy", None, None),
        P("gx", "gy"),
    )
    return jax.shard_map(
        local,
        mesh=mesh,
        in_specs=placed,
        out_specs=(P(None, "gx", "gy", None), P(None, "gx", "gy", None)),
        check_vma=False,
    )
```
